128 devices in a mesh: seq: 64 (over z, x_hi, y, core), head: 2 (over x_lo).
Axes of the slice: x: 4 (x_hi: 2, x_lo: 2; x = x_hi * 2 + x_lo), y: 4, z: 4, core: 2. Of those that a mesh axis runs over, the one named last changes fastest.
Arguments:
- queries: bfloat16 [262144, 512], P('seq', 'head'), may hold values from -6 to 6
- keys: bfloat16 [262144, 512], P('seq', 'head'), may hold values from -6 to 6
- values: bfloat16 [262144, 512], P('seq', 'head'), may hold values from -6 to 6
- offsets: int32 [3, 4], replicated, may hold values from 0 to 63, as said below
- out_weight: bfloat16 [512, 2048], P('head'), may hold values from -0.25 to 0.25
Outputs:
- projected: bfloat16 [262144, 2048], P(('seq', 'head'))
The draws below stay inside these ranges and needn't reach their ends.
Inputs may be any that keep to these rules, and one draw needn't show every extreme that they name: offsets[0, h] < 4, offsets[1, h] < 16, offsets[2, h] < 64; each row holds 0 and its rate minus 1.
All inputs are finite; a program needn't handle non-finite values.
Results may differ from the reference program's by a relative error of at most 0.01.
Values may be sent and summed in bfloat16 or wider, within the bound.
No kernel may reach another device: no remote copies, remote signals or barrier semaphores. Data moves between devices by JAX's collectives and lax.ppermute only.
A program may use at most 128 MiB of HBM per device.

```python
import math
import jax
import jax.numpy as jnp
from jax import lax

D = 2048
HEADS = 4
HD = 128
TOK_DEV = 4096
RATE_MID = 4
RATE_WIDE = 16
RATE_FAR = 64
GROUP_MID = 4
GROUP_WIDE = 16
TOKENS = 262144
N_HEAD = 2


def shared_offsets(key):
    base_key = jax.random.fold_in(key, 7)
    row_list = []
    for level_index, level_rate in enumerate((RATE_MID, RATE_WIDE, RATE_FAR)):
        level_key = jax.random.fold_in(base_key, level_index)
        value_key, order_key = jax.random.split(level_key)
        picked = jax.random.randint(value_key, (HEADS,), 0, level_rate, dtype=jnp.int32)
        ordering = jax.random.permutation(order_key, HEADS)
        picked = picked.at[ordering[0]].set(level_rate - 1).at[ordering[1]].set(0)
        row_list.append(picked)
    return jnp.stack(row_list).astype(jnp.int32)


def draw_offsets(key, part):
    return shared_offsets(key)


def draw_queries(key, part):
    key = jax.random.fold_in(key, 1)
    entries = jnp.clip(1.5 * jax.random.normal(key, (TOKENS, HEADS * HD), jnp.float32), -6.0, 6.0)
    return entries.astype(jnp.bfloat16)


def draw_keys(key, part):
    key = jax.random.fold_in(key, 2)
    entries = jnp.clip(1.5 * jax.random.normal(key, (TOKENS, HEADS * HD), jnp.float32), -6.0, 6.0)
    return entries.astype(jnp.bfloat16)


def level_of(key, shape, pieces, low, high):
    loudness = 1.0
    for dim, blocks in pieces:
        draws = jax.random.uniform(jax.random.fold_in(jax.random.fold_in(key, 6), dim), (blocks,), jnp.float32, low / len(pieces), high / len(pieces))
        loudness = loudness * jnp.repeat(jnp.exp(draws), shape[dim] // blocks).reshape((-1,) + (1,) * (len(shape) - 1 - dim))
    return loudness


def bell_draw(stream_key, shape, width, most, cuts=(), kind=jnp.bfloat16):
    level = level_of(stream_key, shape, cuts, -0.22, 0.18) if cuts else 1.0
    array = jax.random.normal(stream_key, shape, jnp.float32) * width * level
    return jnp.minimum(jnp.maximum(array, -most), most).astype(kind)


def setup_inputs(seed: int = 0) -> dict:
    streams_of = jax.random.split(jax.random.key(seed), 6)
    return {
        "queries": draw_queries(jax.random.fold_in(streams_of[5], 71), 0),
        "keys": draw_keys(jax.random.fold_in(streams_of[5], 71), 0),
        "values": bell_draw(streams_of[2], (TOKENS, HEADS * HD), 1.0, 6.0, ((0, 64), (1, 2))),
        "offsets": draw_offsets(jax.random.fold_in(streams_of[5], 71), 0),
        "out_weight": bell_draw(streams_of[4], (HEADS * HD, D), (HEADS * HD) ** -0.5, 0.25, ((0, 2),)),
    }


masked_fill = -1e+30

def causal_attend(query_rows, key_rows, value_rows):
    scores = jnp.dot(query_rows, key_rows.T, preferred_element_type=jnp.float32) / math.sqrt(HD)
    row_count = scores.shape[0]
    positions = jnp.arange(row_count, dtype=jnp.int32)
    allowed = positions[:, None] >= positions[None, :]
    scores = jnp.where(allowed, scores, masked_fill)
    row_peak = lax.optimization_barrier(jnp.max(scores, axis=1, keepdims=True))
    weights = jnp.where(allowed, jnp.exp(scores - row_peak), 0.0)
    weight_sum = lax.optimization_barrier(jnp.sum(weights, axis=1, keepdims=True))
    blended = jnp.dot(weights.astype(jnp.bfloat16), value_rows, preferred_element_type=jnp.float32) / weight_sum
    return (blended, row_peak[:, 0] + jnp.log(weight_sum[:, 0]))

def dilated_level(column_q, column_k, column_v, offset_value, level_rate, segment):
    picked = []
    for source in (column_q, column_k, column_v):
        shaped = source.reshape(TOKENS // level_rate, level_rate, HD)
        chosen = lax.dynamic_index_in_dim(shaped, offset_value, 1, keepdims=False)
        picked.append(chosen.reshape(TOKENS // segment, segment // level_rate, HD))

    def one_segment(triple):
        return causal_attend(triple[0], triple[1], triple[2])
    outputs, log_total = lax.map(one_segment, (picked[0], picked[1], picked[2]))
    outputs = outputs.reshape(TOKENS // level_rate, HD)
    log_total = log_total.reshape(TOKENS // level_rate)
    covered = jnp.arange(level_rate, dtype=jnp.int32) == offset_value
    full_out = (outputs[:, None, :] * covered[None, :, None].astype(jnp.float32)).reshape(TOKENS, HD)
    full_log = jnp.broadcast_to(log_total[:, None], (TOKENS // level_rate, level_rate)).reshape(TOKENS)
    full_cover = jnp.broadcast_to(covered[None, :], (TOKENS // level_rate, level_rate)).reshape(TOKENS)
    return (full_out, full_log, full_cover)

def reference(queries, keys, values, offsets, out_weight):
    settings = ((1, TOK_DEV), (RATE_MID, GROUP_MID * TOK_DEV), (RATE_WIDE, GROUP_WIDE * TOK_DEV), (RATE_FAR, TOKENS))
    head_columns = []
    for head_index in range(HEADS):
        low = head_index * HD
        column_q = queries[:, low:low + HD]
        column_k = keys[:, low:low + HD]
        column_v = values[:, low:low + HD]
        results = []
        for level_index in range(4):
            level_rate, segment = settings[level_index]
            if level_index == 0:
                offset_value = jnp.zeros((), jnp.int32)
            else:
                offset_value = offsets[level_index - 1, head_index].astype(jnp.int32)
            results.append(dilated_level(column_q, column_k, column_v, offset_value, level_rate, segment))
        first_out, first_log, first_cover = results[0]
        level_peak = first_log
        for level_out, level_log, covered in results[1:]:
            level_peak = jnp.maximum(level_peak, jnp.where(covered, level_log, first_log))
        first_weight = jnp.exp(first_log - level_peak)
        numerator = first_out * first_weight[:, None]
        denominator = first_weight
        for level_out, level_log, covered in results[1:]:
            level_weight = jnp.exp(jnp.where(covered, level_log - level_peak, masked_fill))
            numerator = numerator + level_out * level_weight[:, None]
            denominator = denominator + level_weight
        head_columns.append((numerator / denominator[:, None]).astype(jnp.bfloat16))
    attended = jnp.concatenate(head_columns, axis=1)
    group_width = HEADS * HD // N_HEAD
    projected = jnp.zeros((TOKENS, D), jnp.float32)
    for group_index in range(N_HEAD):
        low = group_index * group_width
        partial_term = jnp.dot(attended[:, low:low + group_width], out_weight[low:low + group_width], preferred_element_type=jnp.float32).astype(jnp.bfloat16)
        partial_term = lax.optimization_barrier(partial_term)
        projected = projected + partial_term.astype(jnp.float32)
    return projected.astype(jnp.bfloat16)
```

```python
import functools
import math

import jax
import jax.numpy as jnp
from jax import lax
from jax.experimental import pallas as pl
from jax.experimental.pallas import tpu as pltpu
from jax.sharding import PartitionSpec as P

HD = 128
HEADS_HERE = 2
RATES = (4, 16, 64)
BLOCK = 1024
TILE = 256
ROWS = 144
LSUM = 128
MROW = 129
LOG2_SCALE = math.log2(math.e) / math.sqrt(HD)
FILL = -1e30
SMALL, LARGE = 2.0**-60, 2.0**100
VMEM_BYTES = 56 * 2**20

f32, bf16 = jnp.float32, jnp.bfloat16


def dot(a, b):
    return jnp.dot(a, b, preferred_element_type=f32)


def aligned(x, n):
    return x if isinstance(x, int) else pl.multiple_of(x, n)


def transposed_queries(q):
    q = q.astype(f32) * LOG2_SCALE
    high = q.astype(bf16)
    low = (q - high.astype(f32)).astype(bf16)
    return jnp.concatenate([high, low], axis=1).T


def scores(k, qt):
    return dot(jnp.concatenate([k, k], axis=1), qt)


def with_ones(v):
    return jnp.concatenate([v.T, jnp.ones((ROWS - HD, v.shape[0]), v.dtype)], axis=0)


def pieces(x):
    first = x.astype(bf16).astype(f32)
    second = (x - first).astype(bf16).astype(f32)
    return first, second, x - first - second


def stat_rows(total, exponent, count):
    row = lax.broadcasted_iota(jnp.int32, (ROWS - HD, count), 0)
    parts = (total,) + (pieces(exponent) if exponent is not None else ())
    out = jnp.zeros((ROWS - HD, count), f32)
    for n, part in enumerate(parts):
        out = jnp.where(row == n, part, out)
    return out


def within_range(total, counted=None):
    ok = (total >= SMALL) & (total <= LARGE)
    if counted is not None:
        ok = ok | ~counted
    return jnp.min(jnp.where(ok, 1.0, 0.0)) > 0.5


def rescaled(store, get_queries, count, blocks, block):
    def step(j, carry):
        peak, acc = carry
        k, vt, allowed = block(j)
        s = jnp.where(allowed, scores(k, get_queries()), FILL)
        new = jnp.maximum(peak, jnp.max(s, axis=0, keepdims=True))
        p = jnp.where(allowed, jnp.exp2(s - new), 0.0)
        return new, acc * jnp.exp2(peak - new) + dot(vt, p.astype(bf16))

    peak, acc = lax.fori_loop(
        0, blocks, step, (jnp.full((1, count), FILL, f32), jnp.zeros((ROWS, count), f32))
    )
    store(acc, acc[LSUM : LSUM + 1], peak)


def position_mask(key_first, query_pos, rows):
    key_pos = key_first + lax.broadcasted_iota(jnp.int32, (rows, query_pos.shape[1]), 0)
    return key_pos <= query_pos


def lane_positions(first, count):
    return first + lax.broadcasted_iota(jnp.int32, (1, count), 1)


def select_kernel(off_ref, q_ref, k_ref, v_ref, vt_ref, mid_ref, few_ref, qm_ref, qw_ref, qf_ref, scr):
    for h in range(HEADS_HERE):
        cols = slice(h * HD, (h + 1) * HD)
        kv_cols = (slice(h * HD, (h + 1) * HD), slice((2 + h) * HD, (3 + h) * HD))
        vt_ref[h] = with_ones(v_ref[:, cols])
        for x_ref, out in (
            (q_ref, ((qm_ref, 0, cols), (qw_ref, 0, cols), (qf_ref, 0, cols))),
            (k_ref, ((mid_ref, 0, kv_cols[0]), (few_ref, 0, kv_cols[0]), (few_ref, 256, kv_cols[0]))),
            (v_ref, ((mid_ref, 0, kv_cols[1]), (few_ref, 0, kv_cols[1]), (few_ref, 256, kv_cols[1]))),
        ):
            scr[...] = x_ref[:, cols].astype(f32)
            for level, (out_ref, row, out_cols) in enumerate(out):
                count = scr.shape[0] // RATES[level]
                picked = scr[pl.ds(off_ref[level, h], count, stride=RATES[level]), :]
                out_ref[row : row + count, out_cols] = picked.astype(bf16)


def vmem(count):
    return [pl.BlockSpec(memory_space=pltpu.VMEM)] * count


SMEM = pl.BlockSpec(memory_space=pltpu.SMEM)


def params():
    return pltpu.CompilerParams(vmem_limit_bytes=VMEM_BYTES)


def cost(pairs, bytes_accessed):
    return pl.CostEstimate(
        flops=int(pairs * 1024 * 1.5), bytes_accessed=int(bytes_accessed), transcendentals=int(pairs)
    )


def select(offs, q, k, v):
    tok = q.shape[0]
    mid, wide, far = (tok // r for r in RATES)
    return pl.pallas_call(
        select_kernel,
        in_specs=[SMEM] + vmem(3),
        out_specs=vmem(6),
        out_shape=[
            jax.ShapeDtypeStruct((HEADS_HERE, ROWS, tok), bf16),
            jax.ShapeDtypeStruct((mid, 512), bf16),
            jax.ShapeDtypeStruct((wide + far, 512), bf16),
            jax.ShapeDtypeStruct((mid, 256), bf16),
            jax.ShapeDtypeStruct((wide, 256), bf16),
            jax.ShapeDtypeStruct((far, 256), bf16),
        ],
        scratch_shapes=[pltpu.VMEM((tok, HD), f32)],
        compiler_params=params(),
        name="select_rows",
    )(offs, q, k, v)


def diagonal(out_ref, h, k_of, vt_of, qt_ref):
    for g in range(BLOCK // TILE):
        cols = slice(g * TILE, (g + 1) * TILE)
        keys = (g + 1) * TILE
        s = scores(k_of(keys), qt_ref[h, :, cols])
        row = lax.broadcasted_iota(jnp.int32, (TILE, TILE), 0)
        col = lax.broadcasted_iota(jnp.int32, (TILE, TILE), 1)
        p = jnp.exp2(s)
        last = jnp.where(row <= col, p[g * TILE :], 0.0)
        p = jnp.concatenate([p[: g * TILE], last], axis=0) if g else last
        out_ref[h, :, cols] += dot(vt_of(keys), p.astype(bf16))


def store_partial(out_ref, h, acc, total, exponent):
    count = acc.shape[1]
    out_ref[h, :HD] = acc[:HD]
    out_ref[h, HD:] = stat_rows(total, exponent, count)


def near_kernel(base_ref, q_ref, k_ref, vt_ref, out_ref, qt):
    block = base_ref[0] + pl.program_id(0)
    for h in range(HEADS_HERE):
        qt[h] = transposed_queries(q_ref[:, h * HD : (h + 1) * HD])
    out_ref[...] = jnp.zeros(out_ref.shape, f32)

    def full(j, carry):
        start = aligned(j * BLOCK, BLOCK)
        for h in range(HEADS_HERE):
            s = scores(k_ref[pl.ds(start, BLOCK), h * HD : (h + 1) * HD], qt[h])
            out_ref[h] += dot(vt_ref[h, :, pl.ds(start, BLOCK)], jnp.exp2(s).astype(bf16))
        return carry

    lax.fori_loop(0, block, full, 0)
    start = aligned(block * BLOCK, BLOCK)
    for h in range(HEADS_HERE):
        cols = slice(h * HD, (h + 1) * HD)
        diagonal(
            out_ref, h, lambda n: k_ref[pl.ds(start, n), cols], lambda n: vt_ref[h, :, pl.ds(start, n)], qt
        )
    for h in range(HEADS_HERE):
        cols = slice(h * HD, (h + 1) * HD)
        total = out_ref[h, LSUM : LSUM + 1]
        ok = within_range(total)
        out_ref[h, HD:] = stat_rows(total, None, BLOCK)

        @pl.when(jnp.logical_not(ok))
        def _():
            query_pos = lane_positions(block * BLOCK, BLOCK)

            def key_block(j):
                first = aligned(j * TILE, TILE)
                return (
                    k_ref[pl.ds(first, TILE), cols],
                    vt_ref[h, :, pl.ds(first, TILE)],
                    position_mask(first, query_pos, TILE),
                )

            rescaled(
                functools.partial(store_partial, out_ref, h),
                lambda: qt[h],
                BLOCK,
                (block + 1) * (BLOCK // TILE),
                key_block,
            )


def near(base, q, k, vt, blocks):
    tok = q.shape[0]
    return pl.pallas_call(
        near_kernel,
        grid_spec=pltpu.PrefetchScalarGridSpec(
            num_scalar_prefetch=1,
            grid=(blocks,),
            in_specs=[
                pl.BlockSpec((BLOCK, 256), lambda i, base: (base[0] + i, 0)),
                pl.BlockSpec((tok, 256), lambda i, base: (0, 0)),
                pl.BlockSpec((HEADS_HERE, ROWS, tok), lambda i, base: (0, 0, 0)),
            ],
            out_specs=pl.BlockSpec((HEADS_HERE, ROWS, BLOCK), lambda i, base: (0, 0, i)),
            scratch_shapes=[pltpu.VMEM((HEADS_HERE, 256, BLOCK), bf16)],
        ),
        out_shape=jax.ShapeDtypeStruct((HEADS_HERE, ROWS, blocks * BLOCK), f32),
        compiler_params=params(),
        cost_estimate=cost(2 * blocks * BLOCK * 2300, 10 * 2**20),
        name="near",
    )(base, q, k, vt)


def mid_kernel(causal, flag_ref, q_ref, *refs):
    *kv_refs, out_ref, qt, vt = refs
    for h in range(HEADS_HERE):
        qt[h] = transposed_queries(q_ref[:, h * HD : (h + 1) * HD])
    out_ref[...] = jnp.zeros(out_ref.shape, f32)

    def keys(n, h):
        return kv_refs[n].at[:, h * HD : (h + 1) * HD]

    for n, kv_ref in enumerate(kv_refs):
        for h in range(HEADS_HERE):
            vt[n, h] = with_ones(kv_ref[:, (2 + h) * HD : (3 + h) * HD])
    if causal:
        for h in range(HEADS_HERE):
            diagonal(out_ref, h, lambda c: keys(0, h)[:c], lambda c: vt[0, h, :, :c], qt)

    @pl.when(flag_ref[0] == 1)
    def _():
        for n in range(1 if causal else 0, len(kv_refs)):
            for h in range(HEADS_HERE):
                p = jnp.exp2(scores(keys(n, h)[...], qt[h])).astype(bf16)
                out_ref[h] += dot(vt[n, h], p)

    for h in range(HEADS_HERE):
        total = out_ref[h, LSUM : LSUM + 1]
        ok = within_range(total)
        out_ref[h, HD:] = stat_rows(total, None, BLOCK)
        used = flag_ref[0] == 1 if not causal else True

        @pl.when(jnp.logical_and(jnp.logical_not(ok), used))
        def _():
            query_pos = lane_positions(0, BLOCK)
            per = BLOCK // TILE
            peak = jnp.full((1, BLOCK), FILL, f32)
            acc = jnp.zeros((ROWS, BLOCK), f32)
            for n in range(len(kv_refs)):
                own = causal and n == 0
                key_first = 0 if own else -BLOCK if not causal else jnp.where(flag_ref[0] == 1, -BLOCK, 2 * BLOCK)

                def step(j, carry):
                    peak, acc = carry
                    first = aligned(j * TILE, TILE)
                    allowed = position_mask(key_first + first, query_pos, TILE)
                    s = jnp.where(allowed, scores(keys(n, h)[pl.ds(first, TILE), :], qt[h]), FILL)
                    new = jnp.maximum(peak, jnp.max(s, axis=0, keepdims=True))
                    p = jnp.where(allowed, jnp.exp2(s - new), 0.0)
                    acc = acc * jnp.exp2(peak - new) + dot(vt[n, h, :, pl.ds(first, TILE)], p.astype(bf16))
                    return new, acc

                peak, acc = lax.fori_loop(0, per, step, (peak, acc))
            store_partial(out_ref, h, acc, acc[LSUM : LSUM + 1], peak)


def mid(causal, flag, q, *kvs):
    return pl.pallas_call(
        functools.partial(mid_kernel, causal),
        in_specs=[SMEM] + vmem(1 + len(kvs)),
        out_specs=vmem(1)[0],
        out_shape=jax.ShapeDtypeStruct((HEADS_HERE, ROWS, BLOCK), f32),
        scratch_shapes=[
            pltpu.VMEM((HEADS_HERE, 256, BLOCK), bf16),
            pltpu.VMEM((len(kvs), HEADS_HERE, ROWS, BLOCK), bf16),
        ],
        compiler_params=params(),
        cost_estimate=cost(2 * BLOCK * BLOCK * 1.8, 5 * 2**20),
        name="mid",
    )(flag, q, *kvs)


def pool_kernel(rows, first_row, q_count, pos_ref, *refs):
    q_refs = refs[:q_count]
    *kv_refs, out_ref, qt, kk, vt = refs[q_count:]
    block_rows = q_refs[0].shape[0]
    count = q_count * block_rows
    total_keys = kk.shape[1]
    chunk = min(total_keys, 1024)
    query_pos = jnp.concatenate([lane_positions(pos_ref[n], block_rows) for n in range(q_count)], axis=1)
    counted = query_pos >= 0
    row = 0
    for kv_ref in kv_refs:
        for start in range(first_row, kv_ref.shape[0], rows[1]):
            for h in range(HEADS_HERE):
                kk[h, row : row + rows[0]] = kv_ref[start : start + rows[0], h * HD : (h + 1) * HD]
                kk[2 + h, row : row + rows[0]] = kv_ref[start : start + rows[0], (2 + h) * HD : (3 + h) * HD]
            row += rows[0]
    key_blocks = total_keys // rows[0]
    key_pos = jnp.concatenate(
        [pos_ref[q_count + n] + lax.broadcasted_iota(jnp.int32, (rows[0], 1), 0) for n in range(key_blocks)], axis=0
    )
    for h in range(HEADS_HERE):
        q = jnp.concatenate([q_ref[:, h * HD : (h + 1) * HD] for q_ref in q_refs], axis=0)
        qt[...] = transposed_queries(q)
        vt[...] = with_ones(kk[2 + h])
        acc = jnp.zeros((ROWS, count), f32)
        for first in range(0, total_keys, chunk):
            s = scores(kk[h, first : first + chunk], qt[...])
            allowed = key_pos[first : first + chunk] <= query_pos
            p = jnp.where(allowed, jnp.exp2(s), 0.0).astype(bf16)
            acc = acc + dot(vt[:, first : first + chunk], p)
        total = acc[LSUM : LSUM + 1]
        store_partial(out_ref, h, acc, total, None)

        @pl.when(jnp.logical_not(within_range(total, counted)))
        def _():
            peak = jnp.full((1, count), FILL, f32)
            acc = jnp.zeros((ROWS, count), f32)
            for first in range(0, total_keys, TILE):
                allowed = key_pos[first : first + TILE] <= query_pos
                s = jnp.where(allowed, scores(kk[h, first : first + TILE], qt[...]), FILL)
                new = jnp.maximum(peak, jnp.max(s, axis=0, keepdims=True))
                p = jnp.where(allowed, jnp.exp2(s - new), 0.0).astype(bf16)
                acc = acc * jnp.exp2(peak - new) + dot(vt[:, first : first + TILE], p)
                peak = new
            store_partial(out_ref, h, acc, acc[LSUM : LSUM + 1], peak)


def pool(name, rows, first_row, positions, qs, kvs):
    count = sum(q.shape[0] for q in qs)
    keys = sum(len(range(first_row, kv.shape[0], rows[1])) * rows[0] for kv in kvs)
    return pl.pallas_call(
        functools.partial(pool_kernel, rows, first_row, len(qs)),
        in_specs=[SMEM] + vmem(len(qs) + len(kvs)),
        out_specs=vmem(1)[0],
        out_shape=jax.ShapeDtypeStruct((HEADS_HERE, ROWS, count), f32),
        scratch_shapes=[
            pltpu.VMEM((256, count), bf16),
            pltpu.VMEM((2 * HEADS_HERE, keys, HD), bf16),
            pltpu.VMEM((ROWS, keys), bf16),
        ],
        compiler_params=params(),
        cost_estimate=cost(2 * count * keys, 4 * 2**20),
        name=name,
    )(positions, *qs, *kvs)


def exponent_of(x):
    m = x[MROW : MROW + 1] + x[MROW + 1 : MROW + 2] + x[MROW + 2 : MROW + 3]
    return jnp.where(x[LSUM : LSUM + 1] > 0.0, m, FILL)


def combined(parts):
    peaks = [exponent_of(x) for x in parts]
    peak = functools.reduce(jnp.maximum, peaks)
    out = sum(x[: LSUM + 1] * jnp.exp2(m - peak) for x, m in zip(parts, peaks))
    return out, peak


def split_rows(x, peak):
    rows = pieces(x[LSUM : LSUM + 1]) + pieces(peak)
    row = lax.broadcasted_iota(jnp.int32, (ROWS - HD, x.shape[1]), 0)
    stats = jnp.zeros((ROWS - HD, x.shape[1]), f32)
    for n, r in enumerate(rows):
        stats = jnp.where(row == n, r, stats)
    return jnp.concatenate([x[:HD], stats], axis=0).astype(bf16)


def merge_kernel(base_ref, off_ref, near_ref, mid_a, mid_b, wide_own, wide_back, far_own, far_b1, far_b2, far_b3, out_ref):
    block = base_ref[0] + pl.program_id(0)
    for h in range(HEADS_HERE):
        first = near_ref[h]
        levels = (
            (0, 4, [mid_a[h], mid_b[h]], 0),
            (1, 16, [wide_own[h][:, :256], wide_back[h]], block * BLOCK),
            (2, 64, [far_own[h][:, :64], far_b1[h], far_b2[h], far_b3[h]], block * BLOCK),
        )
        spread = []
        peak = exponent_of(first)
        for level, rate, parts, start in levels:
            x, x_peak = combined(parts)
            n = x.shape[1]
            row = lax.broadcasted_iota(jnp.int32, (n, BLOCK), 0) * rate + (off_ref[level, h] - start)
            col = lax.broadcasted_iota(jnp.int32, (n, BLOCK), 1)
            take = jnp.where(row == col, 1.0, 0.0).astype(bf16)
            y = dot(split_rows(x, x_peak), take)
            total = y[128:129] + y[129:130] + y[130:131]
            y_peak = jnp.where(total > 0.0, y[131:132] + y[132:133] + y[133:134], FILL)
            spread.append((y, total, y_peak))
            peak = jnp.maximum(peak, y_peak)
        scale = jnp.exp2(exponent_of(first) - peak)
        acc = first[:HD] * scale
        total = first[LSUM : LSUM + 1] * scale
        for y, y_total, y_peak in spread:
            scale = jnp.exp2(y_peak - peak)
            acc = acc + y[:HD] * scale
            total = total + y_total * scale
        out_ref[h * HD : (h + 1) * HD] = (acc / total).astype(bf16)


def merge(base, offs, near_part, mids, wides, fars, blocks):
    whole = [
        pl.BlockSpec(x.shape, lambda i, base: (0, 0, 0)) for x in (*wides, *fars)
    ]
    return pl.pallas_call(
        merge_kernel,
        grid_spec=pltpu.PrefetchScalarGridSpec(
            num_scalar_prefetch=1,
            grid=(blocks,),
            in_specs=[
                SMEM,
                pl.BlockSpec((HEADS_HERE, ROWS, BLOCK), lambda i, base: (0, 0, i)),
                pl.BlockSpec((HEADS_HERE, ROWS, 256), lambda i, base: (0, 0, base[0] + i)),
                pl.BlockSpec((HEADS_HERE, ROWS, 256), lambda i, base: (0, 0, base[0] + i)),
                *whole,
            ],
            out_specs=pl.BlockSpec((256, BLOCK), lambda i, base: (0, i)),
        ),
        out_shape=jax.ShapeDtypeStruct((256, blocks * BLOCK), bf16),
        compiler_params=params(),
        cost_estimate=cost(2 * blocks * BLOCK * 256, 6 * 2**20),
        name="merge",
    )(base, offs, near_part, *mids, *wides, *fars)


def project_kernel(a_ref, b_ref, wa_ref, wb_ref, out_ref):
    a = jnp.concatenate([a_ref[...], b_ref[...]], axis=0).T
    w = jnp.concatenate([wa_ref[...], wb_ref[...]], axis=0)
    out_ref[...] = dot(a, w).astype(bf16)


def project(a, b, wa, wb):
    rows, width = a.shape[1], wa.shape[1]
    tile = 512
    return pl.pallas_call(
        project_kernel,
        grid=(rows // tile,),
        in_specs=[
            pl.BlockSpec((256, tile), lambda i: (0, i)),
            pl.BlockSpec((256, tile), lambda i: (0, i)),
            pl.BlockSpec((256, width), lambda i: (0, 0)),
            pl.BlockSpec((256, width), lambda i: (0, 0)),
        ],
        out_specs=pl.BlockSpec((tile, width), lambda i: (i, 0)),
        out_shape=jax.ShapeDtypeStruct((rows, width), bf16),
        compiler_params=params(),
        cost_estimate=pl.CostEstimate(flops=2 * rows * 512 * width, bytes_accessed=12 * 2**20, transcendentals=0),
        name="project",
    )(a, b, wa, wb)


def place(s):
    return s >> 4, s >> 3 & 1, s >> 1 & 3, s & 1


def index(z, xh, y, core):
    return ((z * 2 + xh) * 4 + y) * 2 + core


def send(x, to):
    pairs = []
    for s in range(64):
        target = to(*place(s))
        if target is not None:
            pairs.append((s, index(*target)))
    return lax.ppermute(x, "seq", pairs)


def other_core(x):
    return send(x, lambda z, xh, y, c: (z, xh, y, 1 - c))


def y_step(x, by):
    return send(x, lambda z, xh, y, c: (z, xh, (y + by) % 4, c))


def later_z(x, by):
    return send(x, lambda z, xh, y, c: (z + by, xh, y, c) if z + by < 4 else None)


def earlier_z(x, by):
    return send(x, lambda z, xh, y, c: (z - by, xh, y, c) if z >= by else None)


def ints(*values):
    return jnp.stack([jnp.asarray(v, jnp.int32) for v in values])


def per_device(queries, keys, values, offsets, out_weight):
    head = lax.axis_index("head")
    z, xh, y, core = place(lax.axis_index("seq"))
    offs = lax.dynamic_slice_in_dim(offsets, head * HEADS_HERE, HEADS_HERE, 1)
    swap_heads = lambda x: lax.ppermute(x, "head", [(0, 1), (1, 0)])

    weight_other = swap_heads(out_weight)
    vt, kv_mid, kv_few, q_mid, q_wide, q_far = select(offs, queries, keys, values)

    below = y_step(kv_few, 1)
    above = y_step(kv_few, -1)
    q_wide_in = send(q_wide, lambda z, xh, y, c: (z, 0, y, c) if xh == 1 else None)
    q_far_in = [earlier_z(q_far, d) for d in (1, 2, 3)]
    kv_few_core = other_core(kv_few)
    kv_mid_core = send(kv_mid, lambda z, xh, y, c: (z, xh, y, 1) if c == 0 else None)
    across = y_step(above, -1)
    kv_mid_below = send(kv_mid, lambda z, xh, y, c: (z, xh, y + 1, c) if y % 2 == 0 else None)
    few_here = [kv_few, below, above, across]
    few_core = [kv_few_core] + [other_core(x) for x in few_here[1:]]
    far_here = jnp.concatenate([x[256:] for x in few_here], axis=0)
    far_xh = send(far_here, lambda z, xh, y, c: (z, 1 - xh, y, c))
    far_xh_core = other_core(far_xh)
    kv_mid_below_core = other_core(kv_mid_below)

    other = 1 - head
    near_other = near(ints(2 * other), queries, keys, vt, 2)
    near_own = near(ints(2 * head), queries, keys, vt, 2)
    mid_a = mid(True, ints(core), q_mid, kv_mid, kv_mid_core)

    ys = [y, (y + 3) % 4, (y + 1) % 4, (y + 2) % 4]
    everything, nothing = 1 << 20, -(1 << 20)
    wide_pos = [
        (y * 2 + core) * 256,
        jnp.where(xh == 0, everything, nothing),
        *[(p * 2 + core) * 256 for p in ys],
        *[(p * 2 + 1 - core) * 256 for p in ys],
    ]
    wide = pool("wide", (256, 320), 0, ints(*wide_pos), [q_wide, q_wide_in], few_here + few_core)
    wide_back = send(wide[:, :, 256:], lambda z, xh, y, c: (z, 1, y, c) if xh == 0 else None)

    far_pos = [
        ((xh * 4 + y) * 2 + core) * 64,
        *[jnp.where(z + d < 4, everything, nothing) for d in (1, 2, 3)],
        *[((xh * 4 + p) * 2 + core) * 64 for p in ys],
        *[((xh * 4 + p) * 2 + 1 - core) * 64 for p in ys],
        *[(((1 - xh) * 4 + p) * 2 + core) * 64 for p in ys],
        *[(((1 - xh) * 4 + p) * 2 + 1 - core) * 64 for p in ys],
    ]
    far_kvs = [x[256:] for x in few_here + few_core] + [far_xh, far_xh_core]
    far = pool("far", (64, 64), 0, ints(*far_pos), [q_far, *q_far_in], far_kvs)
    far_back = [later_z(far[:, :, d * 64 : (d + 1) * 64], d) for d in (1, 2, 3)]

    mid_b = mid(False, ints(y % 2), q_mid, kv_mid_below, kv_mid_below_core)

    parts = ((mid_a, mid_b), (wide, wide_back), (far, *far_back))
    attended_other = merge(ints(2 * other), offs, near_other, *parts, 2)
    received = swap_heads(attended_other)
    attended_own = merge(ints(2 * head), offs, near_own, *parts, 2)
    return project(attended_own, received, out_weight, weight_other)


def solution(mesh):
    return jax.shard_map(
        per_device,
        mesh=mesh,
        in_specs=(P("seq", "head"), P("seq", "head"), P("seq", "head"), P(), P("head", None)),
        out_specs=P(("seq", "head"), None),
        check_vma=False,
    )
```

```python
import functools
import math

import jax
import jax.numpy as jnp
from jax import lax
from jax.experimental import pallas as pl
from jax.experimental.pallas import tpu as pltpu
from jax.sharding import PartitionSpec as P

HD = 128
HEADS_HERE = 2
RATES = (4, 16, 64)
BLOCK = 1024
TILE = 256
ROWS = 144
LSUM = 128
MROW = 129
LOG2_SCALE = math.log2(math.e) / math.sqrt(HD)
FILL = -1e30
SMALL, LARGE = 2.0**-60, 2.0**100
VMEM_BYTES = 56 * 2**20
MID, WIDE, FAR = 1024, 256, 64
FEW = WIDE + FAR
OFFS, OFFS_OTHER, ORDER, HALF, HALF_OTHER, CORE, Y_ODD, WIDE_POS, FAR_POS = 0, 6, 12, 16, 17, 18, 19, 20, 30

f32, bf16 = jnp.float32, jnp.bfloat16


def dot(a, b):
    return jnp.dot(a, b, preferred_element_type=f32)


def aligned(x, n):
    return x if isinstance(x, int) else pl.multiple_of(x, n)


def transposed_queries(q):
    q = q.astype(f32) * LOG2_SCALE
    high = q.astype(bf16)
    low = (q - high.astype(f32)).astype(bf16)
    return jnp.concatenate([high, low], axis=1).T


def scores(k, qt):
    return dot(jnp.concatenate([k, k], axis=1), qt)


def with_ones(v):
    return jnp.concatenate([v.T, jnp.ones((ROWS - HD, v.shape[0]), v.dtype)], axis=0)


def pieces(x):
    first = x.astype(bf16).astype(f32)
    second = (x - first).astype(bf16).astype(f32)
    return first, second, x - first - second


def stat_rows(total, exponent, count):
    row = lax.broadcasted_iota(jnp.int32, (ROWS - HD, count), 0)
    parts = (total,) + (pieces(exponent) if exponent is not None else ())
    out = jnp.zeros((ROWS - HD, count), f32)
    for n, part in enumerate(parts):
        out = jnp.where(row == n, part, out)
    return out


def within_range(total, counted=None):
    ok = (total >= SMALL) & (total <= LARGE)
    if counted is not None:
        ok = ok | ~counted
    return jnp.min(jnp.where(ok, 1.0, 0.0)) > 0.5


def rescaled(store, get_queries, count, blocks, block):
    def step(j, carry):
        peak, acc = carry
        k, vt, allowed = block(j)
        s = jnp.where(allowed, scores(k, get_queries()), FILL)
        new = jnp.maximum(peak, jnp.max(s, axis=0, keepdims=True))
        p = jnp.where(allowed, jnp.exp2(s - new), 0.0)
        return new, acc * jnp.exp2(peak - new) + dot(vt, p.astype(bf16))

    peak, acc = lax.fori_loop(
        0, blocks, step, (jnp.full((1, count), FILL, f32), jnp.zeros((ROWS, count), f32))
    )
    store(acc, acc[LSUM : LSUM + 1], peak)


def position_mask(key_first, query_pos, rows):
    key_pos = key_first + lax.broadcasted_iota(jnp.int32, (rows, query_pos.shape[1]), 0)
    return key_pos <= query_pos


def lane_positions(first, count):
    return first + lax.broadcasted_iota(jnp.int32, (1, count), 1)


def pick(x_ref, cols, scr, off_ref, outs):
    scr[...] = x_ref[:, cols].astype(f32)
    step = pl.program_id(0)
    for level, (out_ref, row, out_cols) in enumerate(outs):
        count = scr.shape[0] // RATES[level]
        picked = scr[pl.ds(off_ref[OFFS + level * HEADS_HERE + scr_head(cols)], count, stride=RATES[level]), :]
        first = pl.multiple_of(row + step * count, 16)
        out_ref[pl.ds(first, count), out_cols] = picked.astype(bf16)


def scr_head(cols):
    return cols.start // HD


def select_kv_kernel(info_ref, k_ref, v_ref, kv_ref, few_ref, scr):
    for h in range(HEADS_HERE):
        cols = slice(h * HD, (h + 1) * HD)
        for n, x_ref in enumerate((k_ref, v_ref)):
            out_cols = slice((2 * n + h) * HD, (2 * n + h + 1) * HD)
            pick(x_ref, cols, scr.at[n, h], info_ref, ((kv_ref, 0, out_cols), (kv_ref, MID, out_cols), (kv_ref, MID + WIDE, out_cols)))

    @pl.when(pl.program_id(0) == pl.num_programs(0) - 1)
    def _():
        few_ref[...] = kv_ref[MID:]


def select_q_kernel(info_ref, q_ref, v_ref, qm_ref, qw_ref, qf_ref, vt_ref, scr):
    for h in range(HEADS_HERE):
        cols = slice(h * HD, (h + 1) * HD)
        pick(q_ref, cols, scr.at[h], info_ref, ((qm_ref, 0, cols), (qw_ref, 0, cols), (qf_ref, 0, cols)))
        vt_ref[h] = with_ones(v_ref[:, cols])


def vmem(count):
    return [pl.BlockSpec(memory_space=pltpu.VMEM)] * count


SMEM = pl.BlockSpec(memory_space=pltpu.SMEM)
ANY = pl.BlockSpec(memory_space=pl.ANY)


def whole(shape):
    return pl.BlockSpec(shape, lambda *_: (0,) * len(shape))


def params():
    return pltpu.CompilerParams(vmem_limit_bytes=VMEM_BYTES)


def cost(pairs, bytes_accessed):
    return pl.CostEstimate(
        flops=int(pairs * 1024 * 1.5), bytes_accessed=int(bytes_accessed), transcendentals=int(pairs)
    )


def shaped(*shape, dtype=bf16):
    return jax.ShapeDtypeStruct(shape, dtype)


def select_kv(info, k, v):
    chunk = pl.BlockSpec((BLOCK, 256), lambda i: (i, 0))
    return pl.pallas_call(
        select_kv_kernel,
        grid=(k.shape[0] // BLOCK,),
        in_specs=[SMEM, chunk, chunk],
        out_specs=[whole((MID + FEW, 512)), whole((FEW, 512))],
        out_shape=[shaped(MID + FEW, 512), shaped(FEW, 512)],
        scratch_shapes=[pltpu.VMEM((2, HEADS_HERE, BLOCK, HD), f32)],
        compiler_params=params(),
        name="select_kv",
    )(info, k, v)


def select_q(info, q, v):
    tok = q.shape[0]
    chunk = pl.BlockSpec((BLOCK, 256), lambda i: (i, 0))
    return pl.pallas_call(
        select_q_kernel,
        grid=(tok // BLOCK,),
        in_specs=[SMEM, chunk, chunk],
        out_specs=[
            whole((MID, 256)),
            whole((WIDE, 256)),
            whole((FAR, 256)),
            pl.BlockSpec((HEADS_HERE, ROWS, BLOCK), lambda i: (0, 0, i)),
        ],
        out_shape=[shaped(MID, 256), shaped(WIDE, 256), shaped(FAR, 256), shaped(HEADS_HERE, ROWS, tok)],
        scratch_shapes=[pltpu.VMEM((HEADS_HERE, BLOCK, HD), f32)],
        compiler_params=params(),
        name="select_q",
    )(info, q, v)


def pack_kernel(after_ref, *refs):
    *src, all_ref, far_ref, sems = refs
    copies = []
    row = 0
    for x_ref in src[1:]:
        rows = x_ref.shape[0]
        copies.append((x_ref, all_ref.at[row : row + rows]))
        row += rows
    for n, x_ref in enumerate(src):
        rows = x_ref.shape[0]
        copies.append((x_ref.at[rows - FAR : rows], far_ref.at[n * FAR : (n + 1) * FAR]))
    copies = [pltpu.make_async_copy(a, b, sems.at[n]) for n, (a, b) in enumerate(copies)]
    for copy in copies:
        copy.start()
    for copy in copies:
        copy.wait()


def pack(after, few, below, above, across):
    total = below.shape[0] + above.shape[0] + across.shape[0]
    return pl.pallas_call(
        pack_kernel,
        in_specs=[ANY] * 5,
        out_specs=[ANY, ANY],
        out_shape=[shaped(total, 512), shaped(4 * FAR, 512)],
        scratch_shapes=[pltpu.SemaphoreType.DMA((7,))],
        cost_estimate=pl.CostEstimate(flops=0, bytes_accessed=4 * 2**20, transcendentals=0),
        name="pack",
    )(after, few, below, above, across)


def diagonal(out_ref, h, k, vt, qt_ref):
    row = lax.broadcasted_iota(jnp.int32, (TILE, TILE), 0)
    col = lax.broadcasted_iota(jnp.int32, (TILE, TILE), 1)
    rows = []
    for g in range(BLOCK // TILE):
        first = g * TILE
        p = jnp.exp2(scores(k[first : first + TILE], qt_ref[h, :, first:]))
        parts = [jnp.where(row <= col, p[:, :TILE], 0.0), p[:, TILE:]]
        if g:
            parts = [jnp.zeros((TILE, first), f32)] + parts
        rows.append(jnp.concatenate([x for x in parts if x.shape[1]], axis=1).astype(bf16))
    out_ref[h] += dot(vt, jnp.concatenate(rows, axis=0))


def store_partial(out_ref, h, acc, total, exponent):
    count = acc.shape[1]
    out_ref[h, :HD] = acc[:HD]
    out_ref[h, HD:] = stat_rows(total, exponent, count)


def near_kernel(info_ref, q_ref, k_ref, vt_ref, out_ref, early_ref, qt):
    step = pl.program_id(0)
    block = info_ref[ORDER + step]
    for h in range(HEADS_HERE):
        qt[h] = transposed_queries(q_ref[:, h * HD : (h + 1) * HD])
    out_ref[...] = jnp.zeros(out_ref.shape, f32)

    def full(j, carry):
        start = aligned(j * BLOCK, BLOCK)
        for h in range(HEADS_HERE):
            s = scores(k_ref[pl.ds(start, BLOCK), h * HD : (h + 1) * HD], qt[h])
            out_ref[h] += dot(vt_ref[h, :, pl.ds(start, BLOCK)], jnp.exp2(s).astype(bf16))
        return carry

    lax.fori_loop(0, block, full, 0)
    start = aligned(block * BLOCK, BLOCK)
    for h in range(HEADS_HERE):
        cols = slice(h * HD, (h + 1) * HD)
        diagonal(out_ref, h, k_ref[pl.ds(start, BLOCK), cols], vt_ref[h, :, pl.ds(start, BLOCK)], qt)
    total = jnp.concatenate([out_ref[h, LSUM : LSUM + 1] for h in range(HEADS_HERE)], axis=0)
    ok = within_range(total)
    for h in range(HEADS_HERE):
        out_ref[h, HD:] = stat_rows(total[h : h + 1], None, BLOCK)

    @pl.when(jnp.logical_not(ok))
    def _():
        for h in range(HEADS_HERE):
            cols = slice(h * HD, (h + 1) * HD)
            query_pos = lane_positions(block * BLOCK, BLOCK)

            def key_block(j):
                first = aligned(j * TILE, TILE)
                return (
                    k_ref[pl.ds(first, TILE), cols],
                    vt_ref[h, :, pl.ds(first, TILE)],
                    position_mask(first, query_pos, TILE),
                )

            rescaled(
                functools.partial(store_partial, out_ref, h),
                lambda: qt[h],
                BLOCK,
                (block + 1) * (BLOCK // TILE),
                key_block,
            )

    @pl.when(step < 2)
    def _():
        for h in range(HEADS_HERE):
            early_ref[h * HD : (h + 1) * HD] = (out_ref[h, :HD] / out_ref[h, LSUM : LSUM + 1]).astype(bf16)


def near(info, q, k, vt):
    tok = q.shape[0]
    return pl.pallas_call(
        near_kernel,
        grid_spec=pltpu.PrefetchScalarGridSpec(
            num_scalar_prefetch=1,
            grid=(tok // BLOCK,),
            in_specs=[
                pl.BlockSpec((BLOCK, 256), lambda i, info: (info[ORDER + i], 0)),
                whole((tok, 256)),
                whole((HEADS_HERE, ROWS, tok)),
            ],
            out_specs=[
                pl.BlockSpec((HEADS_HERE, ROWS, BLOCK), lambda i, info: (0, 0, i)),
                pl.BlockSpec((256, BLOCK), lambda i, info: (0, jnp.minimum(i, 1))),
            ],
            scratch_shapes=[pltpu.VMEM((HEADS_HERE, 256, BLOCK), bf16)],
        ),
        out_shape=[shaped(HEADS_HERE, ROWS, tok, dtype=f32), shaped(256, tok // 2)],
        compiler_params=params(),
        cost_estimate=cost(2 * tok * 2300, 10 * 2**20),
        name="near",
    )(info, q, k, vt)


def mid_kernel(causal, flag_at, info_ref, q_ref, *refs):
    *kv_refs, out_ref, qt, vt = refs
    others = info_ref[flag_at] == 1
    for h in range(HEADS_HERE):
        qt[h] = transposed_queries(q_ref[:, h * HD : (h + 1) * HD])
    out_ref[...] = jnp.zeros(out_ref.shape, f32)

    def keys(n, h):
        return kv_refs[n].at[:, h * HD : (h + 1) * HD]

    def values(n):
        for h in range(HEADS_HERE):
            vt[n, h] = with_ones(kv_refs[n][:, (2 + h) * HD : (3 + h) * HD])

    if causal:
        values(0)
        for h in range(HEADS_HERE):
            diagonal(out_ref, h, keys(0, h)[...], vt[0, h], qt)

    @pl.when(others)
    def _():
        for n in range(1 if causal else 0, len(kv_refs)):
            values(n)
            for h in range(HEADS_HERE):
                p = jnp.exp2(scores(keys(n, h)[...], qt[h])).astype(bf16)
                out_ref[h] += dot(vt[n, h], p)

    total = jnp.concatenate([out_ref[h, LSUM : LSUM + 1] for h in range(HEADS_HERE)], axis=0)
    ok = within_range(total)
    for h in range(HEADS_HERE):
        out_ref[h, HD:] = stat_rows(total[h : h + 1], None, BLOCK)

    @pl.when(jnp.logical_and(jnp.logical_not(ok), True if causal else others))
    def _():
        for h in range(HEADS_HERE):
            query_pos = lane_positions(0, BLOCK)
            peak = jnp.full((1, BLOCK), FILL, f32)
            acc = jnp.zeros((ROWS, BLOCK), f32)
            for n in range(len(kv_refs)):
                own = causal and n == 0
                key_first = 0 if own else jnp.where(others, -BLOCK, BLOCK)

                def step(j, carry):
                    peak, acc = carry
                    first = aligned(j * TILE, TILE)
                    allowed = position_mask(key_first + first, query_pos, TILE)
                    s = jnp.where(allowed, scores(keys(n, h)[pl.ds(first, TILE), :], qt[h]), FILL)
                    new = jnp.maximum(peak, jnp.max(s, axis=0, keepdims=True))
                    p = jnp.where(allowed, jnp.exp2(s - new), 0.0)
                    vt_tile = with_ones(kv_refs[n][pl.ds(first, TILE), (2 + h) * HD : (3 + h) * HD])
                    return new, acc * jnp.exp2(peak - new) + dot(vt_tile, p.astype(bf16))

                peak, acc = lax.fori_loop(0, BLOCK // TILE, step, (peak, acc))
            store_partial(out_ref, h, acc, acc[LSUM : LSUM + 1], peak)


def mid(causal, flag_at, info, q, *kvs):
    return pl.pallas_call(
        functools.partial(mid_kernel, causal, flag_at),
        grid=(1,),
        in_specs=[SMEM, whole((MID, 256))] + [whole((MID, 512))] * len(kvs),
        out_specs=whole((HEADS_HERE, ROWS, BLOCK)),
        out_shape=shaped(HEADS_HERE, ROWS, BLOCK, dtype=f32),
        scratch_shapes=[
            pltpu.VMEM((HEADS_HERE, 256, BLOCK), bf16),
            pltpu.VMEM((len(kvs), HEADS_HERE, ROWS, BLOCK), bf16),
        ],
        compiler_params=params(),
        cost_estimate=cost(2 * BLOCK * BLOCK * 1.8, 5 * 2**20),
        name="mid",
    )(info, q, *kvs)


def pool_kernel(rows, places, q_count, pos_at, info_ref, *refs):
    q_refs = refs[:q_count]
    kv_refs = refs[q_count : len(refs) - q_count - 4]
    out_refs = refs[len(refs) - q_count - 4 : -4]
    kv, qt, vt, sems = refs[-4:]
    block_rows = q_refs[0].shape[0]
    count = q_count * block_rows
    total_keys = kv.shape[0]
    chunk = min(total_keys, 1024)
    copies = []
    for n, (ref, row) in enumerate(places):
        copies.append(
            pltpu.make_async_copy(
                kv_refs[ref].at[row : row + rows], kv.at[n * rows : (n + 1) * rows], sems.at[n]
            )
        )
    for copy in copies:
        copy.start()
    query_pos = jnp.concatenate([lane_positions(info_ref[pos_at + n], block_rows) for n in range(q_count)], axis=1)
    counted = query_pos >= 0
    key_iota = lax.broadcasted_iota(jnp.int32, (rows, 1), 0)
    key_pos = jnp.concatenate([info_ref[pos_at + q_count + n] + key_iota for n in range(len(places))], axis=0)
    for h in range(HEADS_HERE):
        q = jnp.concatenate([q_ref[:, h * HD : (h + 1) * HD] for q_ref in q_refs], axis=0)
        qt[h] = transposed_queries(q)
    for copy in copies:
        copy.wait()

    def store(h, acc, total, peak):
        for n in range(q_count):
            cols = slice(n * block_rows, (n + 1) * block_rows)
            store_partial(out_refs[n], h, acc[:, cols], total[:, cols], None if peak is None else peak[:, cols])

    def keys(h, first, size):
        return kv[first : first + size, h * HD : (h + 1) * HD]

    totals = []
    for h in range(HEADS_HERE):
        vt[h] = with_ones(kv[:, (2 + h) * HD : (3 + h) * HD])
    for h in range(HEADS_HERE):
        acc = jnp.zeros((ROWS, count), f32)
        for first in range(0, total_keys, chunk):
            s = scores(keys(h, first, chunk), qt[h])
            allowed = key_pos[first : first + chunk] <= query_pos
            p = jnp.where(allowed, jnp.exp2(s), 0.0).astype(bf16)
            acc = acc + dot(vt[h, :, first : first + chunk], p)
        total = acc[LSUM : LSUM + 1]
        totals.append(jnp.where(counted, total, 1.0))
        store(h, acc, total, None)

    @pl.when(jnp.logical_not(within_range(jnp.concatenate(totals, axis=0))))
    def _():
        for h in range(HEADS_HERE):
            peak = jnp.full((1, count), FILL, f32)
            acc = jnp.zeros((ROWS, count), f32)
            for first in range(0, total_keys, TILE):
                allowed = key_pos[first : first + TILE] <= query_pos
                s = jnp.where(allowed, scores(keys(h, first, TILE), qt[h]), FILL)
                new = jnp.maximum(peak, jnp.max(s, axis=0, keepdims=True))
                p = jnp.where(allowed, jnp.exp2(s - new), 0.0).astype(bf16)
                acc = acc * jnp.exp2(peak - new) + dot(vt[h, :, first : first + TILE], p)
                peak = new
            store(h, acc, acc[LSUM : LSUM + 1], peak)


def pool(name, rows, places, pos_at, info, qs, kvs):
    count = sum(q.shape[0] for q in qs)
    keys = len(places) * rows
    return pl.pallas_call(
        functools.partial(pool_kernel, rows, tuple(places), len(qs), pos_at),
        in_specs=[SMEM] + vmem(len(qs)) + [ANY] * len(kvs),
        out_specs=vmem(len(qs)),
        out_shape=[shaped(HEADS_HERE, ROWS, q.shape[0], dtype=f32) for q in qs],
        scratch_shapes=[
            pltpu.VMEM((keys, 512), bf16),
            pltpu.VMEM((HEADS_HERE, 256, count), bf16),
            pltpu.VMEM((HEADS_HERE, ROWS, keys), bf16),
            pltpu.SemaphoreType.DMA((len(places),)),
        ],
        compiler_params=params(),
        cost_estimate=cost(2 * count * keys, 4 * 2**20),
        name=name,
    )(info, *qs, *kvs)


def exponent_of(x):
    m = x[MROW : MROW + 1] + x[MROW + 1 : MROW + 2] + x[MROW + 2 : MROW + 3]
    return jnp.where(x[LSUM : LSUM + 1] > 0.0, m, FILL)


def combined(parts):
    peaks = [exponent_of(x) for x in parts]
    peak = functools.reduce(jnp.maximum, peaks)
    out = sum(x[: LSUM + 1] * jnp.exp2(m - peak) for x, m in zip(parts, peaks))
    return out, peak


def split_rows(sums, total, peak):
    rows = pieces(total) + (pieces(peak) if peak is not None else ())
    row = lax.broadcasted_iota(jnp.int32, (ROWS - HD, total.shape[1]), 0)
    stats = jnp.zeros((ROWS - HD, total.shape[1]), f32)
    for n, r in enumerate(rows):
        stats = jnp.where(row == n, r, stats)
    return jnp.concatenate([sums, stats], axis=0).astype(bf16)


def wider(x, count):
    return x if x.shape[1] == count else jnp.concatenate([x, jnp.zeros((x.shape[0], count - x.shape[1]), x.dtype)], axis=1)


def one_hot(targets, count):
    parts = []
    for rows, rate, first in targets:
        row = lax.broadcasted_iota(jnp.int32, (rows, count), 0) * rate + first
        parts.append(jnp.where(row == lax.broadcasted_iota(jnp.int32, (rows, count), 1), 1.0, 0.0).astype(bf16))
    return jnp.concatenate(parts, axis=0)


def merge_kernel(for_other, info_ref, near_ref, mid_a, mid_b, wide_a, wide_b, far_a, far_b, far_c, far_d, out_ref, att):
    step = pl.program_id(0)
    half = info_ref[HALF_OTHER if for_other else HALF]
    start = (2 * half + step) * BLOCK
    parts = [near_ref, mid_a, mid_b, wide_a, wide_b, far_a, far_b, far_c, far_d]
    largest = functools.reduce(
        jnp.maximum, [jnp.max(jnp.abs(x[:, MROW : MROW + 1])) for x in parts]
    )
    for h in range(HEADS_HERE):
        rows = slice(h * HD, (h + 1) * HD)
        offs = [info_ref[OFFS + level * HEADS_HERE + h] for level in range(3)]
        take = one_hot(
            (
                (256, RATES[0], offs[0]),
                (128, RATES[1], offs[1] + half * 2 * BLOCK - start),
                (128, RATES[2], offs[2] - start),
            ),
            BLOCK,
        )

        @pl.when(largest == 0.0)
        def _():
            groups = [mid_a[h] + mid_b[h], wide_a[h] + wide_b[h], wider(far_a[h] + far_b[h] + far_c[h] + far_d[h], 128)]
            x = jnp.concatenate(
                [split_rows(g[:HD], g[LSUM : LSUM + 1], None) for g in groups], axis=1
            )
            y = dot(x, take)
            total = near_ref[h, LSUM : LSUM + 1] + y[HD : HD + 1] + y[HD + 1 : HD + 2] + y[HD + 2 : HD + 3]
            att[rows] = ((near_ref[h, :HD] + y[:HD]) / total).astype(bf16)

        @pl.when(largest != 0.0)
        def _():
            first = near_ref[h]
            spread = []
            peak = exponent_of(first)
            row = 0
            for level in ((mid_a, mid_b), (wide_a, wide_b), (far_a, far_b, far_c, far_d)):
                x, x_peak = combined([part[h] for part in level])
                count = max(x.shape[1], 128)
                split = wider(split_rows(x[:HD], x[LSUM : LSUM + 1], x_peak), count)
                y = dot(split, take[row : row + count])
                row += count
                total = y[128:129] + y[129:130] + y[130:131]
                y_peak = jnp.where(total > 0.0, y[131:132] + y[132:133] + y[133:134], FILL)
                spread.append((y, total, y_peak))
                peak = jnp.maximum(peak, y_peak)
            scale = jnp.exp2(exponent_of(first) - peak)
            acc = first[:HD] * scale
            total = first[LSUM : LSUM + 1] * scale
            for y, y_total, y_peak in spread:
                scale = jnp.exp2(y_peak - peak)
                acc = acc + y[:HD] * scale
                total = total + y_total * scale
            att[rows] = (acc / total).astype(bf16)

        if for_other:
            picked = lax.dot_general(
                att[rows], take, (((1,), (1,)), ((), ())), preferred_element_type=f32
            ).astype(bf16)
            out_ref[rows, pl.ds(aligned(step * 256, 256), 256)] = picked[:, :256]

            @pl.when(step == 0)
            def _():
                out_ref[rows, 512:] = picked[:, 256:]

            @pl.when(step > 0)
            def _():
                out_ref[rows, 512:] += picked[:, 256:]
        else:
            out_ref[rows] = att[rows]


def merge(for_other, info, near_part, mids, wides, fars):
    place_of = HALF_OTHER if for_other else HALF
    first = 0 if for_other else 2
    return pl.pallas_call(
        functools.partial(merge_kernel, for_other),
        grid_spec=pltpu.PrefetchScalarGridSpec(
            num_scalar_prefetch=1,
            grid=(2,),
            in_specs=[
                pl.BlockSpec((HEADS_HERE, ROWS, BLOCK), lambda i, info: (0, 0, first + i)),
                *[pl.BlockSpec((HEADS_HERE, ROWS, 256), lambda i, info: (0, 0, 2 * info[place_of] + i))] * 2,
                *[pl.BlockSpec((HEADS_HERE, ROWS, 128), lambda i, info: (0, 0, info[place_of]))] * 2,
                *[whole((HEADS_HERE, ROWS, FAR))] * 4,
            ],
            out_specs=whole((256, 768)) if for_other else pl.BlockSpec((256, BLOCK), lambda i, info: (0, i)),
            scratch_shapes=[pltpu.VMEM((256, BLOCK), bf16)],
        ),
        out_shape=shaped(256, 768 if for_other else 2 * BLOCK),
        compiler_params=params(),
        cost_estimate=cost(2 * 2 * BLOCK * 256, 6 * 2**20),
        name="merge",
    )(info, near_part, *mids, *wides, *fars)


def project_kernel(info_ref, own_ref, early_ref, late_ref, w_own, w_other, out_ref):
    tile = own_ref.shape[1]
    step = pl.program_id(0)
    half = info_ref[HALF]
    parts = [own_ref[...]]
    col = lane_positions(0, tile)
    for h in range(HEADS_HERE):
        rows = slice(h * HD, (h + 1) * HD)
        mid_off, wide_off, far_off = (info_ref[OFFS_OTHER + level * HEADS_HERE + h] for level in range(3))
        in_mid = wide_off % RATES[0] == mid_off
        far_done = jnp.logical_or(far_off % RATES[0] == mid_off, far_off % RATES[1] == wide_off)
        nowhere = -(1 << 20)
        start = step * tile
        take = one_hot(
            (
                (512, RATES[0], mid_off - start),
                (128, RATES[1], jnp.where(in_mid, nowhere, wide_off - start)),
                (128, RATES[2], jnp.where(far_done, nowhere, far_off - half * 2 * BLOCK - start)),
            ),
            tile,
        )
        late = dot(late_ref[rows], take)
        reached = (col % RATES[0] == mid_off) | (col % RATES[1] == wide_off) | (col % RATES[2] == far_off)
        parts.append(jnp.where(reached, late, early_ref[rows].astype(f32)).astype(bf16))
    w = jnp.concatenate([w_own[...], w_other[...]], axis=0)
    out_ref[...] = dot(jnp.concatenate(parts, axis=0).T, w).astype(bf16)


def project(info, own, early, late, w_own, w_other):
    rows, width = own.shape[1], w_own.shape[1]
    tile = 512
    return pl.pallas_call(
        project_kernel,
        grid=(rows // tile,),
        in_specs=[
            SMEM,
            pl.BlockSpec((256, tile), lambda i: (0, i)),
            pl.BlockSpec((256, tile), lambda i: (0, i)),
            whole((256, 768)),
            whole((256, width)),
            whole((256, width)),
        ],
        out_specs=pl.BlockSpec((tile, width), lambda i: (i, 0)),
        out_shape=shaped(rows, width),
        compiler_params=params(),
        cost_estimate=pl.CostEstimate(flops=2 * rows * 512 * width, bytes_accessed=12 * 2**20, transcendentals=0),
        name="project",
    )(info, own, early, late, w_own, w_other)


def place(s):
    return s >> 4, s >> 3 & 1, s >> 1 & 3, s & 1


def index(z, xh, y, core):
    return ((z * 2 + xh) * 4 + y) * 2 + core


def send(x, to):
    pairs = []
    for s in range(64):
        target = to(*place(s))
        if target is not None:
            pairs.append((s, index(*target)))
    return lax.ppermute(x, "seq", pairs)


def other_core(x):
    return send(x, lambda z, xh, y, c: (z, xh, y, 1 - c))


def y_step(x, by):
    return send(x, lambda z, xh, y, c: (z, xh, (y + by) % 4, c))


def later_z(x, by):
    return send(x, lambda z, xh, y, c: (z + by, xh, y, c) if z + by < 4 else None)


def earlier_z(x, by):
    return send(x, lambda z, xh, y, c: (z - by, xh, y, c) if z >= by else None)


def ints(*values):
    return jnp.stack([jnp.asarray(v, jnp.int32) for v in values])


def swap_heads(x):
    return lax.ppermute(x, "head", [(0, 1), (1, 0)])


def scalars(offsets):
    head = lax.axis_index("head")
    z, xh, y, core = place(lax.axis_index("seq"))
    other = 1 - head
    flat = offsets.astype(jnp.int32)

    def offs(group):
        return lax.dynamic_slice_in_dim(flat, group * HEADS_HERE, HEADS_HERE, 1).reshape(-1)

    ys = [y, (y + 3) % 4, (y + 1) % 4, (y + 2) % 4]
    everything, nothing = 1 << 20, -(1 << 20)
    wide_pos = [
        (y * 2 + core) * WIDE,
        jnp.where(xh == 0, everything, nothing),
        *[(p * 2 + c) * WIDE for c in (core, 1 - core) for p in ys],
    ]
    far_pos = [
        ((xh * 4 + y) * 2 + core) * FAR,
        *[jnp.where(z + d < 4, everything, nothing) for d in (1, 2, 3)],
        *[((x * 4 + p) * 2 + c) * FAR for x in (xh, 1 - xh) for c in (core, 1 - core) for p in ys],
    ]
    order = [2 * other, 2 * other + 1, 2 * head, 2 * head + 1]
    rest = order + [head, other, core, y % 2] + wide_pos + far_pos
    return jnp.concatenate([offs(head), offs(other), ints(*rest)])


def per_device(queries, keys, values, offsets, out_weight):
    weight_other = swap_heads(out_weight)
    info = scalars(offsets)
    kv, few = select_kv(info, keys, values)
    below = y_step(kv, 1)
    above = y_step(few, -1)
    across = y_step(few, 2)
    kv_core = other_core(kv)
    q_mid, q_wide, q_far, vt = select_q(info, queries, values)
    q_wide_in = send(q_wide, lambda z, xh, y, c: (z, 0, y, c) if xh == 1 else None)
    q_far_in = [earlier_z(q_far, d) for d in (1, 2, 3)]

    near_part, early_other = near(info, queries, keys, vt)

    packed, far_here = pack(near_part, few, below, above, across)
    packed_core = other_core(packed)
    far_xh = send(far_here, lambda z, xh, y, c: (z, 1 - xh, y, c))
    early = swap_heads(early_other)
    mid_a = mid(True, CORE, info, q_mid, kv, kv_core)
    far_xh_core = other_core(far_xh)

    sources = [few, below, above, across, kv_core, packed_core, far_xh, far_xh_core]
    third = MID + FEW
    starts = [(0, 0), (1, MID), (2, 0), (3, 0), (4, MID), (5, MID), (5, third), (5, third + FEW)]
    wide, wide_out = pool("wide", WIDE, starts, WIDE_POS, info, [q_wide, q_wide_in], sources[:6])
    wide_back = send(wide_out, lambda z, xh, y, c: (z, 1, y, c) if xh == 0 else None)

    far_starts = [(ref, row + WIDE) for ref, row in starts] + [(ref, n * FAR) for ref in (6, 7) for n in range(4)]
    far, *far_out = pool("far", FAR, far_starts, FAR_POS, info, [q_far, *q_far_in], sources)
    far_back = [later_z(x, d) for d, x in zip((1, 2, 3), far_out)]

    mid_b = mid(False, Y_ODD, info, q_mid, below, packed_core)

    parts = ((mid_a, mid_b), (wide, wide_back), (far, *far_back))
    late = swap_heads(merge(True, info, near_part, *parts))
    attended_own = merge(False, info, near_part, *parts)
    return project(info, attended_own, early, late, out_weight, weight_other)


def solution(mesh):
    return jax.shard_map(
        per_device,
        mesh=mesh,
        in_specs=(P("seq", "head"), P("seq", "head"), P("seq", "head"), P(), P("head", None)),
        out_specs=P(("seq", "head"), None),
        check_vma=False,
    )
```

```python
import functools
import math

import jax
import jax.numpy as jnp
from jax import lax
from jax.experimental import pallas as pl
from jax.experimental.pallas import tpu as pltpu
from jax.sharding import PartitionSpec as P

HD = 128
HEADS_HERE = 2
RATES = (4, 16, 64)
BLOCK = 1024
TILE = 256
ROWS = 144
LSUM = 128
MROW = 129
LOG2_SCALE = math.log2(math.e) / math.sqrt(HD)
FILL = -1e30
SMALL, LARGE = 2.0**-60, 2.0**100
VMEM_BYTES = 56 * 2**20
MID, WIDE, FAR = 1024, 256, 64
FEW = WIDE + FAR
OFFS, OFFS_OTHER, ORDER, HALF, HALF_OTHER, CORE, Y_ODD, WIDE_POS, FAR_POS = 0, 6, 12, 17, 18, 19, 20, 21, 31

f32, bf16 = jnp.float32, jnp.bfloat16


def dot(a, b):
    return jnp.dot(a, b, preferred_element_type=f32)


def aligned(x, n):
    return x if isinstance(x, int) else pl.multiple_of(x, n)


def transposed_queries(q):
    q = q.astype(f32) * LOG2_SCALE
    high = q.astype(bf16)
    low = (q - high.astype(f32)).astype(bf16)
    return jnp.concatenate([high, low], axis=1).T


def scores(k, qt):
    return dot(jnp.concatenate([k, k], axis=1), qt)


def with_ones(v):
    return jnp.concatenate([v.T, jnp.ones((ROWS - HD, v.shape[0]), v.dtype)], axis=0)


def pieces(x):
    first = x.astype(bf16).astype(f32)
    second = (x - first).astype(bf16).astype(f32)
    return first, second, x - first - second


def stat_rows(total, exponent, count):
    row = lax.broadcasted_iota(jnp.int32, (ROWS - HD, count), 0)
    parts = (total,) + (pieces(exponent) if exponent is not None else ())
    out = jnp.zeros((ROWS - HD, count), f32)
    for n, part in enumerate(parts):
        out = jnp.where(row == n, part, out)
    return out


def within_range(total, counted=None):
    ok = (total >= SMALL) & (total <= LARGE)
    if counted is not None:
        ok = ok | ~counted
    return jnp.min(jnp.where(ok, 1.0, 0.0)) > 0.5


def rescaled(store, get_queries, count, blocks, block):
    def step(j, carry):
        peak, acc = carry
        k, vt, allowed = block(j)
        s = jnp.where(allowed, scores(k, get_queries()), FILL)
        new = jnp.maximum(peak, jnp.max(s, axis=0, keepdims=True))
        p = jnp.where(allowed, jnp.exp2(s - new), 0.0)
        return new, acc * jnp.exp2(peak - new) + dot(vt, p.astype(bf16))

    peak, acc = lax.fori_loop(
        0, blocks, step, (jnp.full((1, count), FILL, f32), jnp.zeros((ROWS, count), f32))
    )
    store(acc, acc[LSUM : LSUM + 1], peak)


def position_mask(key_first, query_pos, rows):
    key_pos = key_first + lax.broadcasted_iota(jnp.int32, (rows, query_pos.shape[1]), 0)
    return key_pos <= query_pos


def lane_positions(first, count):
    return first + lax.broadcasted_iota(jnp.int32, (1, count), 1)


def pick(x_ref, cols, scr, off_ref, outs):
    scr[...] = x_ref[:, cols].astype(f32)
    step = pl.program_id(0)
    for level, (out_ref, row, out_cols) in enumerate(outs):
        count = scr.shape[0] // RATES[level]
        picked = scr[pl.ds(off_ref[OFFS + level * HEADS_HERE + scr_head(cols)], count, stride=RATES[level]), :]
        first = pl.multiple_of(row + step * count, 16)
        out_ref[pl.ds(first, count), out_cols] = picked.astype(bf16)


def scr_head(cols):
    return cols.start // HD


def select_kv_kernel(info_ref, k_ref, v_ref, mid_ref, few_ref, scr):
    for h in range(HEADS_HERE):
        cols = slice(h * HD, (h + 1) * HD)
        for n, x_ref in enumerate((k_ref, v_ref)):
            out_cols = slice((2 * n + h) * HD, (2 * n + h + 1) * HD)
            pick(x_ref, cols, scr.at[n, h], info_ref, ((mid_ref, 0, out_cols), (few_ref, 0, out_cols), (few_ref, WIDE, out_cols)))


def select_q_kernel(info_ref, q_ref, qm_ref, qw_ref, qf_ref, scr):
    for h in range(HEADS_HERE):
        cols = slice(h * HD, (h + 1) * HD)
        pick(q_ref, cols, scr.at[h], info_ref, ((qm_ref, 0, cols), (qw_ref, 0, cols), (qf_ref, 0, cols)))


def values_kernel(v_ref, after_ref, vt_ref):
    for h in range(HEADS_HERE):
        vt_ref[h] = with_ones(v_ref[:, h * HD : (h + 1) * HD])


def vmem(count):
    return [pl.BlockSpec(memory_space=pltpu.VMEM)] * count


SMEM = pl.BlockSpec(memory_space=pltpu.SMEM)
ANY = pl.BlockSpec(memory_space=pl.ANY)


def whole(shape):
    return pl.BlockSpec(shape, lambda *_: (0,) * len(shape))


def params():
    return pltpu.CompilerParams(vmem_limit_bytes=VMEM_BYTES)


def cost(pairs, bytes_accessed):
    return pl.CostEstimate(
        flops=int(pairs * 1024 * 1.5), bytes_accessed=int(bytes_accessed), transcendentals=int(pairs)
    )


def shaped(*shape, dtype=bf16):
    return jax.ShapeDtypeStruct(shape, dtype)


def select_kv(info, k, v):
    chunk = pl.BlockSpec((BLOCK, 256), lambda i: (i, 0))
    return pl.pallas_call(
        select_kv_kernel,
        grid=(k.shape[0] // BLOCK,),
        in_specs=[SMEM, chunk, chunk],
        out_specs=[whole((MID, 512)), whole((FEW, 512))],
        out_shape=[shaped(MID, 512), shaped(FEW, 512)],
        scratch_shapes=[pltpu.VMEM((2, HEADS_HERE, BLOCK, HD), f32)],
        compiler_params=params(),
        name="select_kv",
    )(info, k, v)


def select_q(info, q):
    return pl.pallas_call(
        select_q_kernel,
        grid=(q.shape[0] // BLOCK,),
        in_specs=[SMEM, pl.BlockSpec((BLOCK, 256), lambda i: (i, 0))],
        out_specs=[whole((MID, 256)), whole((WIDE, 256)), whole((FAR, 256))],
        out_shape=[shaped(MID, 256), shaped(WIDE, 256), shaped(FAR, 256)],
        scratch_shapes=[pltpu.VMEM((HEADS_HERE, BLOCK, HD), f32)],
        compiler_params=params(),
        name="select_q",
    )(info, q)


def transposed_values(v, after):
    tok = v.shape[0]
    return pl.pallas_call(
        values_kernel,
        grid=(tok // BLOCK,),
        in_specs=[pl.BlockSpec((BLOCK, 256), lambda i: (i, 0)), ANY],
        out_specs=pl.BlockSpec((HEADS_HERE, ROWS, BLOCK), lambda i: (0, 0, i)),
        out_shape=shaped(HEADS_HERE, ROWS, tok),
        compiler_params=params(),
        cost_estimate=cost(4 * tok * 256, 5 * 2**20),
        name="values",
    )(v, after)


def pack_kernel(count, *refs):
    *_, all_ref, far_ref = refs
    for n, x_ref in enumerate(refs[:count]):
        all_ref[n * FEW : (n + 1) * FEW] = x_ref[...]
        far_ref[n * FAR : (n + 1) * FAR] = x_ref[WIDE:]


def pack(few, after):
    count = len(few)
    return pl.pallas_call(
        functools.partial(pack_kernel, count),
        in_specs=vmem(count) + [ANY] * len(after),
        out_specs=vmem(2),
        out_shape=[shaped(count * FEW, 512), shaped(count * FAR, 512)],
        compiler_params=params(),
        cost_estimate=pl.CostEstimate(flops=0, bytes_accessed=4 * 2**20, transcendentals=0),
        name="pack",
    )(*few, *after)


def diagonal(out_ref, h, k, vt, qt_ref):
    row = lax.broadcasted_iota(jnp.int32, (TILE, TILE), 0)
    col = lax.broadcasted_iota(jnp.int32, (TILE, TILE), 1)
    rows = []
    for g in range(BLOCK // TILE):
        first = g * TILE
        p = jnp.exp2(scores(k[first : first + TILE], qt_ref[h, :, first:]))
        parts = [jnp.where(row <= col, p[:, :TILE], 0.0), p[:, TILE:]]
        if g:
            parts = [jnp.zeros((TILE, first), f32)] + parts
        rows.append(jnp.concatenate([x for x in parts if x.shape[1]], axis=1).astype(bf16))
    out_ref[h] += dot(vt, jnp.concatenate(rows, axis=0))


def store_partial(out_ref, h, acc, total, exponent):
    count = acc.shape[1]
    out_ref[h, :HD] = acc[:HD]
    out_ref[h, HD:] = stat_rows(total, exponent, count)


def near_kernel(first, skipped, info_ref, q_ref, k_ref, vt_ref, *refs):
    refs = refs[skipped:]
    block = info_ref[ORDER + first + pl.program_id(0)]

    @pl.when(block >= 0)
    def _():
        near_block(first, block, q_ref, k_ref, vt_ref, *refs)


def near_block(first, block, q_ref, k_ref, vt_ref, *refs):
    out_ref, *early_ref, qt = refs
    for h in range(HEADS_HERE):
        qt[h] = transposed_queries(q_ref[:, h * HD : (h + 1) * HD])
    out_ref[...] = jnp.zeros(out_ref.shape, f32)

    def full(j, carry):
        start = aligned(j * BLOCK, BLOCK)
        for h in range(HEADS_HERE):
            s = scores(k_ref[pl.ds(start, BLOCK), h * HD : (h + 1) * HD], qt[h])
            out_ref[h] += dot(vt_ref[h, :, pl.ds(start, BLOCK)], jnp.exp2(s).astype(bf16))
        return carry

    lax.fori_loop(0, block, full, 0)
    start = aligned(block * BLOCK, BLOCK)
    for h in range(HEADS_HERE):
        cols = slice(h * HD, (h + 1) * HD)
        diagonal(out_ref, h, k_ref[pl.ds(start, BLOCK), cols], vt_ref[h, :, pl.ds(start, BLOCK)], qt)
    total = jnp.concatenate([out_ref[h, LSUM : LSUM + 1] for h in range(HEADS_HERE)], axis=0)
    ok = within_range(total)
    for h in range(HEADS_HERE):
        out_ref[h, HD:] = stat_rows(total[h : h + 1], None, BLOCK)

    @pl.when(jnp.logical_not(ok))
    def _():
        for h in range(HEADS_HERE):
            cols = slice(h * HD, (h + 1) * HD)
            query_pos = lane_positions(block * BLOCK, BLOCK)

            def key_block(j):
                first = aligned(j * TILE, TILE)
                return (
                    k_ref[pl.ds(first, TILE), cols],
                    vt_ref[h, :, pl.ds(first, TILE)],
                    position_mask(first, query_pos, TILE),
                )

            rescaled(
                functools.partial(store_partial, out_ref, h),
                lambda: qt[h],
                BLOCK,
                (block + 1) * (BLOCK // TILE),
                key_block,
            )

    if early_ref:

        @pl.when(pl.program_id(0) < 2)
        def _():
            for h in range(HEADS_HERE):
                scale = 1.0 / out_ref[h, LSUM : LSUM + 1]
                early_ref[0][h * HD : (h + 1) * HD] = (out_ref[h, :HD] * scale).astype(bf16)


def near(first, steps, info, q, k, vt, after):
    tok = q.shape[0]
    early = first == 0
    return pl.pallas_call(
        functools.partial(near_kernel, first, len(after)),
        grid_spec=pltpu.PrefetchScalarGridSpec(
            num_scalar_prefetch=1,
            grid=(steps,),
            in_specs=[
                pl.BlockSpec((BLOCK, 256), lambda i, info: (jnp.maximum(info[ORDER + first + i], 0), 0)),
                whole((tok, 256)),
                whole((HEADS_HERE, ROWS, tok)),
            ]
            + [ANY] * len(after),
            out_specs=[pl.BlockSpec((HEADS_HERE, ROWS, BLOCK), lambda i, info: (0, 0, i))]
            + [pl.BlockSpec((256, BLOCK), lambda i, info: (0, jnp.minimum(i, 1)))] * early,
            scratch_shapes=[pltpu.VMEM((HEADS_HERE, 256, BLOCK), bf16)],
        ),
        out_shape=[shaped(HEADS_HERE, ROWS, steps * BLOCK, dtype=f32)] + [shaped(256, tok // 2)] * early,
        compiler_params=params(),
        cost_estimate=cost(steps * BLOCK * 2300 * 2, 10 * 2**20),
        name="near",
    )(info, q, k, vt, *after)


def mid_kernel(causal, flag_at, info_ref, q_ref, *refs):
    *kv_refs, out_ref, qt, vt = refs
    kv_refs = kv_refs[:2]
    others = info_ref[flag_at] == 1
    for h in range(HEADS_HERE):
        qt[h] = transposed_queries(q_ref[:, h * HD : (h + 1) * HD])
    out_ref[...] = jnp.zeros(out_ref.shape, f32)

    def keys(n, h):
        return kv_refs[n].at[:, h * HD : (h + 1) * HD]

    def values(n):
        for h in range(HEADS_HERE):
            vt[n, h] = with_ones(kv_refs[n][:, (2 + h) * HD : (3 + h) * HD])

    if causal:
        values(0)
        for h in range(HEADS_HERE):
            diagonal(out_ref, h, keys(0, h)[...], vt[0, h], qt)

    @pl.when(others)
    def _():
        for n in range(1 if causal else 0, len(kv_refs)):
            values(n)
            for h in range(HEADS_HERE):
                p = jnp.exp2(scores(keys(n, h)[...], qt[h])).astype(bf16)
                out_ref[h] += dot(vt[n, h], p)

    total = jnp.concatenate([out_ref[h, LSUM : LSUM + 1] for h in range(HEADS_HERE)], axis=0)
    ok = within_range(total)
    for h in range(HEADS_HERE):
        out_ref[h, HD:] = stat_rows(total[h : h + 1], None, BLOCK)

    @pl.when(jnp.logical_and(jnp.logical_not(ok), True if causal else others))
    def _():
        for h in range(HEADS_HERE):
            query_pos = lane_positions(0, BLOCK)
            peak = jnp.full((1, BLOCK), FILL, f32)
            acc = jnp.zeros((ROWS, BLOCK), f32)
            for n in range(len(kv_refs)):
                own = causal and n == 0
                key_first = 0 if own else jnp.where(others, -BLOCK, BLOCK)

                def step(j, carry):
                    peak, acc = carry
                    first = aligned(j * TILE, TILE)
                    allowed = position_mask(key_first + first, query_pos, TILE)
                    s = jnp.where(allowed, scores(keys(n, h)[pl.ds(first, TILE), :], qt[h]), FILL)
                    new = jnp.maximum(peak, jnp.max(s, axis=0, keepdims=True))
                    p = jnp.where(allowed, jnp.exp2(s - new), 0.0)
                    vt_tile = with_ones(kv_refs[n][pl.ds(first, TILE), (2 + h) * HD : (3 + h) * HD])
                    return new, acc * jnp.exp2(peak - new) + dot(vt_tile, p.astype(bf16))

                peak, acc = lax.fori_loop(0, BLOCK // TILE, step, (peak, acc))
            store_partial(out_ref, h, acc, acc[LSUM : LSUM + 1], peak)


def mid(causal, flag_at, info, q, kvs, after=()):
    return pl.pallas_call(
        functools.partial(mid_kernel, causal, flag_at),
        grid=(1,),
        in_specs=[SMEM, whole((MID, 256))] + [whole((MID, 512))] * len(kvs) + [ANY] * len(after),
        out_specs=whole((HEADS_HERE, ROWS, BLOCK)),
        out_shape=shaped(HEADS_HERE, ROWS, BLOCK, dtype=f32),
        scratch_shapes=[
            pltpu.VMEM((HEADS_HERE, 256, BLOCK), bf16),
            pltpu.VMEM((len(kvs), HEADS_HERE, ROWS, BLOCK), bf16),
        ],
        compiler_params=params(),
        cost_estimate=cost(2 * BLOCK * BLOCK * 1.8, 5 * 2**20),
        name="mid",
    )(info, q, *kvs, *after)


def pool_level(rows, pos_at, info_ref, q_refs, kv, qt, vt, out_refs):
    q_count = len(q_refs)
    block_rows = q_refs[0].shape[0]
    count = q_count * block_rows
    total_keys = kv.shape[0]
    chunk = min(total_keys, 1024)
    query_pos = jnp.concatenate([lane_positions(info_ref[pos_at + n], block_rows) for n in range(q_count)], axis=1)
    counted = query_pos >= 0
    key_iota = lax.broadcasted_iota(jnp.int32, (rows, 1), 0)
    key_pos = jnp.concatenate(
        [info_ref[pos_at + q_count + n] + key_iota for n in range(total_keys // rows)], axis=0
    )
    for h in range(HEADS_HERE):
        q = jnp.concatenate([q_ref[:, h * HD : (h + 1) * HD] for q_ref in q_refs], axis=0)
        qt[h] = transposed_queries(q)
        vt[h] = with_ones(kv[:, (2 + h) * HD : (3 + h) * HD])

    def store(h, acc, total, peak):
        for n in range(q_count):
            cols = slice(n * block_rows, (n + 1) * block_rows)
            peak_here = None if peak is None else peak[:, cols]
            if n == 0:
                store_partial(out_refs[n], h, acc[:, cols], total[:, cols], peak_here)
            else:
                out_refs[n][h] = split_rows(acc[:HD, cols], total[:, cols], peak_here)

    def keys(h, first, size):
        return kv[first : first + size, h * HD : (h + 1) * HD]

    totals = []
    for h in range(HEADS_HERE):
        acc = jnp.zeros((ROWS, count), f32)
        for first in range(0, total_keys, chunk):
            s = scores(keys(h, first, chunk), qt[h])
            allowed = key_pos[first : first + chunk] <= query_pos
            p = jnp.where(allowed, jnp.exp2(s), 0.0).astype(bf16)
            acc = acc + dot(vt[h, :, first : first + chunk], p)
        total = acc[LSUM : LSUM + 1]
        totals.append(jnp.where(counted, total, 1.0))
        store(h, acc, total, None)

    @pl.when(jnp.logical_not(within_range(jnp.concatenate(totals, axis=0))))
    def _():
        for h in range(HEADS_HERE):
            peak = jnp.full((1, count), FILL, f32)
            acc = jnp.zeros((ROWS, count), f32)
            for first in range(0, total_keys, TILE):
                allowed = key_pos[first : first + TILE] <= query_pos
                s = jnp.where(allowed, scores(keys(h, first, TILE), qt[h]), FILL)
                new = jnp.maximum(peak, jnp.max(s, axis=0, keepdims=True))
                p = jnp.where(allowed, jnp.exp2(s - new), 0.0).astype(bf16)
                acc = acc * jnp.exp2(peak - new) + dot(vt[h, :, first : first + TILE], p)
                peak = new
            store(h, acc, acc[LSUM : LSUM + 1], peak)


def level_kernel(rows, pos_at, places, q_count, info_ref, *refs):
    *refs, kv, qt, vt, sems = refs
    q_refs, sources, out_refs = refs[:q_count], refs[q_count:-q_count], refs[-q_count:]
    copies = []
    place = 0
    for n, (source, row, count) in enumerate(places):
        dst = kv.at[place : place + count]
        copies.append(pltpu.make_async_copy(sources[source].at[row : row + count], dst, sems.at[n]))
        place += count
    for copy in copies:
        copy.start()
    for copy in copies:
        copy.wait()
    pool_level(rows, pos_at, info_ref, q_refs, kv, qt, vt, out_refs)


def level(name, rows, pos_at, places, info, qs, sources):
    keys = sum(count for _, _, count in places)
    count = len(qs) * rows
    return pl.pallas_call(
        functools.partial(level_kernel, rows, pos_at, tuple(places), len(qs)),
        in_specs=[SMEM] + vmem(len(qs)) + [ANY] * len(sources),
        out_specs=vmem(len(qs)),
        out_shape=[shaped(HEADS_HERE, ROWS, rows, dtype=bf16 if n else f32) for n in range(len(qs))],
        scratch_shapes=[
            pltpu.VMEM((keys, 512), bf16),
            pltpu.VMEM((HEADS_HERE, 256, count), bf16),
            pltpu.VMEM((HEADS_HERE, ROWS, keys), bf16),
            pltpu.SemaphoreType.DMA((len(places),)),
        ],
        compiler_params=params(),
        cost_estimate=cost(2 * count * keys, 4 * 2**20),
        name=name,
    )(info, *qs, *sources)


def exponent_of(x):
    m = x[MROW : MROW + 1] + x[MROW + 1 : MROW + 2] + x[MROW + 2 : MROW + 3]
    return jnp.where(x[LSUM : LSUM + 1] > 0.0, m, FILL)


def combined(parts):
    peaks = [exponent_of(x) for x in parts]
    peak = functools.reduce(jnp.maximum, peaks)
    out = sum(x[: LSUM + 1] * jnp.exp2(m - peak) for x, m in zip(parts, peaks))
    return out, peak


def split_rows(sums, total, peak):
    rows = pieces(total) + (pieces(peak) if peak is not None else ())
    row = lax.broadcasted_iota(jnp.int32, (ROWS - HD, total.shape[1]), 0)
    stats = jnp.zeros((ROWS - HD, total.shape[1]), f32)
    for n, r in enumerate(rows):
        stats = jnp.where(row == n, r, stats)
    return jnp.concatenate([sums, stats], axis=0).astype(bf16)


def wider(x, count):
    return x if x.shape[1] == count else jnp.concatenate([x, jnp.zeros((x.shape[0], count - x.shape[1]), x.dtype)], axis=1)


def one_hot(targets, count):
    parts = []
    col = lax.broadcasted_iota(jnp.int32, (1, count), 1)
    for rows, rate, first in targets:
        at = col - first
        row_of = jnp.where(at & (rate - 1) == 0, at >> (rate.bit_length() - 1), -1)
        row = lax.broadcasted_iota(jnp.int32, (rows, count), 0)
        parts.append(jnp.where(row == row_of, 1.0, 0.0).astype(bf16))
    return jnp.concatenate(parts, axis=0)


def whole_form(x):
    x = x.astype(f32)
    total = x[LSUM : LSUM + 1] + x[LSUM + 1 : LSUM + 2] + x[LSUM + 2 : LSUM + 3]
    return jnp.concatenate([x[:HD], total, x[LSUM + 3 : LSUM + 6], x[LSUM + 6 :], x[LSUM + 6 : LSUM + 8]], axis=0)


def largest_exponent(parts, places):
    seen = []
    for x, place in zip(parts, places):
        for h in range(HEADS_HERE):
            row = jnp.abs(x[h, place : place + 1].astype(f32))
            width = min(row.shape[1], 128)
            for first in range(0, row.shape[1], width):
                seen.append(wider(row[:, first : first + width], 128))
    return jnp.max(functools.reduce(jnp.maximum, seen))


def merge_kernel(for_other, info_ref, near_ref, *refs):
    near_2, *refs = (None, *refs) if for_other else refs
    mid_a, mid_b, wide_a, wide_b, far_a, far_b, far_c, far_d, out_ref, att, first_ref = refs
    step = pl.program_id(0)
    half = info_ref[HALF_OTHER if for_other else HALF]
    start = (2 * half + step) * BLOCK
    if for_other:
        first_ref = near_ref
    else:
        in_first = jnp.logical_and(half == 1, step == 1)

        @pl.when(in_first)
        def _():
            first_ref[...] = near_ref[...]

        @pl.when(jnp.logical_not(in_first))
        def _():
            first_ref[...] = near_2[...]

    local, sent = [first_ref, mid_a, mid_b, wide_a, far_a], [wide_b, far_b, far_c, far_d]
    largest = largest_exponent(local + sent, [MROW] * len(local) + [LSUM + 3] * len(sent))
    for h in range(HEADS_HERE):
        rows = slice(h * HD, (h + 1) * HD)
        offs = [info_ref[OFFS + level * HEADS_HERE + h] for level in range(3)]
        take = one_hot(
            (
                (256, RATES[0], offs[0]),
                (128, RATES[1], offs[1] + half * 2 * BLOCK - start),
                (128, RATES[2], offs[2] - start),
            ),
            BLOCK,
        )

        @pl.when(largest == 0.0)
        def _():
            far = far_a[h] + whole_form(far_b[h]) + whole_form(far_c[h]) + whole_form(far_d[h])
            groups = [mid_a[h] + mid_b[h], wide_a[h] + whole_form(wide_b[h]), wider(far, 128)]
            x = jnp.concatenate(
                [split_rows(g[:HD], g[LSUM : LSUM + 1], None) for g in groups], axis=1
            )
            y = dot(x, take)
            total = first_ref[h, LSUM : LSUM + 1] + y[HD : HD + 1] + y[HD + 1 : HD + 2] + y[HD + 2 : HD + 3]
            att[rows] = ((first_ref[h, :HD] + y[:HD]) * (1.0 / total)).astype(bf16)

        @pl.when(largest != 0.0)
        def _():
            first = first_ref[h]
            spread = []
            peak = exponent_of(first)
            row = 0
            for level in ((mid_a, mid_b), (wide_a, wide_b), (far_a, far_b, far_c, far_d)):
                x, x_peak = combined([whole_form(x[h]) if x.dtype == bf16 else x[h] for x in level])
                count = max(x.shape[1], 128)
                split = wider(split_rows(x[:HD], x[LSUM : LSUM + 1], x_peak), count)
                y = dot(split, take[row : row + count])
                row += count
                total = y[128:129] + y[129:130] + y[130:131]
                y_peak = jnp.where(total > 0.0, y[131:132] + y[132:133] + y[133:134], FILL)
                spread.append((y, total, y_peak))
                peak = jnp.maximum(peak, y_peak)
            scale = jnp.exp2(exponent_of(first) - peak)
            acc = first[:HD] * scale
            total = first[LSUM : LSUM + 1] * scale
            for y, y_total, y_peak in spread:
                scale = jnp.exp2(y_peak - peak)
                acc = acc + y[:HD] * scale
                total = total + y_total * scale
            att[rows] = (acc / total).astype(bf16)

        if for_other:
            picked = lax.dot_general(
                att[rows], take, (((1,), (1,)), ((), ())), preferred_element_type=f32
            ).astype(bf16)
            out_ref[rows, pl.ds(aligned(step * 256, 256), 256)] = picked[:, :256]

            @pl.when(step == 0)
            def _():
                out_ref[rows, 512:] = picked[:, 256:]

            @pl.when(step > 0)
            def _():
                out_ref[rows, 512:] += picked[:, 256:]
        else:
            out_ref[rows] = att[rows]


def merge(for_other, info, nears, mids, wides, fars):
    place_of = HALF_OTHER if for_other else HALF
    near_block_shape = (HEADS_HERE, ROWS, BLOCK)
    if for_other:
        near_specs = [pl.BlockSpec(near_block_shape, lambda i, info: (0, 0, i))]
    else:
        near_specs = [
            pl.BlockSpec(near_block_shape, lambda i, info: (0, 0, 2)),
            pl.BlockSpec(near_block_shape, lambda i, info: (0, 0, i)),
        ]
    return pl.pallas_call(
        functools.partial(merge_kernel, for_other),
        grid_spec=pltpu.PrefetchScalarGridSpec(
            num_scalar_prefetch=1,
            grid=(2,),
            in_specs=[
                *near_specs,
                *[pl.BlockSpec((HEADS_HERE, ROWS, 256), lambda i, info: (0, 0, 2 * info[place_of] + i))] * 2,
                *[pl.BlockSpec((HEADS_HERE, ROWS, 128), lambda i, info: (0, 0, info[place_of]))] * 2,
                *[whole((HEADS_HERE, ROWS, FAR))] * 4,
            ],
            out_specs=whole((256, 768)) if for_other else pl.BlockSpec((256, BLOCK), lambda i, info: (0, i)),
            scratch_shapes=[
                pltpu.VMEM((256, BLOCK), bf16),
                pltpu.VMEM((HEADS_HERE, ROWS, 128 if for_other else BLOCK), f32),
            ],
        ),
        out_shape=shaped(256, 768 if for_other else 2 * BLOCK),
        compiler_params=params(),
        cost_estimate=cost(2 * 2 * BLOCK * 256, 6 * 2**20),
        name="merge",
    )(info, *nears, *mids, *wides, *fars)


def project_kernel(info_ref, own_ref, early_ref, late_ref, w_own, w_other, out_ref):
    tile = own_ref.shape[1]
    step = pl.program_id(0)
    half = info_ref[HALF]
    parts = [own_ref[...]]
    col = lane_positions(0, tile)
    for h in range(HEADS_HERE):
        rows = slice(h * HD, (h + 1) * HD)
        mid_off, wide_off, far_off = (info_ref[OFFS_OTHER + level * HEADS_HERE + h] for level in range(3))
        in_mid = wide_off % RATES[0] == mid_off
        far_done = jnp.logical_or(far_off % RATES[0] == mid_off, far_off % RATES[1] == wide_off)
        nowhere = -(1 << 20)
        start = step * tile
        take = one_hot(
            (
                (512, RATES[0], mid_off - start),
                (128, RATES[1], jnp.where(in_mid, nowhere, wide_off - start)),
                (128, RATES[2], jnp.where(far_done, nowhere, far_off - half * 2 * BLOCK - start)),
            ),
            tile,
        )
        late = dot(late_ref[rows], take)
        reached = (col % RATES[0] == mid_off) | (col % RATES[1] == wide_off) | (col % RATES[2] == far_off)
        parts.append(jnp.where(reached, late, early_ref[rows].astype(f32)).astype(bf16))
    w = jnp.concatenate([w_own[...], w_other[...]], axis=0)
    out_ref[...] = dot(jnp.concatenate(parts, axis=0).T, w).astype(bf16)


def project(info, own, early, late, w_own, w_other):
    rows, width = own.shape[1], w_own.shape[1]
    tile = 512
    return pl.pallas_call(
        project_kernel,
        grid=(rows // tile,),
        in_specs=[
            SMEM,
            pl.BlockSpec((256, tile), lambda i: (0, i)),
            pl.BlockSpec((256, tile), lambda i: (0, i)),
            whole((256, 768)),
            whole((256, width)),
            whole((256, width)),
        ],
        out_specs=pl.BlockSpec((tile, width), lambda i: (i, 0)),
        out_shape=shaped(rows, width),
        compiler_params=params(),
        cost_estimate=pl.CostEstimate(flops=2 * rows * 512 * width, bytes_accessed=12 * 2**20, transcendentals=0),
        name="project",
    )(info, own, early, late, w_own, w_other)


def place(s):
    return s >> 4, s >> 3 & 1, s >> 1 & 3, s & 1


def index(z, xh, y, core):
    return ((z * 2 + xh) * 4 + y) * 2 + core


def send(x, to):
    pairs = []
    for s in range(64):
        target = to(*place(s))
        if target is not None:
            pairs.append((s, index(*target)))
    return lax.ppermute(x, "seq", pairs)


def other_core(x):
    return send(x, lambda z, xh, y, c: (z, xh, y, 1 - c))


def y_step(x, by):
    return send(x, lambda z, xh, y, c: (z, xh, (y + by) % 4, c))


def later_z(x, by):
    return send(x, lambda z, xh, y, c: (z + by, xh, y, c) if z + by < 4 else None)


def earlier_z(x, by):
    return send(x, lambda z, xh, y, c: (z - by, xh, y, c) if z >= by else None)


def ints(*values):
    return jnp.stack([jnp.asarray(v, jnp.int32) for v in values])


def swap_heads(x):
    return lax.ppermute(x, "head", [(0, 1), (1, 0)])


def scalars(offsets):
    head = lax.axis_index("head")
    z, xh, y, core = place(lax.axis_index("seq"))
    other = 1 - head
    flat = offsets.astype(jnp.int32)

    def offs(group):
        return lax.dynamic_slice_in_dim(flat, group * HEADS_HERE, HEADS_HERE, 1).reshape(-1)

    ys = [y, (y + 3) % 4, (y + 1) % 4, (y + 2) % 4]
    everything, nothing = 1 << 20, -(1 << 20)
    wide_pos = [
        (y * 2 + core) * WIDE,
        jnp.where(xh == 0, everything, nothing),
        *[(p * 2 + c) * WIDE for c in (core, 1 - core) for p in ys],
    ]
    far_pos = [
        ((xh * 4 + y) * 2 + core) * FAR,
        *[jnp.where(z + d < 4, everything, nothing) for d in (1, 2, 3)],
        *[((x * 4 + p) * 2 + c) * FAR for x in (xh, 1 - xh) for c in (core, 1 - core) for p in ys],
    ]
    order = [2 * other, 2 * other + 1, jnp.where(head == 1, 3, -1), 2 * head, jnp.where(head == 1, -1, 1)]
    rest = order + [head, other, core, y % 2] + wide_pos + far_pos
    return jnp.concatenate([offs(head), offs(other), ints(*rest)])


def per_device(queries, keys, values, offsets, out_weight):
    info = scalars(offsets)
    kv_mid, few = select_kv(info, keys, values)
    below = y_step(few, 1)
    above = y_step(few, -1)
    across = y_step(few, 2)
    kv_mid_core = send(kv_mid, lambda z, xh, y, c: (z, xh, y, 1) if c == 0 else None)
    kv_mid_below = send(kv_mid, lambda z, xh, y, c: (z, xh, y + 1, c) if y % 2 == 0 else None)
    q_mid, q_wide, q_far = select_q(info, queries)
    q_wide_in = send(q_wide, lambda z, xh, y, c: (z, 0, y, c) if xh == 1 else None)
    q_far_in = [earlier_z(q_far, d) for d in (1, 2, 3)]
    vt = transposed_values(values, q_mid)

    near_1, early_other = near(0, 3, info, queries, keys, vt, [kv_mid_core, q_wide_in, *q_far_in])
    weight_other = swap_heads(out_weight)
    packed, far_here = pack([few, below, above, across], [near_1])
    far_xh = send(far_here, lambda z, xh, y, c: (z, 1 - xh, y, c))
    far_xh_core = send(far_here, lambda z, xh, y, c: (z, 1 - xh, y, 1 - c))
    packed_core = other_core(packed)
    early = swap_heads(early_other)
    mid_a = mid(True, CORE, info, q_mid, [kv_mid, kv_mid_core], [packed, weight_other])

    wide_places = [(n, b * FEW, WIDE) for n in (0, 1) for b in range(4)]
    wide, wide_out = level("wide", WIDE, WIDE_POS, wide_places, info, [q_wide, q_wide_in], [packed, packed_core, mid_a])
    wide_back = send(wide_out, lambda z, xh, y, c: (z, 1, y, c) if xh == 0 else None)
    far_places = [(n, b * FEW + WIDE, FAR) for n in (0, 1) for b in range(4)] + [(2, 0, 4 * FAR), (3, 0, 4 * FAR)]
    far, *far_out = level(
        "far", FAR, FAR_POS, far_places, info, [q_far, *q_far_in], [packed, packed_core, far_xh, far_xh_core, wide]
    )
    far_back = [later_z(x, d) for d, x in zip((1, 2, 3), far_out)]
    kv_mid_below_core = other_core(kv_mid_below)
    mid_b = mid(False, Y_ODD, info, q_mid, [kv_mid_below, kv_mid_below_core], [early, far])

    parts = ((mid_a, mid_b), (wide, wide_back), (far, *far_back))
    late_rows = merge(True, info, [near_1], *parts)
    late = swap_heads(late_rows)
    (near_2,) = near(3, 2, info, queries, keys, vt, [late_rows])
    attended_own = merge(False, info, [near_1, near_2], *parts)
    return project(info, attended_own, early, late, out_weight, weight_other)


def solution(mesh):
    return jax.shard_map(
        per_device,
        mesh=mesh,
        in_specs=(P("seq", "head"), P("seq", "head"), P("seq", "head"), P(), P("head", None)),
        out_specs=P(("seq", "head"), None),
        check_vma=False,
    )
```

```python
import functools
import math

import jax
import jax.numpy as jnp
from jax import lax
from jax.experimental import pallas as pl
from jax.experimental.pallas import tpu as pltpu
from jax.sharding import PartitionSpec as P

HD = 128
HEADS_HERE = 2
RATES = (4, 16, 64)
BLOCK = 1024
TILE = 256
ROWS = 144
LSUM = 128
MROW = 129
LOG2_SCALE = math.log2(math.e) / math.sqrt(HD)
FILL = -1e30
SMALL, LARGE = 2.0**-60, 2.0**100
VMEM_BYTES = 56 * 2**20
MID, WIDE, FAR = 1024, 256, 64
FEW = WIDE + FAR
LATE = MID // 2 + WIDE // 2 + 2 * FAR
OFFS, OFFS_OTHER, ORDER, HALF, HALF_OTHER, CORE, Y_ODD, WIDE_POS, FAR_POS = 0, 6, 12, 17, 18, 19, 20, 21, 31

f32, bf16 = jnp.float32, jnp.bfloat16


def dot(a, b):
    return jnp.dot(a, b, preferred_element_type=f32)


def aligned(x, n):
    return x if isinstance(x, int) else pl.multiple_of(x, n)


def transposed_queries(q):
    q = q.astype(f32) * LOG2_SCALE
    high = q.astype(bf16)
    low = (q - high.astype(f32)).astype(bf16)
    return jnp.concatenate([high, low], axis=1).T


def scores(k, qt):
    return dot(jnp.concatenate([k, k], axis=1), qt)


def with_ones(v):
    return jnp.concatenate([v.T, jnp.ones((ROWS - HD, v.shape[0]), v.dtype)], axis=0)


def pieces(x):
    first = x.astype(bf16).astype(f32)
    second = (x - first).astype(bf16).astype(f32)
    return first, second, x - first - second


def stat_rows(total, exponent, count):
    row = lax.broadcasted_iota(jnp.int32, (ROWS - HD, count), 0)
    parts = (total,) + (pieces(exponent) if exponent is not None else ())
    out = jnp.zeros((ROWS - HD, count), f32)
    for n, part in enumerate(parts):
        out = jnp.where(row == n, part, out)
    return out


def within_range(total, counted=None):
    ok = (total >= SMALL) & (total <= LARGE)
    if counted is not None:
        ok = ok | ~counted
    return jnp.min(jnp.where(ok, 1.0, 0.0)) > 0.5


def rescaled(store, get_queries, count, blocks, block):
    def step(j, carry):
        peak, acc = carry
        k, vt, allowed = block(j)
        s = jnp.where(allowed, scores(k, get_queries()), FILL)
        new = jnp.maximum(peak, jnp.max(s, axis=0, keepdims=True))
        p = jnp.where(allowed, jnp.exp2(s - new), 0.0)
        return new, acc * jnp.exp2(peak - new) + dot(vt, p.astype(bf16))

    peak, acc = lax.fori_loop(
        0, blocks, step, (jnp.full((1, count), FILL, f32), jnp.zeros((ROWS, count), f32))
    )
    store(acc, acc[LSUM : LSUM + 1], peak)


def position_mask(key_first, query_pos, rows):
    key_pos = key_first + lax.broadcasted_iota(jnp.int32, (rows, query_pos.shape[1]), 0)
    return key_pos <= query_pos


def lane_positions(first, count):
    return first + lax.broadcasted_iota(jnp.int32, (1, count), 1)


def pick(x_ref, cols, scr, off_ref, outs):
    scr[...] = x_ref[:, cols].astype(f32)
    step = pl.program_id(0)
    for level, (out_ref, row, out_cols) in enumerate(outs):
        count = scr.shape[0] // RATES[level]
        picked = scr[pl.ds(off_ref[OFFS + level * HEADS_HERE + scr_head(cols)], count, stride=RATES[level]), :]
        first = pl.multiple_of(row + step * count, 16)
        out_ref[pl.ds(first, count), out_cols] = picked.astype(bf16)


def scr_head(cols):
    return cols.start // HD


def select_kv_kernel(info_ref, k_ref, v_ref, mid_ref, few_ref, scr):
    for h in range(HEADS_HERE):
        cols = slice(h * HD, (h + 1) * HD)
        for n, x_ref in enumerate((k_ref, v_ref)):
            out_cols = slice((2 * n + h) * HD, (2 * n + h + 1) * HD)
            pick(x_ref, cols, scr.at[n, h], info_ref, ((mid_ref, 0, out_cols), (few_ref, 0, out_cols), (few_ref, WIDE, out_cols)))


def select_q_kernel(info_ref, q_ref, qm_ref, qw_ref, qf_ref, scr):
    for h in range(HEADS_HERE):
        cols = slice(h * HD, (h + 1) * HD)
        pick(q_ref, cols, scr.at[h], info_ref, ((qm_ref, 0, cols), (qw_ref, 0, cols), (qf_ref, 0, cols)))


def vmem(count):
    return [pl.BlockSpec(memory_space=pltpu.VMEM)] * count


SMEM = pl.BlockSpec(memory_space=pltpu.SMEM)
ANY = pl.BlockSpec(memory_space=pl.ANY)


def whole(shape):
    return pl.BlockSpec(shape, lambda *_: (0,) * len(shape))


def params():
    return pltpu.CompilerParams(vmem_limit_bytes=VMEM_BYTES)


def cost(pairs, bytes_accessed):
    return pl.CostEstimate(
        flops=int(pairs * 1024 * 1.5), bytes_accessed=int(bytes_accessed), transcendentals=int(pairs)
    )


def shaped(*shape, dtype=bf16):
    return jax.ShapeDtypeStruct(shape, dtype)


def select_kv(info, k, v):
    chunk = pl.BlockSpec((BLOCK, 256), lambda i: (i, 0))
    return pl.pallas_call(
        select_kv_kernel,
        grid=(k.shape[0] // BLOCK,),
        in_specs=[SMEM, chunk, chunk],
        out_specs=[whole((MID, 512)), whole((FEW, 512))],
        out_shape=[shaped(MID, 512), shaped(FEW, 512)],
        scratch_shapes=[pltpu.VMEM((2, HEADS_HERE, BLOCK, HD), f32)],
        compiler_params=params(),
        name="select_kv",
    )(info, k, v)


def select_q(info, q):
    return pl.pallas_call(
        select_q_kernel,
        grid=(q.shape[0] // BLOCK,),
        in_specs=[SMEM, pl.BlockSpec((BLOCK, 256), lambda i: (i, 0))],
        out_specs=[whole((MID, 256)), whole((WIDE, 256)), whole((FAR, 256))],
        out_shape=[shaped(MID, 256), shaped(WIDE, 256), shaped(FAR, 256)],
        scratch_shapes=[pltpu.VMEM((HEADS_HERE, BLOCK, HD), f32)],
        compiler_params=params(),
        name="select_q",
    )(info, q)


def pack_kernel(count, *refs):
    *_, all_ref, far_ref = refs
    for n, x_ref in enumerate(refs[:count]):
        all_ref[n * FEW : (n + 1) * FEW] = x_ref[...]
        far_ref[n * FAR : (n + 1) * FAR] = x_ref[WIDE:]


def pack(few, after):
    count = len(few)
    return pl.pallas_call(
        functools.partial(pack_kernel, count),
        in_specs=vmem(count) + [ANY] * len(after),
        out_specs=vmem(2),
        out_shape=[shaped(count * FEW, 512), shaped(count * FAR, 512)],
        compiler_params=params(),
        cost_estimate=pl.CostEstimate(flops=0, bytes_accessed=4 * 2**20, transcendentals=0),
        name="pack",
    )(*few, *after)


def diagonal(out_ref, h, k, vt, qt_ref):
    row = lax.broadcasted_iota(jnp.int32, (TILE, TILE), 0)
    col = lax.broadcasted_iota(jnp.int32, (TILE, TILE), 1)
    rows = []
    for g in range(BLOCK // TILE):
        first = g * TILE
        p = jnp.exp2(scores(k[first : first + TILE], qt_ref[h, :, first:]))
        parts = [jnp.where(row <= col, p[:, :TILE], 0.0), p[:, TILE:]]
        if g:
            parts = [jnp.zeros((TILE, first), f32)] + parts
        rows.append(jnp.concatenate([x for x in parts if x.shape[1]], axis=1).astype(bf16))
    out_ref[h] += dot(vt, jnp.concatenate(rows, axis=0))


def store_partial(out_ref, h, acc, total, exponent):
    count = acc.shape[1]
    out_ref[h, :HD] = acc[:HD]
    out_ref[h, HD:] = stat_rows(total, exponent, count)


def near_kernel(first, skipped, info_ref, q_ref, k_ref, v_ref, *refs):
    refs = refs[skipped:]
    block = info_ref[ORDER + first + pl.program_id(0)]

    @pl.when(block >= 0)
    def _():
        near_block(first, block, q_ref, k_ref, v_ref, *refs)


def near_block(first, block, q_ref, k_ref, v_ref, *refs):
    out_ref, *early_ref, qt = refs

    def values_at(start, rows, h):
        return with_ones(v_ref[pl.ds(start, rows), h * HD : (h + 1) * HD])

    for h in range(HEADS_HERE):
        qt[h] = transposed_queries(q_ref[:, h * HD : (h + 1) * HD])
    out_ref[...] = jnp.zeros(out_ref.shape, f32)

    def full(j, carry):
        start = aligned(j * BLOCK, BLOCK)
        for h in range(HEADS_HERE):
            s = scores(k_ref[pl.ds(start, BLOCK), h * HD : (h + 1) * HD], qt[h])
            out_ref[h] += dot(values_at(start, BLOCK, h), jnp.exp2(s).astype(bf16))
        return carry

    lax.fori_loop(0, block, full, 0)
    start = aligned(block * BLOCK, BLOCK)
    for h in range(HEADS_HERE):
        cols = slice(h * HD, (h + 1) * HD)
        diagonal(out_ref, h, k_ref[pl.ds(start, BLOCK), cols], values_at(start, BLOCK, h), qt)
    total = jnp.concatenate([out_ref[h, LSUM : LSUM + 1] for h in range(HEADS_HERE)], axis=0)
    ok = within_range(total)
    for h in range(HEADS_HERE):
        out_ref[h, HD:] = stat_rows(total[h : h + 1], None, BLOCK)

    @pl.when(jnp.logical_not(ok))
    def _():
        for h in range(HEADS_HERE):
            cols = slice(h * HD, (h + 1) * HD)
            query_pos = lane_positions(block * BLOCK, BLOCK)

            def key_block(j):
                first = aligned(j * TILE, TILE)
                return (
                    k_ref[pl.ds(first, TILE), cols],
                    values_at(first, TILE, h),
                    position_mask(first, query_pos, TILE),
                )

            rescaled(
                functools.partial(store_partial, out_ref, h),
                lambda: qt[h],
                BLOCK,
                (block + 1) * (BLOCK // TILE),
                key_block,
            )

    if early_ref:

        @pl.when(pl.program_id(0) < 2)
        def _():
            for h in range(HEADS_HERE):
                scale = 1.0 / out_ref[h, LSUM : LSUM + 1]
                early_ref[0][h * HD : (h + 1) * HD] = (out_ref[h, :HD] * scale).astype(bf16)


def near(first, steps, info, q, k, v, after):
    tok = q.shape[0]
    early = first == 0
    return pl.pallas_call(
        functools.partial(near_kernel, first, len(after)),
        grid_spec=pltpu.PrefetchScalarGridSpec(
            num_scalar_prefetch=1,
            grid=(steps,),
            in_specs=[
                pl.BlockSpec((BLOCK, 256), lambda i, info: (jnp.maximum(info[ORDER + first + i], 0), 0)),
                whole((tok, 256)),
                whole((tok, 256)),
            ]
            + [ANY] * len(after),
            out_specs=[pl.BlockSpec((HEADS_HERE, ROWS, BLOCK), lambda i, info: (0, 0, i))]
            + [pl.BlockSpec((256, BLOCK), lambda i, info: (0, jnp.minimum(i, 1)))] * early,
            scratch_shapes=[pltpu.VMEM((HEADS_HERE, 256, BLOCK), bf16)],
        ),
        out_shape=[shaped(HEADS_HERE, ROWS, steps * BLOCK, dtype=f32)] + [shaped(256, tok // 2)] * early,
        compiler_params=params(),
        cost_estimate=cost(steps * BLOCK * 2300 * 2, 10 * 2**20),
        name="near",
    )(info, q, k, v, *after)


def mid_kernel(causal, flag_at, info_ref, q_ref, *refs):
    kv_refs, out_ref, (qt, vt) = refs[:2], refs[-4], refs[-2:]
    others = info_ref[flag_at] == 1
    for h in range(HEADS_HERE):
        qt[h] = transposed_queries(q_ref[:, h * HD : (h + 1) * HD])
    out_ref[...] = jnp.zeros(out_ref.shape, f32)

    def keys(n, h):
        return kv_refs[n].at[:, h * HD : (h + 1) * HD]

    def values(n):
        for h in range(HEADS_HERE):
            vt[n, h] = with_ones(kv_refs[n][:, (2 + h) * HD : (3 + h) * HD])

    if causal:
        values(0)
        for h in range(HEADS_HERE):
            diagonal(out_ref, h, keys(0, h)[...], vt[0, h], qt)

    @pl.when(others)
    def _():
        for n in range(1 if causal else 0, len(kv_refs)):
            values(n)
            for h in range(HEADS_HERE):
                p = jnp.exp2(scores(keys(n, h)[...], qt[h])).astype(bf16)
                out_ref[h] += dot(vt[n, h], p)

    total = jnp.concatenate([out_ref[h, LSUM : LSUM + 1] for h in range(HEADS_HERE)], axis=0)
    ok = within_range(total)
    for h in range(HEADS_HERE):
        out_ref[h, HD:] = stat_rows(total[h : h + 1], None, BLOCK)

    @pl.when(jnp.logical_and(jnp.logical_not(ok), True if causal else others))
    def _():
        for h in range(HEADS_HERE):
            query_pos = lane_positions(0, BLOCK)
            peak = jnp.full((1, BLOCK), FILL, f32)
            acc = jnp.zeros((ROWS, BLOCK), f32)
            for n in range(len(kv_refs)):
                own = causal and n == 0
                key_first = 0 if own else jnp.where(others, -BLOCK, BLOCK)

                def step(j, carry):
                    peak, acc = carry
                    first = aligned(j * TILE, TILE)
                    allowed = position_mask(key_first + first, query_pos, TILE)
                    s = jnp.where(allowed, scores(keys(n, h)[pl.ds(first, TILE), :], qt[h]), FILL)
                    new = jnp.maximum(peak, jnp.max(s, axis=0, keepdims=True))
                    p = jnp.where(allowed, jnp.exp2(s - new), 0.0)
                    vt_tile = with_ones(kv_refs[n][pl.ds(first, TILE), (2 + h) * HD : (3 + h) * HD])
                    return new, acc * jnp.exp2(peak - new) + dot(vt_tile, p.astype(bf16))

                peak, acc = lax.fori_loop(0, BLOCK // TILE, step, (peak, acc))
            store_partial(out_ref, h, acc, acc[LSUM : LSUM + 1], peak)


def mid(causal, flag_at, info, q, kvs, through, after):
    before = 2 + len(kvs)
    return pl.pallas_call(
        functools.partial(mid_kernel, causal, flag_at),
        grid=(1,),
        in_specs=[SMEM, whole((MID, 256))] + [whole((MID, 512))] * len(kvs) + [ANY] * (len(through) + len(after)),
        out_specs=[whole((HEADS_HERE, ROWS, BLOCK))] + [ANY] * len(through),
        out_shape=[shaped(HEADS_HERE, ROWS, BLOCK, dtype=f32)] + [shaped(*x.shape) for x in through],
        input_output_aliases={before + n: 1 + n for n in range(len(through))},
        scratch_shapes=[
            pltpu.VMEM((HEADS_HERE, 256, BLOCK), bf16),
            pltpu.VMEM((len(kvs), HEADS_HERE, ROWS, BLOCK), bf16),
        ],
        compiler_params=params(),
        cost_estimate=cost(2 * BLOCK * BLOCK * 1.8, 5 * 2**20),
        name="mid",
    )(info, q, *kvs, *through, *after)


def pool_level(rows, pos_at, info_ref, q_refs, kv, qt, vt, out_refs):
    q_count = len(q_refs)
    block_rows = q_refs[0].shape[0]
    count = q_count * block_rows
    total_keys = kv.shape[0]
    chunk = min(total_keys, 1024)
    query_pos = jnp.concatenate([lane_positions(info_ref[pos_at + n], block_rows) for n in range(q_count)], axis=1)
    counted = query_pos >= 0
    key_iota = lax.broadcasted_iota(jnp.int32, (rows, 1), 0)
    key_pos = jnp.concatenate(
        [info_ref[pos_at + q_count + n] + key_iota for n in range(total_keys // rows)], axis=0
    )
    for h in range(HEADS_HERE):
        q = jnp.concatenate([q_ref[:, h * HD : (h + 1) * HD] for q_ref in q_refs], axis=0)
        qt[h] = transposed_queries(q)
        vt[h] = with_ones(kv[:, (2 + h) * HD : (3 + h) * HD])

    def store(h, acc, total, peak):
        for n in range(q_count):
            cols = slice(n * block_rows, (n + 1) * block_rows)
            peak_here = None if peak is None else peak[:, cols]
            if n == 0:
                store_partial(out_refs[n], h, acc[:, cols], total[:, cols], peak_here)
            else:
                out_refs[n][h] = split_rows(acc[:HD, cols], total[:, cols], peak_here)

    def keys(h, first, size):
        return kv[first : first + size, h * HD : (h + 1) * HD]

    totals = []
    for h in range(HEADS_HERE):
        acc = jnp.zeros((ROWS, count), f32)
        for first in range(0, total_keys, chunk):
            s = scores(keys(h, first, chunk), qt[h])
            allowed = key_pos[first : first + chunk] <= query_pos
            p = jnp.where(allowed, jnp.exp2(s), 0.0).astype(bf16)
            acc = acc + dot(vt[h, :, first : first + chunk], p)
        total = acc[LSUM : LSUM + 1]
        totals.append(jnp.where(counted, total, 1.0))
        store(h, acc, total, None)

    @pl.when(jnp.logical_not(within_range(jnp.concatenate(totals, axis=0))))
    def _():
        for h in range(HEADS_HERE):
            peak = jnp.full((1, count), FILL, f32)
            acc = jnp.zeros((ROWS, count), f32)
            for first in range(0, total_keys, TILE):
                allowed = key_pos[first : first + TILE] <= query_pos
                s = jnp.where(allowed, scores(keys(h, first, TILE), qt[h]), FILL)
                new = jnp.maximum(peak, jnp.max(s, axis=0, keepdims=True))
                p = jnp.where(allowed, jnp.exp2(s - new), 0.0).astype(bf16)
                acc = acc * jnp.exp2(peak - new) + dot(vt[h, :, first : first + TILE], p)
                peak = new
            store(h, acc, acc[LSUM : LSUM + 1], peak)


def level_kernel(rows, pos_at, places, q_count, source_count, info_ref, *refs):
    *refs, kv, qt, vt, sems = refs
    q_refs, sources, refs = refs[:q_count], refs[q_count : q_count + source_count], refs[q_count + source_count :]
    through = (len(refs) - q_count) // 2
    out_refs = refs[through : through + q_count]
    copies = []
    place = 0
    for n, (source, row, count) in enumerate(places):
        dst = kv.at[place : place + count]
        copies.append(pltpu.make_async_copy(sources[source].at[row : row + count], dst, sems.at[n]))
        place += count
    for copy in copies:
        copy.start()
    for copy in copies:
        copy.wait()
    pool_level(rows, pos_at, info_ref, q_refs, kv, qt, vt, out_refs)


def level(name, rows, pos_at, places, info, qs, sources, through=()):
    keys = sum(count for _, _, count in places)
    count = len(qs) * rows
    return pl.pallas_call(
        functools.partial(level_kernel, rows, pos_at, tuple(places), len(qs), len(sources)),
        in_specs=[SMEM] + vmem(len(qs)) + [ANY] * (len(sources) + len(through)),
        out_specs=vmem(len(qs)) + [ANY] * len(through),
        out_shape=[shaped(HEADS_HERE, ROWS, rows, dtype=bf16 if n else f32) for n in range(len(qs))]
        + [shaped(*x.shape) for x in through],
        input_output_aliases={1 + len(qs) + len(sources) + n: len(qs) + n for n in range(len(through))},
        scratch_shapes=[
            pltpu.VMEM((keys, 512), bf16),
            pltpu.VMEM((HEADS_HERE, 256, count), bf16),
            pltpu.VMEM((HEADS_HERE, ROWS, keys), bf16),
            pltpu.SemaphoreType.DMA((len(places),)),
        ],
        compiler_params=params(),
        cost_estimate=cost(2 * count * keys, 4 * 2**20),
        name=name,
    )(info, *qs, *sources, *through)


def exponent_of(x):
    m = x[MROW : MROW + 1] + x[MROW + 1 : MROW + 2] + x[MROW + 2 : MROW + 3]
    return jnp.where(x[LSUM : LSUM + 1] > 0.0, m, FILL)


def combined(parts):
    peaks = [exponent_of(x) for x in parts]
    peak = functools.reduce(jnp.maximum, peaks)
    out = sum(x[: LSUM + 1] * jnp.exp2(m - peak) for x, m in zip(parts, peaks))
    return out, peak


def split_rows(sums, total, peak):
    rows = pieces(total) + (pieces(peak) if peak is not None else ())
    row = lax.broadcasted_iota(jnp.int32, (ROWS - HD, total.shape[1]), 0)
    stats = jnp.zeros((ROWS - HD, total.shape[1]), f32)
    for n, r in enumerate(rows):
        stats = jnp.where(row == n, r, stats)
    return jnp.concatenate([sums, stats], axis=0).astype(bf16)


def wider(x, count):
    return x if x.shape[1] == count else jnp.concatenate([x, jnp.zeros((x.shape[0], count - x.shape[1]), x.dtype)], axis=1)


def one_hot(targets, count):
    parts = []
    for rows, rate, first, *offset in targets:
        width = count if first is not None else TILE
        at = lax.broadcasted_iota(jnp.int32, (1, width), 1) - (offset[0] if first is None else first)
        row_of = jnp.where(at & (rate - 1) == 0, at >> (rate.bit_length() - 1), -1)
        here = rows if first is not None else TILE // rate
        row = lax.broadcasted_iota(jnp.int32, (here, width), 0)
        part = jnp.where(row == row_of, 1.0, 0.0).astype(bf16)
        if first is None:
            groups = []
            for g in range(count // TILE):
                above, below = g * here, rows - (g + 1) * here
                column = [jnp.zeros((above, TILE), bf16)] * (above > 0) + [part] + [jnp.zeros((below, TILE), bf16)] * (below > 0)
                groups.append(jnp.concatenate(column, axis=0))
            part = jnp.concatenate(groups, axis=1)
        parts.append(part)
    return jnp.concatenate(parts, axis=0)


def whole_form(x):
    x = x.astype(f32)
    total = x[LSUM : LSUM + 1] + x[LSUM + 1 : LSUM + 2] + x[LSUM + 2 : LSUM + 3]
    return jnp.concatenate([x[:HD], total, x[LSUM + 3 : LSUM + 6], x[LSUM + 6 :], x[LSUM + 6 : LSUM + 8]], axis=0)


def largest_exponent(parts, places):
    seen = []
    for x, place in zip(parts, places):
        for h in range(HEADS_HERE):
            row = jnp.abs(x[h, place : place + 1].astype(f32))
            width = min(row.shape[1], 128)
            for first in range(0, row.shape[1], width):
                seen.append(wider(row[:, first : first + width], 128))
    return jnp.max(functools.reduce(jnp.maximum, seen))


def merge_kernel(for_other, info_ref, near_ref, *refs):
    near_2, *refs = (None, *refs) if for_other else refs
    mid_a, mid_b, wide_a, wide_b, far_a, far_b, far_c, far_d, out_ref, first_ref = refs
    step = pl.program_id(0)
    half = info_ref[HALF_OTHER if for_other else HALF]
    start = (2 * half + step) * BLOCK
    if for_other:
        first_ref = near_ref
    else:
        in_first = jnp.logical_and(half == 1, step == 1)

        @pl.when(in_first)
        def _():
            first_ref[...] = near_ref[...]

        @pl.when(jnp.logical_not(in_first))
        def _():
            first_ref[...] = near_2[...]

    local, sent = [first_ref, mid_a, mid_b, wide_a, far_a], [wide_b, far_b, far_c, far_d]
    largest = largest_exponent(local + sent, [MROW] * len(local) + [LSUM + 3] * len(sent))

    def take_of(h):
        offs = [info_ref[OFFS + level * HEADS_HERE + h] for level in range(3)]
        return one_hot(
            (
                (256, RATES[0], None, offs[0]),
                (128, RATES[1], offs[1] + half * 2 * BLOCK - start),
                (128, RATES[2], offs[2] - start),
            ),
            BLOCK,
        )

    def finish(h, take, rows):
        where = slice(h * HD, (h + 1) * HD)
        if not for_other:
            out_ref[where] = rows
            return
        picked = lax.dot_general(rows, take, (((1,), (1,)), ((), ())), preferred_element_type=f32).astype(bf16)
        out_ref[where, pl.ds(aligned(step * 256, 256), 256)] = picked[:, :256]
        out_ref[where, 512:] = jnp.where(step == 0, picked[:, 256:], out_ref[where, 512:] + picked[:, 256:])

    @pl.when(largest == 0.0)
    def _():
        for h in range(HEADS_HERE):
            take = take_of(h)
            far = far_a[h] + whole_form(far_b[h]) + whole_form(far_c[h]) + whole_form(far_d[h])
            groups = [mid_a[h] + mid_b[h], wide_a[h] + whole_form(wide_b[h]), wider(far, 128)]
            x = jnp.concatenate([split_rows(g[:HD], g[LSUM : LSUM + 1], None) for g in groups], axis=1)
            y = dot(x, take)
            total = first_ref[h, LSUM : LSUM + 1] + y[HD : HD + 1] + y[HD + 1 : HD + 2] + y[HD + 2 : HD + 3]
            finish(h, take, ((first_ref[h, :HD] + y[:HD]) * (1.0 / total)).astype(bf16))

    @pl.when(largest != 0.0)
    def _():
        for h in range(HEADS_HERE):
            take = take_of(h)
            first = first_ref[h]
            spread = []
            peak = exponent_of(first)
            row = 0
            for level in ((mid_a, mid_b), (wide_a, wide_b), (far_a, far_b, far_c, far_d)):
                x, x_peak = combined([whole_form(x[h]) if x.dtype == bf16 else x[h] for x in level])
                count = max(x.shape[1], 128)
                split = wider(split_rows(x[:HD], x[LSUM : LSUM + 1], x_peak), count)
                y = dot(split, take[row : row + count])
                row += count
                total = y[128:129] + y[129:130] + y[130:131]
                y_peak = jnp.where(total > 0.0, y[131:132] + y[132:133] + y[133:134], FILL)
                spread.append((y, total, y_peak))
                peak = jnp.maximum(peak, y_peak)
            scale = jnp.exp2(exponent_of(first) - peak)
            acc = first[:HD] * scale
            total = first[LSUM : LSUM + 1] * scale
            for y, y_total, y_peak in spread:
                scale = jnp.exp2(y_peak - peak)
                acc = acc + y[:HD] * scale
                total = total + y_total * scale
            finish(h, take, (acc / total).astype(bf16))


def merge(for_other, info, nears, mids, wides, fars):
    place_of = HALF_OTHER if for_other else HALF
    near_block_shape = (HEADS_HERE, ROWS, BLOCK)
    if for_other:
        near_specs = [pl.BlockSpec(near_block_shape, lambda i, info: (0, 0, i))]
    else:
        near_specs = [
            pl.BlockSpec(near_block_shape, lambda i, info: (0, 0, 2)),
            pl.BlockSpec(near_block_shape, lambda i, info: (0, 0, i)),
        ]
    return pl.pallas_call(
        functools.partial(merge_kernel, for_other),
        grid_spec=pltpu.PrefetchScalarGridSpec(
            num_scalar_prefetch=1,
            grid=(2,),
            in_specs=[
                *near_specs,
                *[pl.BlockSpec((HEADS_HERE, ROWS, 256), lambda i, info: (0, 0, 2 * info[place_of] + i))] * 2,
                *[pl.BlockSpec((HEADS_HERE, ROWS, 128), lambda i, info: (0, 0, info[place_of]))] * 2,
                *[whole((HEADS_HERE, ROWS, FAR))] * 4,
            ],
            out_specs=whole((256, LATE)) if for_other else pl.BlockSpec((256, BLOCK), lambda i, info: (0, i)),
            scratch_shapes=[
                pltpu.VMEM((HEADS_HERE, ROWS, 128 if for_other else BLOCK), f32),
            ],
        ),
        out_shape=shaped(256, LATE if for_other else 2 * BLOCK),
        compiler_params=params(),
        cost_estimate=cost(2 * 2 * BLOCK * 256, 6 * 2**20),
        name="merge",
    )(info, *nears, *mids, *wides, *fars)


def project_kernel(info_ref, own_ref, early_ref, late_ref, w_own, w_other, out_ref):
    tile = own_ref.shape[1]
    step = pl.program_id(0)
    half = info_ref[HALF]
    parts = [own_ref[...]]
    col = lane_positions(0, tile)
    for h in range(HEADS_HERE):
        rows = slice(h * HD, (h + 1) * HD)
        mid_off, wide_off, far_off = (info_ref[OFFS_OTHER + level * HEADS_HERE + h] for level in range(3))
        in_mid = wide_off % RATES[0] == mid_off
        far_done = jnp.logical_or(far_off % RATES[0] == mid_off, far_off % RATES[1] == wide_off)
        nowhere = -(1 << 20)
        start = step * tile
        take = one_hot(
            (
                (tile // RATES[0], RATES[0], None, mid_off),
                (128, RATES[1], jnp.where(in_mid, nowhere, wide_off - start)),
                (128, RATES[2], jnp.where(far_done, nowhere, far_off - half * 2 * BLOCK - start)),
            ),
            tile,
        )
        near_rows = late_ref[rows, pl.ds(aligned(step * (tile // RATES[0]), tile // RATES[0]), tile // RATES[0])]
        late = dot(jnp.concatenate([near_rows, late_ref[rows, 512:]], axis=1), take)
        reached = (col % RATES[0] == mid_off) | (col % RATES[1] == wide_off) | (col % RATES[2] == far_off)
        parts.append(jnp.where(reached, late, early_ref[rows].astype(f32)).astype(bf16))
    w = jnp.concatenate([w_own[...], w_other[...]], axis=0)
    out_ref[...] = dot(jnp.concatenate(parts, axis=0).T, w).astype(bf16)


def project(info, own, early, late, w_own, w_other):
    rows, width = own.shape[1], w_own.shape[1]
    tile = 512
    return pl.pallas_call(
        project_kernel,
        grid=(rows // tile,),
        in_specs=[
            SMEM,
            pl.BlockSpec((256, tile), lambda i: (0, i)),
            pl.BlockSpec((256, tile), lambda i: (0, i)),
            whole((256, LATE)),
            whole((256, width)),
            whole((256, width)),
        ],
        out_specs=pl.BlockSpec((tile, width), lambda i: (i, 0)),
        out_shape=shaped(rows, width),
        compiler_params=params(),
        cost_estimate=pl.CostEstimate(flops=2 * rows * 512 * width, bytes_accessed=12 * 2**20, transcendentals=0),
        name="project",
    )(info, own, early, late, w_own, w_other)


def place(s):
    return s >> 4, s >> 3 & 1, s >> 1 & 3, s & 1


def index(z, xh, y, core):
    return ((z * 2 + xh) * 4 + y) * 2 + core


def send(x, to):
    pairs = []
    for s in range(64):
        target = to(*place(s))
        if target is not None:
            pairs.append((s, index(*target)))
    return lax.ppermute(x, "seq", pairs)


def other_core(x):
    return send(x, lambda z, xh, y, c: (z, xh, y, 1 - c))


def y_step(x, by):
    return send(x, lambda z, xh, y, c: (z, xh, (y + by) % 4, c))


def later_z(x, by):
    return send(x, lambda z, xh, y, c: (z + by, xh, y, c) if z + by < 4 else None)


def earlier_z(x, by):
    return send(x, lambda z, xh, y, c: (z - by, xh, y, c) if z >= by else None)


def ints(*values):
    return jnp.stack([jnp.asarray(v, jnp.int32) for v in values])


def swap_heads(x):
    return lax.ppermute(x, "head", [(0, 1), (1, 0)])


def scalars(offsets):
    head = lax.axis_index("head")
    z, xh, y, core = place(lax.axis_index("seq"))
    other = 1 - head
    flat = offsets.astype(jnp.int32)

    def offs(group):
        return lax.dynamic_slice_in_dim(flat, group * HEADS_HERE, HEADS_HERE, 1).reshape(-1)

    ys = [y, (y + 3) % 4, (y + 1) % 4, (y + 2) % 4]
    everything, nothing = 1 << 20, -(1 << 20)
    wide_pos = [
        (y * 2 + core) * WIDE,
        jnp.where(xh == 0, everything, nothing),
        *[(p * 2 + c) * WIDE for c in (core, 1 - core) for p in ys],
    ]
    far_pos = [
        ((xh * 4 + y) * 2 + core) * FAR,
        *[jnp.where(z + d < 4, everything, nothing) for d in (1, 2, 3)],
        *[((x * 4 + p) * 2 + c) * FAR for x in (xh, 1 - xh) for c in (core, 1 - core) for p in ys],
    ]
    order = [2 * other, 2 * other + 1, jnp.where(head == 1, 3, -1), 2 * head, jnp.where(head == 1, -1, 1)]
    rest = order + [head, other, core, y % 2] + wide_pos + far_pos
    return jnp.concatenate([offs(head), offs(other), ints(*rest)])


def per_device(queries, keys, values, offsets, out_weight):
    info = scalars(offsets)
    kv_mid, few = select_kv(info, keys, values)
    below = y_step(few, 1)
    above = y_step(few, -1)
    across = y_step(few, 2)
    kv_mid_core = send(kv_mid, lambda z, xh, y, c: (z, xh, y, 1) if c == 0 else None)
    kv_mid_below = send(kv_mid, lambda z, xh, y, c: (z, xh, y + 1, c) if y % 2 == 0 else None)
    q_mid, q_wide, q_far = select_q(info, queries)
    q_wide_in = send(q_wide, lambda z, xh, y, c: (z, 0, y, c) if xh == 1 else None)
    q_far_in = [earlier_z(q_far, d) for d in (1, 2, 3)]

    near_1, early_other = near(0, 3, info, queries, keys, values, [kv_mid_core, q_wide_in, *q_far_in])
    weight_other = swap_heads(out_weight)
    packed, far_here = pack([few, below, above, across], [near_1])
    far_xh = send(far_here, lambda z, xh, y, c: (z, 1 - xh, y, c))
    far_xh_core = other_core(far_xh)
    packed_core = other_core(packed)
    mid_a, kv_mid_below = mid(
        True, CORE, info, q_mid, [kv_mid, kv_mid_core], [kv_mid_below], [packed, weight_other]
    )
    kv_mid_below_core = other_core(kv_mid_below)

    wide_places = [(n, b * FEW, WIDE) for n in (0, 1) for b in range(4)]
    wide, wide_out = level("wide", WIDE, WIDE_POS, wide_places, info, [q_wide, q_wide_in], [packed, packed_core, mid_a])
    wide_back = send(wide_out, lambda z, xh, y, c: (z, 1, y, c) if xh == 0 else None)
    mid_b, early_other = mid(False, Y_ODD, info, q_mid, [kv_mid_below, kv_mid_below_core], [early_other], [wide])
    early = swap_heads(early_other)
    far_places = [(n, b * FEW + WIDE, FAR) for n in (0, 1) for b in range(4)] + [(2, 0, 4 * FAR), (3, 0, 4 * FAR)]
    far, *far_out = level(
        "far", FAR, FAR_POS, far_places, info, [q_far, *q_far_in], [packed, packed_core, far_xh, far_xh_core, mid_b]
    )
    far_back = [later_z(x, d) for d, x in zip((1, 2, 3), far_out)]

    parts = ((mid_a, mid_b), (wide, wide_back), (far, *far_back))
    late_rows = merge(True, info, [near_1], *parts)
    late = swap_heads(late_rows)
    (near_2,) = near(3, 2, info, queries, keys, values, [late_rows])
    attended_own = merge(False, info, [near_1, near_2], *parts)
    return project(info, attended_own, early, late, out_weight, weight_other)


def solution(mesh):
    return jax.shard_map(
        per_device,
        mesh=mesh,
        in_specs=(P("seq", "head"), P("seq", "head"), P("seq", "head"), P(), P("head", None)),
        out_specs=P(("seq", "head"), None),
        check_vma=False,
    )
```

```python
import functools
import math

import jax
import jax.numpy as jnp
from jax import lax
from jax.experimental import pallas as pl
from jax.experimental.pallas import tpu as pltpu
from jax.sharding import PartitionSpec as P

HD = 128
HEADS_HERE = 2
RATES = (4, 16, 64)
BLOCK = 1024
TILE = 256
ROWS = 144
LSUM = 128
MROW = 129
LOG2_SCALE = math.log2(math.e) / math.sqrt(HD)
FILL = -1e30
SMALL, LARGE = 2.0**-60, 2.0**100
VMEM_BYTES = 18 * 2**20
MID, WIDE, FAR = 1024, 256, 64
FEW = WIDE + FAR
LATE = MID // 2 + WIDE // 2 + 2 * FAR
OFFS, OFFS_OTHER, ORDER, HALF, HALF_OTHER, CORE, Y_ODD, WIDE_POS, FAR_POS = 0, 6, 12, 17, 18, 19, 20, 21, 31

f32, bf16 = jnp.float32, jnp.bfloat16


def dot(a, b):
    return jnp.dot(a, b, preferred_element_type=f32)


def aligned(x, n):
    return x if isinstance(x, int) else pl.multiple_of(x, n)


def transposed_queries(q):
    q = q.astype(f32) * LOG2_SCALE
    high = q.astype(bf16)
    low = (q - high.astype(f32)).astype(bf16)
    return jnp.concatenate([high, low], axis=1).T


def scores(k, qt):
    return dot(jnp.concatenate([k, k], axis=1), qt)


def with_ones(v):
    return jnp.concatenate([v.T, jnp.ones((ROWS - HD, v.shape[0]), v.dtype)], axis=0)


def pieces(x):
    first = x.astype(bf16).astype(f32)
    second = (x - first).astype(bf16).astype(f32)
    return first, second, x - first - second


def stat_rows(total, exponent, count):
    row = lax.broadcasted_iota(jnp.int32, (ROWS - HD, count), 0)
    parts = (total,) + (pieces(exponent) if exponent is not None else ())
    out = jnp.zeros((ROWS - HD, count), f32)
    for n, part in enumerate(parts):
        out = jnp.where(row == n, part, out)
    return out


def within_range(total, counted=None):
    ok = (total >= SMALL) & (total <= LARGE)
    if counted is not None:
        ok = ok | ~counted
    return jnp.min(jnp.where(ok, 1.0, 0.0)) > 0.5


def rescaled(store, get_queries, count, blocks, block):
    def step(j, carry):
        peak, acc = carry
        k, vt, allowed = block(j)
        s = jnp.where(allowed, scores(k, get_queries()), FILL)
        new = jnp.maximum(peak, jnp.max(s, axis=0, keepdims=True))
        p = jnp.where(allowed, jnp.exp2(s - new), 0.0)
        return new, acc * jnp.exp2(peak - new) + dot(vt, p.astype(bf16))

    peak, acc = lax.fori_loop(
        0, blocks, step, (jnp.full((1, count), FILL, f32), jnp.zeros((ROWS, count), f32))
    )
    store(acc, acc[LSUM : LSUM + 1], peak)


def position_mask(key_first, query_pos, rows):
    key_pos = key_first + lax.broadcasted_iota(jnp.int32, (rows, query_pos.shape[1]), 0)
    return key_pos <= query_pos


def lane_positions(first, count):
    return first + lax.broadcasted_iota(jnp.int32, (1, count), 1)


def pick(x_ref, cols, scr, off_ref, outs):
    scr[...] = x_ref[:, cols].astype(f32)
    step = pl.program_id(0)
    for level, (out_ref, row, out_cols) in enumerate(outs):
        count = scr.shape[0] // RATES[level]
        picked = scr[pl.ds(off_ref[OFFS + level * HEADS_HERE + scr_head(cols)], count, stride=RATES[level]), :]
        first = pl.multiple_of(row + step * count, 16)
        out_ref[pl.ds(first, count), out_cols] = picked.astype(bf16)


def scr_head(cols):
    return cols.start // HD


def select_kv_kernel(info_ref, k_ref, v_ref, mid_ref, few_ref, scr):
    for h in range(HEADS_HERE):
        cols = slice(h * HD, (h + 1) * HD)
        for n, x_ref in enumerate((k_ref, v_ref)):
            out_cols = slice((2 * n + h) * HD, (2 * n + h + 1) * HD)
            pick(x_ref, cols, scr.at[n, h], info_ref, ((mid_ref, 0, out_cols), (few_ref, 0, out_cols), (few_ref, WIDE, out_cols)))


def select_q_kernel(info_ref, q_ref, qm_ref, few_ref, scr):
    for h in range(HEADS_HERE):
        cols = slice(h * HD, (h + 1) * HD)
        pick(q_ref, cols, scr.at[h], info_ref, ((qm_ref, 0, cols), (few_ref, 0, cols), (few_ref, WIDE, cols)))


def vmem(count):
    return [pl.BlockSpec(memory_space=pltpu.VMEM)] * count


SMEM = pl.BlockSpec(memory_space=pltpu.SMEM)
ANY = pl.BlockSpec(memory_space=pl.ANY)


def whole(shape):
    return pl.BlockSpec(shape, lambda *_: (0,) * len(shape))


def params():
    return pltpu.CompilerParams(vmem_limit_bytes=VMEM_BYTES)


def cost(pairs, bytes_accessed):
    return pl.CostEstimate(
        flops=int(pairs * 1024 * 1.5), bytes_accessed=int(bytes_accessed), transcendentals=int(pairs)
    )


def shaped(*shape, dtype=bf16):
    return jax.ShapeDtypeStruct(shape, dtype)


def select_kv(info, k, v):
    chunk = pl.BlockSpec((BLOCK, 256), lambda i: (i, 0))
    return pl.pallas_call(
        select_kv_kernel,
        grid=(k.shape[0] // BLOCK,),
        in_specs=[SMEM, chunk, chunk],
        out_specs=[whole((MID, 512)), whole((FEW, 512))],
        out_shape=[shaped(MID, 512), shaped(FEW, 512)],
        scratch_shapes=[pltpu.VMEM((2, HEADS_HERE, BLOCK, HD), f32)],
        compiler_params=params(),
        name="select_kv",
    )(info, k, v)


def select_q(info, q):
    return pl.pallas_call(
        select_q_kernel,
        grid=(q.shape[0] // BLOCK,),
        in_specs=[SMEM, pl.BlockSpec((BLOCK, 256), lambda i: (i, 0))],
        out_specs=[whole((MID, 256)), whole((FEW, 256))],
        out_shape=[shaped(MID, 256), shaped(FEW, 256)],
        scratch_shapes=[pltpu.VMEM((HEADS_HERE, BLOCK, HD), f32)],
        compiler_params=params(),
        name="select_q",
    )(info, q)


def pack_kernel(count, *refs):
    *_, all_ref, far_ref, _ = refs
    for n, x_ref in enumerate(refs[:count]):
        all_ref[n * FEW : (n + 1) * FEW] = x_ref[...]
        far_ref[n * FAR : (n + 1) * FAR] = x_ref[WIDE:]


def pack(few, through, after):
    count = len(few)
    return pl.pallas_call(
        functools.partial(pack_kernel, count),
        in_specs=vmem(count) + [ANY] * (1 + len(after)),
        out_specs=vmem(2) + [ANY],
        out_shape=[shaped(count * FEW, 512), shaped(count * FAR, 512), shaped(*through.shape)],
        input_output_aliases={count: 2},
        compiler_params=params(),
        cost_estimate=pl.CostEstimate(flops=0, bytes_accessed=4 * 2**20, transcendentals=0),
        name="pack",
    )(*few, through, *after)


def diagonal(out_ref, h, k, vt, qt_ref):
    row = lax.broadcasted_iota(jnp.int32, (TILE, TILE), 0)
    col = lax.broadcasted_iota(jnp.int32, (TILE, TILE), 1)
    rows = []
    for g in range(BLOCK // TILE):
        first = g * TILE
        p = jnp.exp2(scores(k[first : first + TILE], qt_ref[h, :, first:]))
        parts = [jnp.where(row <= col, p[:, :TILE], 0.0), p[:, TILE:]]
        if g:
            parts = [jnp.zeros((TILE, first), f32)] + parts
        rows.append(jnp.concatenate([x for x in parts if x.shape[1]], axis=1).astype(bf16))
    out_ref[h] += dot(vt, jnp.concatenate(rows, axis=0))


def store_partial(out_ref, h, acc, total, exponent):
    count = acc.shape[1]
    out_ref[h, :HD] = acc[:HD]
    out_ref[h, HD:] = stat_rows(total, exponent, count)


def near_kernel(first, skipped, info_ref, q_ref, k_ref, v_ref, *refs):
    refs = refs[skipped:]
    block = info_ref[ORDER + first + pl.program_id(0)]

    @pl.when(block >= 0)
    def _():
        near_block(first, block, q_ref, k_ref, v_ref, *refs)


def near_block(first, block, q_ref, k_ref, v_ref, *refs):
    out_ref, *early_ref, qt = refs

    def values_at(start, rows, h):
        return with_ones(v_ref[pl.ds(start, rows), h * HD : (h + 1) * HD])

    for h in range(HEADS_HERE):
        qt[h] = transposed_queries(q_ref[:, h * HD : (h + 1) * HD])
    out_ref[...] = jnp.zeros(out_ref.shape, f32)

    def full(j, carry):
        start = aligned(j * BLOCK, BLOCK)
        for h in range(HEADS_HERE):
            s = scores(k_ref[pl.ds(start, BLOCK), h * HD : (h + 1) * HD], qt[h])
            out_ref[h] += dot(values_at(start, BLOCK, h), jnp.exp2(s).astype(bf16))
        return carry

    lax.fori_loop(0, block, full, 0)
    start = aligned(block * BLOCK, BLOCK)
    for h in range(HEADS_HERE):
        cols = slice(h * HD, (h + 1) * HD)
        diagonal(out_ref, h, k_ref[pl.ds(start, BLOCK), cols], values_at(start, BLOCK, h), qt)
    total = jnp.concatenate([out_ref[h, LSUM : LSUM + 1] for h in range(HEADS_HERE)], axis=0)
    ok = within_range(total)
    for h in range(HEADS_HERE):
        out_ref[h, HD:] = stat_rows(total[h : h + 1], None, BLOCK)

    @pl.when(jnp.logical_not(ok))
    def _():
        for h in range(HEADS_HERE):
            cols = slice(h * HD, (h + 1) * HD)
            query_pos = lane_positions(block * BLOCK, BLOCK)

            def key_block(j):
                first = aligned(j * TILE, TILE)
                return (
                    k_ref[pl.ds(first, TILE), cols],
                    values_at(first, TILE, h),
                    position_mask(first, query_pos, TILE),
                )

            rescaled(
                functools.partial(store_partial, out_ref, h),
                lambda: qt[h],
                BLOCK,
                (block + 1) * (BLOCK // TILE),
                key_block,
            )

    if early_ref:

        @pl.when(pl.program_id(0) < 2)
        def _():
            for h in range(HEADS_HERE):
                scale = 1.0 / out_ref[h, LSUM : LSUM + 1]
                early_ref[0][h * HD : (h + 1) * HD] = (out_ref[h, :HD] * scale).astype(bf16)


def near(first, steps, info, q, k, v, after):
    tok = q.shape[0]
    early = first == 0
    return pl.pallas_call(
        functools.partial(near_kernel, first, len(after)),
        grid_spec=pltpu.PrefetchScalarGridSpec(
            num_scalar_prefetch=1,
            grid=(steps,),
            in_specs=[
                pl.BlockSpec((BLOCK, 256), lambda i, info: (jnp.maximum(info[ORDER + first + i], 0), 0)),
                whole((tok, 256)),
                whole((tok, 256)),
            ]
            + [ANY] * len(after),
            out_specs=[pl.BlockSpec((HEADS_HERE, ROWS, BLOCK), lambda i, info: (0, 0, i))]
            + [pl.BlockSpec((256, BLOCK), lambda i, info: (0, jnp.minimum(i, 1)))] * early,
            scratch_shapes=[pltpu.VMEM((HEADS_HERE, 256, BLOCK), bf16)],
        ),
        out_shape=[shaped(HEADS_HERE, ROWS, steps * BLOCK, dtype=f32)] + [shaped(256, tok // 2)] * early,
        compiler_params=params(),
        cost_estimate=cost(steps * BLOCK * 2300 * 2, 10 * 2**20),
        name="near",
    )(info, q, k, v, *after)


def mid_kernel(causal, flag_at, info_ref, q_ref, *refs):
    kv_refs, (out_ref, qt, vt) = refs[:2], refs[-3:]
    others = info_ref[flag_at] == 1
    for h in range(HEADS_HERE):
        qt[h] = transposed_queries(q_ref[:, h * HD : (h + 1) * HD])
    out_ref[...] = jnp.zeros(out_ref.shape, f32)

    def keys(n, h):
        return kv_refs[n].at[:, h * HD : (h + 1) * HD]

    def values(n):
        for h in range(HEADS_HERE):
            vt[n, h] = with_ones(kv_refs[n][:, (2 + h) * HD : (3 + h) * HD])

    if causal:
        values(0)
        for h in range(HEADS_HERE):
            diagonal(out_ref, h, keys(0, h)[...], vt[0, h], qt)

    @pl.when(others)
    def _():
        for n in range(1 if causal else 0, len(kv_refs)):
            values(n)
            for h in range(HEADS_HERE):
                p = jnp.exp2(scores(keys(n, h)[...], qt[h])).astype(bf16)
                out_ref[h] += dot(vt[n, h], p)

    total = jnp.concatenate([out_ref[h, LSUM : LSUM + 1] for h in range(HEADS_HERE)], axis=0)
    ok = within_range(total)
    for h in range(HEADS_HERE):
        out_ref[h, HD:] = stat_rows(total[h : h + 1], None, BLOCK)

    @pl.when(jnp.logical_and(jnp.logical_not(ok), True if causal else others))
    def _():
        for h in range(HEADS_HERE):
            query_pos = lane_positions(0, BLOCK)
            peak = jnp.full((1, BLOCK), FILL, f32)
            acc = jnp.zeros((ROWS, BLOCK), f32)
            for n in range(len(kv_refs)):
                own = causal and n == 0
                key_first = 0 if own else jnp.where(others, -BLOCK, BLOCK)

                def step(j, carry):
                    peak, acc = carry
                    first = aligned(j * TILE, TILE)
                    allowed = position_mask(key_first + first, query_pos, TILE)
                    s = jnp.where(allowed, scores(keys(n, h)[pl.ds(first, TILE), :], qt[h]), FILL)
                    new = jnp.maximum(peak, jnp.max(s, axis=0, keepdims=True))
                    p = jnp.where(allowed, jnp.exp2(s - new), 0.0)
                    vt_tile = with_ones(kv_refs[n][pl.ds(first, TILE), (2 + h) * HD : (3 + h) * HD])
                    return new, acc * jnp.exp2(peak - new) + dot(vt_tile, p.astype(bf16))

                peak, acc = lax.fori_loop(0, BLOCK // TILE, step, (peak, acc))
            store_partial(out_ref, h, acc, acc[LSUM : LSUM + 1], peak)


def mid(causal, flag_at, info, q, kvs, after):
    return pl.pallas_call(
        functools.partial(mid_kernel, causal, flag_at),
        grid=(1,),
        in_specs=[SMEM, whole((MID, 256))] + [whole((MID, 512))] * len(kvs) + [ANY] * len(after),
        out_specs=whole((HEADS_HERE, ROWS, BLOCK)),
        out_shape=shaped(HEADS_HERE, ROWS, BLOCK, dtype=f32),
        scratch_shapes=[
            pltpu.VMEM((HEADS_HERE, 256, BLOCK), bf16),
            pltpu.VMEM((len(kvs), HEADS_HERE, ROWS, BLOCK), bf16),
        ],
        compiler_params=params(),
        cost_estimate=cost(2 * BLOCK * BLOCK * 1.8, 5 * 2**20),
        name="mid",
    )(info, q, *kvs, *after)


def pool_level(rows, pos_at, info_ref, q_refs, kv, qt, vt, out_refs):
    q_count = len(q_refs)
    block_rows = q_refs[0].shape[0]
    count = q_count * block_rows
    total_keys = kv.shape[0]
    chunk = min(total_keys, 1024)
    query_pos = jnp.concatenate([lane_positions(info_ref[pos_at + n], block_rows) for n in range(q_count)], axis=1)
    counted = query_pos >= 0
    key_iota = lax.broadcasted_iota(jnp.int32, (rows, 1), 0)
    key_pos = jnp.concatenate(
        [info_ref[pos_at + q_count + n] + key_iota for n in range(total_keys // rows)], axis=0
    )
    for h in range(HEADS_HERE):
        q = jnp.concatenate([q_ref[:, h * HD : (h + 1) * HD] for q_ref in q_refs], axis=0)
        qt[h] = transposed_queries(q)
        vt[h] = with_ones(kv[:, (2 + h) * HD : (3 + h) * HD])

    def store(h, acc, total, peak):
        for n in range(q_count):
            cols = slice(n * block_rows, (n + 1) * block_rows)
            peak_here = None if peak is None else peak[:, cols]
            if n == 0:
                store_partial(out_refs[n], h, acc[:, cols], total[:, cols], peak_here)
            else:
                out_refs[n][h] = split_rows(acc[:HD, cols], total[:, cols], peak_here)

    def keys(h, first, size):
        return kv[first : first + size, h * HD : (h + 1) * HD]

    totals = []
    for h in range(HEADS_HERE):
        acc = jnp.zeros((ROWS, count), f32)
        for first in range(0, total_keys, chunk):
            s = scores(keys(h, first, chunk), qt[h])
            allowed = key_pos[first : first + chunk] <= query_pos
            p = jnp.where(allowed, jnp.exp2(s), 0.0).astype(bf16)
            acc = acc + dot(vt[h, :, first : first + chunk], p)
        total = acc[LSUM : LSUM + 1]
        totals.append(jnp.where(counted, total, 1.0))
        store(h, acc, total, None)

    @pl.when(jnp.logical_not(within_range(jnp.concatenate(totals, axis=0))))
    def _():
        for h in range(HEADS_HERE):
            peak = jnp.full((1, count), FILL, f32)
            acc = jnp.zeros((ROWS, count), f32)
            for first in range(0, total_keys, TILE):
                allowed = key_pos[first : first + TILE] <= query_pos
                s = jnp.where(allowed, scores(keys(h, first, TILE), qt[h]), FILL)
                new = jnp.maximum(peak, jnp.max(s, axis=0, keepdims=True))
                p = jnp.where(allowed, jnp.exp2(s - new), 0.0).astype(bf16)
                acc = acc * jnp.exp2(peak - new) + dot(vt[h, :, first : first + TILE], p)
                peak = new
            store(h, acc, acc[LSUM : LSUM + 1], peak)


def level_kernel(rows, q_row, pos_at, places, q_count, source_count, info_ref, *refs):
    *refs, kv, qt, vt, sems = refs
    q_refs = [q.at[q_row : q_row + rows] for q in refs[:q_count]]
    sources, out_refs = refs[q_count : q_count + source_count], refs[-q_count:]
    copies = []
    place = 0
    for n, (source, row, count) in enumerate(places):
        dst = kv.at[place : place + count]
        copies.append(pltpu.make_async_copy(sources[source].at[row : row + count], dst, sems.at[n]))
        place += count
    for copy in copies:
        copy.start()
    for copy in copies:
        copy.wait()
    pool_level(rows, pos_at, info_ref, q_refs, kv, qt, vt, out_refs)


def level(name, rows, q_row, pos_at, places, info, qs, sources, after):
    keys = sum(count for _, _, count in places)
    count = len(qs) * rows
    return pl.pallas_call(
        functools.partial(level_kernel, rows, q_row, pos_at, tuple(places), len(qs), len(sources)),
        in_specs=[SMEM] + vmem(len(qs)) + [ANY] * (len(sources) + len(after)),
        out_specs=vmem(len(qs)),
        out_shape=[shaped(HEADS_HERE, ROWS, rows, dtype=bf16 if n else f32) for n in range(len(qs))],
        scratch_shapes=[
            pltpu.VMEM((keys, 512), bf16),
            pltpu.VMEM((HEADS_HERE, 256, count), bf16),
            pltpu.VMEM((HEADS_HERE, ROWS, keys), bf16),
            pltpu.SemaphoreType.DMA((len(places),)),
        ],
        compiler_params=params(),
        cost_estimate=cost(2 * count * keys, 4 * 2**20),
        name=name,
    )(info, *qs, *sources, *after)


def exponent_of(x):
    m = x[MROW : MROW + 1] + x[MROW + 1 : MROW + 2] + x[MROW + 2 : MROW + 3]
    return jnp.where(x[LSUM : LSUM + 1] > 0.0, m, FILL)


def combined(parts):
    peaks = [exponent_of(x) for x in parts]
    peak = functools.reduce(jnp.maximum, peaks)
    out = sum(x[: LSUM + 1] * jnp.exp2(m - peak) for x, m in zip(parts, peaks))
    return out, peak


def split_rows(sums, total, peak):
    rows = pieces(total) + (pieces(peak) if peak is not None else ())
    row = lax.broadcasted_iota(jnp.int32, (ROWS - HD, total.shape[1]), 0)
    stats = jnp.zeros((ROWS - HD, total.shape[1]), f32)
    for n, r in enumerate(rows):
        stats = jnp.where(row == n, r, stats)
    return jnp.concatenate([sums, stats], axis=0).astype(bf16)


def wider(x, count):
    return x if x.shape[1] == count else jnp.concatenate([x, jnp.zeros((x.shape[0], count - x.shape[1]), x.dtype)], axis=1)


def one_hot(targets, count):
    parts = []
    for rows, rate, first, *offset in targets:
        width = count if first is not None else TILE
        at = lax.broadcasted_iota(jnp.int32, (1, width), 1) - (offset[0] if first is None else first)
        row_of = jnp.where(at & (rate - 1) == 0, at >> (rate.bit_length() - 1), -1)
        here = rows if first is not None else TILE // rate
        row = lax.broadcasted_iota(jnp.int32, (here, width), 0)
        part = jnp.where(row == row_of, 1.0, 0.0).astype(bf16)
        if first is None:
            groups = []
            for g in range(count // TILE):
                above, below = g * here, rows - (g + 1) * here
                column = [jnp.zeros((above, TILE), bf16)] * (above > 0) + [part] + [jnp.zeros((below, TILE), bf16)] * (below > 0)
                groups.append(jnp.concatenate(column, axis=0))
            part = jnp.concatenate(groups, axis=1)
        parts.append(part)
    return jnp.concatenate(parts, axis=0)


def whole_form(x):
    x = x.astype(f32)
    total = x[LSUM : LSUM + 1] + x[LSUM + 1 : LSUM + 2] + x[LSUM + 2 : LSUM + 3]
    return jnp.concatenate([x[:HD], total, x[LSUM + 3 : LSUM + 6], x[LSUM + 6 :], x[LSUM + 6 : LSUM + 8]], axis=0)


def largest_exponent(parts, places):
    seen = []
    for x, place in zip(parts, places):
        for h in range(HEADS_HERE):
            row = jnp.abs(x[h, place : place + 1].astype(f32))
            width = min(row.shape[1], 128)
            for first in range(0, row.shape[1], width):
                seen.append(wider(row[:, first : first + width], 128))
    return jnp.max(functools.reduce(jnp.maximum, seen))


def merge_kernel(for_other, info_ref, near_ref, *refs):
    near_2, *refs = (None, *refs) if for_other else refs
    mid_a, mid_b, wide_a, wide_b, far_a, far_b, out_ref, first_ref = refs
    step = pl.program_id(0)
    half = info_ref[HALF_OTHER if for_other else HALF]
    start = (2 * half + step) * BLOCK
    if for_other:
        first_ref = near_ref
    else:
        in_first = jnp.logical_and(half == 1, step == 1)

        @pl.when(in_first)
        def _():
            first_ref[...] = near_ref[...]

        @pl.when(jnp.logical_not(in_first))
        def _():
            first_ref[...] = near_2[...]

    local, sent = [first_ref, mid_a, mid_b, wide_a, far_a], [wide_b, far_b]
    largest = largest_exponent(local + sent, [MROW] * len(local) + [LSUM + 3] * len(sent))

    def take_of(h):
        offs = [info_ref[OFFS + level * HEADS_HERE + h] for level in range(3)]
        return one_hot(
            (
                (256, RATES[0], None, offs[0]),
                (128, RATES[1], offs[1] + half * 2 * BLOCK - start),
                (128, RATES[2], offs[2] - start),
            ),
            BLOCK,
        )

    def finish(h, take, rows):
        where = slice(h * HD, (h + 1) * HD)
        if not for_other:
            out_ref[where] = rows
            return
        picked = lax.dot_general(rows, take, (((1,), (1,)), ((), ())), preferred_element_type=f32).astype(bf16)
        out_ref[where, pl.ds(aligned(step * 256, 256), 256)] = picked[:, :256]
        out_ref[where, 512:] = jnp.where(step == 0, picked[:, 256:], out_ref[where, 512:] + picked[:, 256:])

    @pl.when(largest == 0.0)
    def _():
        for h in range(HEADS_HERE):
            take = take_of(h)
            far = far_a[h] + whole_form(far_b[h])
            groups = [mid_a[h] + mid_b[h], wide_a[h] + whole_form(wide_b[h]), wider(far, 128)]
            x = jnp.concatenate([split_rows(g[:HD], g[LSUM : LSUM + 1], None) for g in groups], axis=1)
            y = dot(x, take)
            total = first_ref[h, LSUM : LSUM + 1] + y[HD : HD + 1] + y[HD + 1 : HD + 2] + y[HD + 2 : HD + 3]
            finish(h, take, ((first_ref[h, :HD] + y[:HD]) * (1.0 / total)).astype(bf16))

    @pl.when(largest != 0.0)
    def _():
        for h in range(HEADS_HERE):
            take = take_of(h)
            first = first_ref[h]
            spread = []
            peak = exponent_of(first)
            row = 0
            for level in ((mid_a, mid_b), (wide_a, wide_b), (far_a, far_b)):
                x, x_peak = combined([whole_form(x[h]) if x.dtype == bf16 else x[h] for x in level])
                count = max(x.shape[1], 128)
                split = wider(split_rows(x[:HD], x[LSUM : LSUM + 1], x_peak), count)
                y = dot(split, take[row : row + count])
                row += count
                total = y[128:129] + y[129:130] + y[130:131]
                y_peak = jnp.where(total > 0.0, y[131:132] + y[132:133] + y[133:134], FILL)
                spread.append((y, total, y_peak))
                peak = jnp.maximum(peak, y_peak)
            scale = jnp.exp2(exponent_of(first) - peak)
            acc = first[:HD] * scale
            total = first[LSUM : LSUM + 1] * scale
            for y, y_total, y_peak in spread:
                scale = jnp.exp2(y_peak - peak)
                acc = acc + y[:HD] * scale
                total = total + y_total * scale
            finish(h, take, (acc / total).astype(bf16))


def merge(for_other, info, nears, mids, wides, fars):
    place_of = HALF_OTHER if for_other else HALF
    near_block_shape = (HEADS_HERE, ROWS, BLOCK)
    if for_other:
        near_specs = [pl.BlockSpec(near_block_shape, lambda i, info: (0, 0, i))]
    else:
        near_specs = [
            pl.BlockSpec(near_block_shape, lambda i, info: (0, 0, 2)),
            pl.BlockSpec(near_block_shape, lambda i, info: (0, 0, i)),
        ]
    return pl.pallas_call(
        functools.partial(merge_kernel, for_other),
        grid_spec=pltpu.PrefetchScalarGridSpec(
            num_scalar_prefetch=1,
            grid=(2,),
            in_specs=[
                *near_specs,
                *[pl.BlockSpec((HEADS_HERE, ROWS, 256), lambda i, info: (0, 0, 2 * info[place_of] + i))] * 2,
                *[pl.BlockSpec((HEADS_HERE, ROWS, 128), lambda i, info: (0, 0, info[place_of]))] * 2,
                *[whole((HEADS_HERE, ROWS, FAR))] * 2,
            ],
            out_specs=whole((256, LATE)) if for_other else pl.BlockSpec((256, BLOCK), lambda i, info: (0, i)),
            scratch_shapes=[
                pltpu.VMEM((HEADS_HERE, ROWS, 128 if for_other else BLOCK), f32),
            ],
        ),
        out_shape=shaped(256, LATE if for_other else 2 * BLOCK),
        compiler_params=params(),
        cost_estimate=cost(2 * 2 * BLOCK * 256, 6 * 2**20),
        name="merge",
    )(info, *nears, *mids, *wides, *fars)


def project_kernel(info_ref, own_ref, early_ref, late_ref, w_own, w_other, out_ref):
    tile = own_ref.shape[1]
    step = pl.program_id(0)
    half = info_ref[HALF]
    parts = [own_ref[...]]
    col = lane_positions(0, tile)
    for h in range(HEADS_HERE):
        rows = slice(h * HD, (h + 1) * HD)
        mid_off, wide_off, far_off = (info_ref[OFFS_OTHER + level * HEADS_HERE + h] for level in range(3))
        in_mid = wide_off % RATES[0] == mid_off
        far_done = jnp.logical_or(far_off % RATES[0] == mid_off, far_off % RATES[1] == wide_off)
        nowhere = -(1 << 20)
        start = step * tile
        take = one_hot(
            (
                (tile // RATES[0], RATES[0], None, mid_off),
                (128, RATES[1], jnp.where(in_mid, nowhere, wide_off - start)),
                (128, RATES[2], jnp.where(far_done, nowhere, far_off - half * 2 * BLOCK - start)),
            ),
            tile,
        )
        near_rows = late_ref[rows, pl.ds(aligned(step * (tile // RATES[0]), tile // RATES[0]), tile // RATES[0])]
        late = dot(jnp.concatenate([near_rows, late_ref[rows, 512:]], axis=1), take)
        reached = (col % RATES[0] == mid_off) | (col % RATES[1] == wide_off) | (col % RATES[2] == far_off)
        parts.append(jnp.where(reached, late, early_ref[rows].astype(f32)).astype(bf16))
    w = jnp.concatenate([w_own[...], w_other[...]], axis=0)
    out_ref[...] = dot(jnp.concatenate(parts, axis=0).T, w).astype(bf16)


def project(info, own, early, late, w_own, w_other):
    rows, width = own.shape[1], w_own.shape[1]
    tile = 512
    return pl.pallas_call(
        project_kernel,
        grid=(rows // tile,),
        in_specs=[
            SMEM,
            pl.BlockSpec((256, tile), lambda i: (0, i)),
            pl.BlockSpec((256, tile), lambda i: (0, i)),
            whole((256, LATE)),
            whole((256, width)),
            whole((256, width)),
        ],
        out_specs=pl.BlockSpec((tile, width), lambda i: (i, 0)),
        out_shape=shaped(rows, width),
        compiler_params=params(),
        cost_estimate=pl.CostEstimate(flops=2 * rows * 512 * width, bytes_accessed=12 * 2**20, transcendentals=0),
        name="project",
    )(info, own, early, late, w_own, w_other)


def place(s):
    return s >> 4, s >> 3 & 1, s >> 1 & 3, s & 1


def index(z, xh, y, core):
    return ((z * 2 + xh) * 4 + y) * 2 + core


def send(x, to):
    pairs = []
    for s in range(64):
        target = to(*place(s))
        if target is not None:
            pairs.append((s, index(*target)))
    return lax.ppermute(x, "seq", pairs)


def other_core(x):
    return send(x, lambda z, xh, y, c: (z, xh, y, 1 - c))


def y_step(x, by):
    return send(x, lambda z, xh, y, c: (z, xh, (y + by) % 4, c))


def later_z(x, by):
    return send(x, lambda z, xh, y, c: (z + by, xh, y, c) if z + by < 4 else None)


def ints(*values):
    return jnp.stack([jnp.asarray(v, jnp.int32) for v in values])


def swap_heads(x):
    return lax.ppermute(x, "head", [(0, 1), (1, 0)])


def scalars(offsets):
    head = lax.axis_index("head")
    z, xh, y, core = place(lax.axis_index("seq"))
    other = 1 - head
    flat = offsets.astype(jnp.int32)

    def offs(group):
        return lax.dynamic_slice_in_dim(flat, group * HEADS_HERE, HEADS_HERE, 1).reshape(-1)

    ys = [y, (y + 3) % 4, (y + 1) % 4, (y + 2) % 4]
    everything, nothing = 1 << 20, -(1 << 20)
    wide_pos = [
        (y * 2 + core) * WIDE,
        jnp.where(xh == 0, everything, nothing),
        *[(p * 2 + c) * WIDE for c in (core, 1 - core) for p in ys],
    ]
    far_pos = [
        ((z * 2 + xh) * 8 + y * 2 + core) * FAR,
        jnp.where((z == 0) & (xh == 1), nothing, ((z * 2 + 1 - xh) * 8 + y * 2 + core) * FAR),
    ]
    for cores, back in ((core, 0), (1 - core, 0), (core, 1), (core, 2), (core, 3), (1 - core, 1), (1 - core, 2), (1 - core, 3)):
        for p in ys:
            here = (((z - back) * 2 + xh) * 8 + p * 2 + cores) * FAR
            far_pos.append(jnp.where(z >= back, here, 2 * everything))
    order = [2 * other, 2 * other + 1, jnp.where(head == 1, 3, -1), 2 * head, jnp.where(head == 1, -1, 1)]
    rest = order + [head, other, core, y % 2] + wide_pos + far_pos
    return jnp.concatenate([offs(head), offs(other), ints(*rest)])


def per_device(queries, keys, values, offsets, out_weight):
    info = scalars(offsets)
    kv_mid, few = select_kv(info, keys, values)
    below = y_step(few, 1)
    above = y_step(few, -1)
    across = y_step(few, 2)
    kv_mid_core = send(kv_mid, lambda z, xh, y, c: (z, xh, y, 1) if c == 0 else None)
    q_mid, q_few = select_q(info, queries)
    q_few_in = send(q_few, lambda z, xh, y, c: (z, 1 - xh, y, c))

    near_1, early_other = near(0, 3, info, queries, keys, values, [kv_mid_core, q_few_in])
    weight_other = swap_heads(out_weight)
    packed, far_here, kv_mid_later = pack([few, below, above, across], kv_mid, [near_1, weight_other])
    packed_core = other_core(packed)
    kv_mid_below = send(kv_mid_later, lambda z, xh, y, c: (z, xh, y + 1, c) if y % 2 == 0 else None)
    far_z = [later_z(far_here, d) for d in (1, 2, 3)]
    early = swap_heads(early_other)
    mid_a = mid(True, CORE, info, q_mid, [kv_mid, kv_mid_core], [packed])
    (near_2,) = near(3, 2, info, queries, keys, values, [mid_a])
    wide_places = [(n, b * FEW, WIDE) for n in (0, 1) for b in range(4)]
    wide, wide_out = level("wide", WIDE, 0, WIDE_POS, wide_places, info, [q_few, q_few_in], [packed, packed_core], [near_2])
    wide_back = send(wide_out, lambda z, xh, y, c: (z, 1, y, c) if xh == 0 else None)
    kv_mid_below_core = other_core(kv_mid_below)
    far_z_core = other_core(jnp.concatenate(far_z, axis=0))
    far_places = [(n, b * FEW + WIDE, FAR) for n in (0, 1) for b in range(4)]
    far_places += [(n, 0, 4 * FAR) for n in (2, 3, 4)] + [(5, 0, 12 * FAR)]
    far_sources = [packed, packed_core, *far_z, far_z_core]
    far, far_out = level("far", FAR, WIDE, FAR_POS, far_places, info, [q_few, q_few_in], far_sources, [wide])
    far_back = send(far_out, lambda z, xh, y, c: (z, 1 - xh, y, c))
    mid_b = mid(False, Y_ODD, info, q_mid, [kv_mid_below, kv_mid_below_core], [far, early])

    parts = ((mid_a, mid_b), (wide, wide_back), (far, far_back))
    late_rows = merge(True, info, [near_1], *parts)
    late = swap_heads(late_rows)
    attended_own = merge(False, info, [near_1, near_2], *parts)
    return project(info, attended_own, early, late, out_weight, weight_other)


def solution(mesh):
    return jax.shard_map(
        per_device,
        mesh=mesh,
        in_specs=(P("seq", "head"), P("seq", "head"), P("seq", "head"), P(), P("head", None)),
        out_specs=P(("seq", "head"), None),
        check_vma=False,
    )
```

```python
import functools
import math

import jax
import jax.numpy as jnp
from jax import lax
from jax.experimental import pallas as pl
from jax.experimental.pallas import tpu as pltpu
from jax.sharding import PartitionSpec as P

HD = 128
HEADS_HERE = 2
RATES = (4, 16, 64)
BLOCK = 1024
TILE = 256
ROWS = 144
LSUM = 128
MROW = 129
LOG2_SCALE = math.log2(math.e) / math.sqrt(HD)
FILL = -1e30
SMALL, LARGE = 2.0**-60, 2.0**100
VMEM_BYTES = 12 * 2**20
MID, WIDE, FAR = 1024, 256, 64
FEW = WIDE + FAR
LATE = MID // 2 + WIDE // 2 + 2 * FAR
OFFS, OFFS_OTHER, ORDER, HALF, HALF_OTHER, CORE, Y_ODD, WIDE_POS, FAR_POS = 0, 6, 12, 17, 18, 19, 20, 21, 31

f32, bf16 = jnp.float32, jnp.bfloat16


def dot(a, b):
    return jnp.dot(a, b, preferred_element_type=f32)


def aligned(x, n):
    return x if isinstance(x, int) else pl.multiple_of(x, n)


def transposed_queries(q):
    q = q.astype(f32) * LOG2_SCALE
    high = q.astype(bf16)
    low = (q - high.astype(f32)).astype(bf16)
    return jnp.concatenate([high, low], axis=1).T


def scores(k, qt):
    return dot(jnp.concatenate([k, k], axis=1), qt)


def with_ones(v):
    return jnp.concatenate([v.T, jnp.ones((ROWS - HD, v.shape[0]), v.dtype)], axis=0)


def pieces(x):
    first = x.astype(bf16).astype(f32)
    second = (x - first).astype(bf16).astype(f32)
    return first, second, x - first - second


def stat_rows(total, exponent, count):
    row = lax.broadcasted_iota(jnp.int32, (ROWS - HD, count), 0)
    parts = (total,) + (pieces(exponent) if exponent is not None else ())
    out = jnp.zeros((ROWS - HD, count), f32)
    for n, part in enumerate(parts):
        out = jnp.where(row == n, part, out)
    return out


def within_range(total, counted=None):
    ok = (total >= SMALL) & (total <= LARGE)
    if counted is not None:
        ok = ok | ~counted
    return jnp.min(jnp.where(ok, 1.0, 0.0)) > 0.5


def rescaled(store, get_queries, count, blocks, block):
    def step(j, carry):
        peak, acc = carry
        k, vt, allowed = block(j)
        s = jnp.where(allowed, scores(k, get_queries()), FILL)
        new = jnp.maximum(peak, jnp.max(s, axis=0, keepdims=True))
        p = jnp.where(allowed, jnp.exp2(s - new), 0.0)
        return new, acc * jnp.exp2(peak - new) + dot(vt, p.astype(bf16))

    peak, acc = lax.fori_loop(
        0, blocks, step, (jnp.full((1, count), FILL, f32), jnp.zeros((ROWS, count), f32))
    )
    store(acc, acc[LSUM : LSUM + 1], peak)


def position_mask(key_first, query_pos, rows):
    key_pos = key_first + lax.broadcasted_iota(jnp.int32, (rows, query_pos.shape[1]), 0)
    return key_pos <= query_pos


def lane_positions(first, count):
    return first + lax.broadcasted_iota(jnp.int32, (1, count), 1)


def pick(x_ref, cols, scr, off_ref, outs):
    scr[...] = x_ref[:, cols].astype(f32)
    step = pl.program_id(0)
    for level, (out_ref, row, out_cols) in enumerate(outs):
        count = scr.shape[0] // RATES[level]
        picked = scr[pl.ds(off_ref[OFFS + level * HEADS_HERE + scr_head(cols)], count, stride=RATES[level]), :]
        first = pl.multiple_of(row + step * count, 16)
        out_ref[pl.ds(first, count), out_cols] = picked.astype(bf16)


def scr_head(cols):
    return cols.start // HD


def select_kv_kernel(info_ref, k_ref, v_ref, mid_ref, few_ref, again_ref, scr):
    for h in range(HEADS_HERE):
        cols = slice(h * HD, (h + 1) * HD)
        for n, x_ref in enumerate((k_ref, v_ref)):
            out_cols = slice((2 * n + h) * HD, (2 * n + h + 1) * HD)
            pick(x_ref, cols, scr.at[n, h], info_ref, ((mid_ref, 0, out_cols), (few_ref, 0, out_cols), (few_ref, WIDE, out_cols)))

    @pl.when(pl.program_id(0) == pl.num_programs(0) - 1)
    def _():
        again_ref[...] = mid_ref[...]


def select_q_kernel(info_ref, q_ref, w_ref, qm_ref, few_ref, part_ref, scr, sem):
    copy = pltpu.make_async_copy(w_ref.at[pl.ds(aligned(info_ref[CORE] * HD, HD), HD)], part_ref, sem)
    pl.when(pl.program_id(0) == 0)(copy.start)
    pl.when(pl.program_id(0) == pl.num_programs(0) - 1)(copy.wait)
    for h in range(HEADS_HERE):
        cols = slice(h * HD, (h + 1) * HD)
        pick(q_ref, cols, scr.at[h], info_ref, ((qm_ref, 0, cols), (few_ref, 0, cols), (few_ref, WIDE, cols)))


def vmem(count):
    return [pl.BlockSpec(memory_space=pltpu.VMEM)] * count


SMEM = pl.BlockSpec(memory_space=pltpu.SMEM)
ANY = pl.BlockSpec(memory_space=pl.ANY)


def whole(shape):
    return pl.BlockSpec(shape, lambda *_: (0,) * len(shape), pipeline_mode=pl.Buffered(1))


def params():
    return pltpu.CompilerParams(vmem_limit_bytes=VMEM_BYTES)


def cost(pairs, bytes_accessed):
    return pl.CostEstimate(
        flops=int(pairs * 1024 * 1.5), bytes_accessed=int(bytes_accessed), transcendentals=int(pairs)
    )


def shaped(*shape, dtype=bf16):
    return jax.ShapeDtypeStruct(shape, dtype)


def select_kv(info, k, v):
    chunk = pl.BlockSpec((BLOCK, 256), lambda i: (i, 0))
    return pl.pallas_call(
        select_kv_kernel,
        grid=(k.shape[0] // BLOCK,),
        in_specs=[SMEM, chunk, chunk],
        out_specs=[whole((MID, 512)), whole((FEW, 512)), whole((MID, 512))],
        out_shape=[shaped(MID, 512), shaped(FEW, 512), shaped(MID, 512)],
        scratch_shapes=[pltpu.VMEM((2, HEADS_HERE, BLOCK, HD), f32)],
        compiler_params=params(),
        name="select_kv",
    )(info, k, v)


def select_q(info, q, w):
    return pl.pallas_call(
        select_q_kernel,
        grid=(q.shape[0] // BLOCK,),
        in_specs=[SMEM, pl.BlockSpec((BLOCK, 256), lambda i: (i, 0)), ANY],
        out_specs=[whole((MID, 256)), whole((FEW, 256)), whole((HD, w.shape[1]))],
        out_shape=[shaped(MID, 256), shaped(FEW, 256), shaped(HD, w.shape[1])],
        scratch_shapes=[pltpu.VMEM((HEADS_HERE, BLOCK, HD), f32), pltpu.SemaphoreType.DMA],
        compiler_params=params(),
        name="select_q",
    )(info, q, w)


def pack_kernel(count, *refs):
    *_, all_ref, far_ref, _ = refs
    for n, x_ref in enumerate(refs[:count]):
        all_ref[n * FEW : (n + 1) * FEW] = x_ref[...]
        far_ref[n * FAR : (n + 1) * FAR] = x_ref[WIDE:]


def pack(few, through, after):
    count = len(few)
    return pl.pallas_call(
        functools.partial(pack_kernel, count),
        in_specs=vmem(count) + [ANY] * (1 + len(after)),
        out_specs=vmem(2) + [ANY],
        out_shape=[shaped(count * FEW, 512), shaped(count * FAR, 512), shaped(*through.shape)],
        input_output_aliases={count: 2},
        compiler_params=params(),
        cost_estimate=pl.CostEstimate(flops=0, bytes_accessed=4 * 2**20, transcendentals=0),
        name="pack",
    )(*few, through, *after)


def diagonal(out_ref, h, k, vt, qt_ref):
    row = lax.broadcasted_iota(jnp.int32, (TILE, TILE), 0)
    col = lax.broadcasted_iota(jnp.int32, (TILE, TILE), 1)
    rows = []
    for g in range(BLOCK // TILE):
        first = g * TILE
        p = jnp.exp2(scores(k[first : first + TILE], qt_ref[h, :, first:]))
        parts = [jnp.where(row <= col, p[:, :TILE], 0.0), p[:, TILE:]]
        if g:
            parts = [jnp.zeros((TILE, first), f32)] + parts
        rows.append(jnp.concatenate([x for x in parts if x.shape[1]], axis=1).astype(bf16))
    out_ref[h] += dot(vt, jnp.concatenate(rows, axis=0))


def store_partial(out_ref, h, acc, total, exponent):
    count = acc.shape[1]
    out_ref[h, :HD] = acc[:HD]
    out_ref[h, HD:] = stat_rows(total, exponent, count)


def near_kernel(first, skipped, info_ref, q_ref, k_ref, v_ref, *refs):
    refs = refs[skipped:]
    block = info_ref[ORDER + first + pl.program_id(0)]

    @pl.when(block >= 0)
    def _():
        near_block(first, block, q_ref, k_ref, v_ref, *refs)


def near_block(first, block, q_ref, k_ref, v_ref, *refs):
    out_ref, *early_ref, qt = refs

    def values_at(start, rows, h):
        return with_ones(v_ref[pl.ds(start, rows), h * HD : (h + 1) * HD])

    for h in range(HEADS_HERE):
        qt[h] = transposed_queries(q_ref[:, h * HD : (h + 1) * HD])
    out_ref[...] = jnp.zeros(out_ref.shape, f32)

    def full(j, carry):
        start = aligned(j * BLOCK, BLOCK)
        for h in range(HEADS_HERE):
            s = scores(k_ref[pl.ds(start, BLOCK), h * HD : (h + 1) * HD], qt[h])
            out_ref[h] += dot(values_at(start, BLOCK, h), jnp.exp2(s).astype(bf16))
        return carry

    lax.fori_loop(0, block, full, 0)
    start = aligned(block * BLOCK, BLOCK)
    for h in range(HEADS_HERE):
        cols = slice(h * HD, (h + 1) * HD)
        diagonal(out_ref, h, k_ref[pl.ds(start, BLOCK), cols], values_at(start, BLOCK, h), qt)
    total = jnp.concatenate([out_ref[h, LSUM : LSUM + 1] for h in range(HEADS_HERE)], axis=0)
    ok = within_range(total)
    for h in range(HEADS_HERE):
        out_ref[h, HD:] = stat_rows(total[h : h + 1], None, BLOCK)

    @pl.when(jnp.logical_not(ok))
    def _():
        for h in range(HEADS_HERE):
            cols = slice(h * HD, (h + 1) * HD)
            query_pos = lane_positions(block * BLOCK, BLOCK)

            def key_block(j):
                first = aligned(j * TILE, TILE)
                return (
                    k_ref[pl.ds(first, TILE), cols],
                    values_at(first, TILE, h),
                    position_mask(first, query_pos, TILE),
                )

            rescaled(
                functools.partial(store_partial, out_ref, h),
                lambda: qt[h],
                BLOCK,
                (block + 1) * (BLOCK // TILE),
                key_block,
            )

    if early_ref:

        @pl.when(pl.program_id(0) < 2)
        def _():
            for h in range(HEADS_HERE):
                scale = 1.0 / out_ref[h, LSUM : LSUM + 1]
                early_ref[0][h * HD : (h + 1) * HD] = (out_ref[h, :HD] * scale).astype(bf16)


def near(first, steps, info, q, k, v, after):
    tok = q.shape[0]
    early = first == 0
    return pl.pallas_call(
        functools.partial(near_kernel, first, len(after)),
        grid_spec=pltpu.PrefetchScalarGridSpec(
            num_scalar_prefetch=1,
            grid=(steps,),
            in_specs=[
                pl.BlockSpec((BLOCK, 256), lambda i, info: (jnp.maximum(info[ORDER + first + i], 0), 0)),
                whole((tok, 256)),
                whole((tok, 256)),
            ]
            + [ANY] * len(after),
            out_specs=[pl.BlockSpec((HEADS_HERE, ROWS, BLOCK), lambda i, info: (0, 0, i))]
            + [pl.BlockSpec((256, BLOCK), lambda i, info: (0, jnp.minimum(i, 1)))] * early,
            scratch_shapes=[pltpu.VMEM((HEADS_HERE, 256, BLOCK), bf16)],
        ),
        out_shape=[shaped(HEADS_HERE, ROWS, steps * BLOCK, dtype=f32)] + [shaped(256, tok // 2)] * early,
        compiler_params=params(),
        cost_estimate=cost(steps * BLOCK * 2300 * 2, 10 * 2**20),
        name="near",
    )(info, q, k, v, *after)


def mid_kernel(causal, flag_at, info_ref, q_ref, *refs):
    kv_refs, (out_ref, qt, vt) = refs[:2], refs[-3:]
    others = info_ref[flag_at] == 1
    for h in range(HEADS_HERE):
        qt[h] = transposed_queries(q_ref[:, h * HD : (h + 1) * HD])
    out_ref[...] = jnp.zeros(out_ref.shape, f32)

    def keys(n, h):
        return kv_refs[n].at[:, h * HD : (h + 1) * HD]

    def values(n):
        for h in range(HEADS_HERE):
            vt[n, h] = with_ones(kv_refs[n][:, (2 + h) * HD : (3 + h) * HD])

    if causal:
        values(0)
        for h in range(HEADS_HERE):
            diagonal(out_ref, h, keys(0, h)[...], vt[0, h], qt)

    @pl.when(others)
    def _():
        for n in range(1 if causal else 0, len(kv_refs)):
            values(n)
            for h in range(HEADS_HERE):
                p = jnp.exp2(scores(keys(n, h)[...], qt[h])).astype(bf16)
                out_ref[h] += dot(vt[n, h], p)

    total = jnp.concatenate([out_ref[h, LSUM : LSUM + 1] for h in range(HEADS_HERE)], axis=0)
    ok = within_range(total)
    for h in range(HEADS_HERE):
        out_ref[h, HD:] = stat_rows(total[h : h + 1], None, BLOCK)

    @pl.when(jnp.logical_and(jnp.logical_not(ok), True if causal else others))
    def _():
        for h in range(HEADS_HERE):
            query_pos = lane_positions(0, BLOCK)
            peak = jnp.full((1, BLOCK), FILL, f32)
            acc = jnp.zeros((ROWS, BLOCK), f32)
            for n in range(len(kv_refs)):
                own = causal and n == 0
                key_first = 0 if own else jnp.where(others, -BLOCK, BLOCK)

                def step(j, carry):
                    peak, acc = carry
                    first = aligned(j * TILE, TILE)
                    allowed = position_mask(key_first + first, query_pos, TILE)
                    s = jnp.where(allowed, scores(keys(n, h)[pl.ds(first, TILE), :], qt[h]), FILL)
                    new = jnp.maximum(peak, jnp.max(s, axis=0, keepdims=True))
                    p = jnp.where(allowed, jnp.exp2(s - new), 0.0)
                    vt_tile = with_ones(kv_refs[n][pl.ds(first, TILE), (2 + h) * HD : (3 + h) * HD])
                    return new, acc * jnp.exp2(peak - new) + dot(vt_tile, p.astype(bf16))

                peak, acc = lax.fori_loop(0, BLOCK // TILE, step, (peak, acc))
            store_partial(out_ref, h, acc, acc[LSUM : LSUM + 1], peak)


def mid(causal, flag_at, info, q, kvs, after):
    return pl.pallas_call(
        functools.partial(mid_kernel, causal, flag_at),
        grid=(1,),
        in_specs=[SMEM, whole((MID, 256))] + [whole((MID, 512))] * len(kvs) + [ANY] * len(after),
        out_specs=whole((HEADS_HERE, ROWS, BLOCK)),
        out_shape=shaped(HEADS_HERE, ROWS, BLOCK, dtype=f32),
        scratch_shapes=[
            pltpu.VMEM((HEADS_HERE, 256, BLOCK), bf16),
            pltpu.VMEM((len(kvs), HEADS_HERE, ROWS, BLOCK), bf16),
        ],
        compiler_params=params(),
        cost_estimate=cost(2 * BLOCK * BLOCK * 1.8, 5 * 2**20),
        name="mid",
    )(info, q, *kvs, *after)


def pool_level(rows, pos_at, info_ref, q_refs, kv, qt, vt, out_refs):
    q_count = len(q_refs)
    block_rows = q_refs[0].shape[0]
    count = q_count * block_rows
    total_keys = kv.shape[0]
    chunk = min(total_keys, 1024)
    query_pos = jnp.concatenate([lane_positions(info_ref[pos_at + n], block_rows) for n in range(q_count)], axis=1)
    counted = query_pos >= 0
    key_iota = lax.broadcasted_iota(jnp.int32, (rows, 1), 0)
    key_pos = jnp.concatenate(
        [info_ref[pos_at + q_count + n] + key_iota for n in range(total_keys // rows)], axis=0
    )
    for h in range(HEADS_HERE):
        q = jnp.concatenate([q_ref[:, h * HD : (h + 1) * HD] for q_ref in q_refs], axis=0)
        qt[h] = transposed_queries(q)
        vt[h] = with_ones(kv[:, (2 + h) * HD : (3 + h) * HD])

    def store(h, acc, total, peak):
        for n in range(q_count):
            cols = slice(n * block_rows, (n + 1) * block_rows)
            peak_here = None if peak is None else peak[:, cols]
            if n == 0:
                store_partial(out_refs[n], h, acc[:, cols], total[:, cols], peak_here)
            else:
                out_refs[n][h] = split_rows(acc[:HD, cols], total[:, cols], peak_here)

    def keys(h, first, size):
        return kv[first : first + size, h * HD : (h + 1) * HD]

    totals = []
    for h in range(HEADS_HERE):
        acc = jnp.zeros((ROWS, count), f32)
        for first in range(0, total_keys, chunk):
            s = scores(keys(h, first, chunk), qt[h])
            allowed = key_pos[first : first + chunk] <= query_pos
            p = jnp.where(allowed, jnp.exp2(s), 0.0).astype(bf16)
            acc = acc + dot(vt[h, :, first : first + chunk], p)
        total = acc[LSUM : LSUM + 1]
        totals.append(jnp.where(counted, total, 1.0))
        store(h, acc, total, None)

    @pl.when(jnp.logical_not(within_range(jnp.concatenate(totals, axis=0))))
    def _():
        for h in range(HEADS_HERE):
            peak = jnp.full((1, count), FILL, f32)
            acc = jnp.zeros((ROWS, count), f32)
            for first in range(0, total_keys, TILE):
                allowed = key_pos[first : first + TILE] <= query_pos
                s = jnp.where(allowed, scores(keys(h, first, TILE), qt[h]), FILL)
                new = jnp.maximum(peak, jnp.max(s, axis=0, keepdims=True))
                p = jnp.where(allowed, jnp.exp2(s - new), 0.0).astype(bf16)
                acc = acc * jnp.exp2(peak - new) + dot(vt[h, :, first : first + TILE], p)
                peak = new
            store(h, acc, acc[LSUM : LSUM + 1], peak)


def level_kernel(rows, q_row, pos_at, places, q_count, source_count, through, info_ref, *refs):
    *refs, kv, qt, vt, sems = refs
    refs = refs[: len(refs) - through]
    q_refs = [q.at[q_row : q_row + rows] for q in refs[:q_count]]
    sources, out_refs = refs[q_count : q_count + source_count], refs[-q_count:]
    copies = []
    place = 0
    for n, (source, row, count) in enumerate(places):
        dst = kv.at[place : place + count]
        copies.append(pltpu.make_async_copy(sources[source].at[row : row + count], dst, sems.at[n]))
        place += count
    for copy in copies:
        copy.start()
    for copy in copies:
        copy.wait()
    pool_level(rows, pos_at, info_ref, q_refs, kv, qt, vt, out_refs)


def level(name, rows, q_row, pos_at, places, info, qs, sources, after, through=()):
    keys = sum(count for _, _, count in places)
    count = len(qs) * rows
    return pl.pallas_call(
        functools.partial(level_kernel, rows, q_row, pos_at, tuple(places), len(qs), len(sources), len(through)),
        in_specs=[SMEM] + vmem(len(qs)) + [ANY] * (len(sources) + len(after) + len(through)),
        out_specs=vmem(len(qs)) + [ANY] * len(through),
        out_shape=[shaped(HEADS_HERE, ROWS, rows, dtype=bf16 if n else f32) for n in range(len(qs))]
        + [shaped(*x.shape) for x in through],
        input_output_aliases={1 + len(qs) + len(sources) + len(after) + n: len(qs) + n for n in range(len(through))},
        scratch_shapes=[
            pltpu.VMEM((keys, 512), bf16),
            pltpu.VMEM((HEADS_HERE, 256, count), bf16),
            pltpu.VMEM((HEADS_HERE, ROWS, keys), bf16),
            pltpu.SemaphoreType.DMA((len(places),)),
        ],
        compiler_params=params(),
        cost_estimate=cost(2 * count * keys, 4 * 2**20),
        name=name,
    )(info, *qs, *sources, *after, *through)


def exponent_of(x):
    m = x[MROW : MROW + 1] + x[MROW + 1 : MROW + 2] + x[MROW + 2 : MROW + 3]
    return jnp.where(x[LSUM : LSUM + 1] > 0.0, m, FILL)


def combined(parts):
    peaks = [exponent_of(x) for x in parts]
    peak = functools.reduce(jnp.maximum, peaks)
    out = sum(x[: LSUM + 1] * jnp.exp2(m - peak) for x, m in zip(parts, peaks))
    return out, peak


def split_rows(sums, total, peak):
    rows = pieces(total) + (pieces(peak) if peak is not None else ())
    row = lax.broadcasted_iota(jnp.int32, (ROWS - HD, total.shape[1]), 0)
    stats = jnp.zeros((ROWS - HD, total.shape[1]), f32)
    for n, r in enumerate(rows):
        stats = jnp.where(row == n, r, stats)
    return jnp.concatenate([sums, stats], axis=0).astype(bf16)


def wider(x, count):
    return x if x.shape[1] == count else jnp.concatenate([x, jnp.zeros((x.shape[0], count - x.shape[1]), x.dtype)], axis=1)


def one_hot(targets, count):
    parts = []
    for rows, rate, first, *offset in targets:
        width = count if first is not None else TILE
        at = lax.broadcasted_iota(jnp.int32, (1, width), 1) - (offset[0] if first is None else first)
        row_of = jnp.where(at & (rate - 1) == 0, at >> (rate.bit_length() - 1), -1)
        here = rows if first is not None else TILE // rate
        row = lax.broadcasted_iota(jnp.int32, (here, width), 0)
        part = jnp.where(row == row_of, 1.0, 0.0).astype(bf16)
        if first is None:
            groups = []
            for g in range(count // TILE):
                above, below = g * here, rows - (g + 1) * here
                column = [jnp.zeros((above, TILE), bf16)] * (above > 0) + [part] + [jnp.zeros((below, TILE), bf16)] * (below > 0)
                groups.append(jnp.concatenate(column, axis=0))
            part = jnp.concatenate(groups, axis=1)
        parts.append(part)
    return jnp.concatenate(parts, axis=0)


def whole_form(x):
    x = x.astype(f32)
    total = x[LSUM : LSUM + 1] + x[LSUM + 1 : LSUM + 2] + x[LSUM + 2 : LSUM + 3]
    return jnp.concatenate([x[:HD], total, x[LSUM + 3 : LSUM + 6], x[LSUM + 6 :], x[LSUM + 6 : LSUM + 8]], axis=0)


def largest_exponent(parts, places):
    seen = []
    for x, place in zip(parts, places):
        for h in range(HEADS_HERE):
            row = jnp.abs(x[h, place : place + 1].astype(f32))
            width = min(row.shape[1], 128)
            for first in range(0, row.shape[1], width):
                seen.append(wider(row[:, first : first + width], 128))
    return jnp.max(functools.reduce(jnp.maximum, seen))


def merge_kernel(for_other, info_ref, near_ref, *refs):
    near_2, *refs = (None, *refs) if for_other else refs
    mid_a, mid_b, wide_a, wide_b, far_a, far_b, out_ref, first_ref = refs
    step = pl.program_id(0)
    half = info_ref[HALF_OTHER if for_other else HALF]
    start = (2 * half + step) * BLOCK
    if for_other:
        first_ref = near_ref
    else:
        in_first = jnp.logical_and(half == 1, step == 1)

        @pl.when(in_first)
        def _():
            first_ref[...] = near_ref[...]

        @pl.when(jnp.logical_not(in_first))
        def _():
            first_ref[...] = near_2[...]

    local, sent = [first_ref, mid_a, mid_b, wide_a, far_a], [wide_b, far_b]
    largest = largest_exponent(local + sent, [MROW] * len(local) + [LSUM + 3] * len(sent))

    def take_of(h):
        offs = [info_ref[OFFS + level * HEADS_HERE + h] for level in range(3)]
        return one_hot(
            (
                (256, RATES[0], None, offs[0]),
                (128, RATES[1], offs[1] + half * 2 * BLOCK - start),
                (128, RATES[2], offs[2] - start),
            ),
            BLOCK,
        )

    def finish(h, take, rows):
        where = slice(h * HD, (h + 1) * HD)
        if not for_other:
            out_ref[where] = rows
            return
        picked = lax.dot_general(rows, take, (((1,), (1,)), ((), ())), preferred_element_type=f32).astype(bf16)
        out_ref[where, pl.ds(aligned(step * 256, 256), 256)] = picked[:, :256]
        out_ref[where, 512:] = jnp.where(step == 0, picked[:, 256:], out_ref[where, 512:] + picked[:, 256:])

    @pl.when(largest == 0.0)
    def _():
        for h in range(HEADS_HERE):
            take = take_of(h)
            far = far_a[h] + whole_form(far_b[h])
            groups = [mid_a[h] + mid_b[h], wide_a[h] + whole_form(wide_b[h]), wider(far, 128)]
            x = jnp.concatenate([split_rows(g[:HD], g[LSUM : LSUM + 1], None) for g in groups], axis=1)
            y = dot(x, take)
            total = first_ref[h, LSUM : LSUM + 1] + y[HD : HD + 1] + y[HD + 1 : HD + 2] + y[HD + 2 : HD + 3]
            finish(h, take, ((first_ref[h, :HD] + y[:HD]) * (1.0 / total)).astype(bf16))

    @pl.when(largest != 0.0)
    def _():
        for h in range(HEADS_HERE):
            take = take_of(h)
            first = first_ref[h]
            spread = []
            peak = exponent_of(first)
            row = 0
            for level in ((mid_a, mid_b), (wide_a, wide_b), (far_a, far_b)):
                x, x_peak = combined([whole_form(x[h]) if x.dtype == bf16 else x[h] for x in level])
                count = max(x.shape[1], 128)
                split = wider(split_rows(x[:HD], x[LSUM : LSUM + 1], x_peak), count)
                y = dot(split, take[row : row + count])
                row += count
                total = y[128:129] + y[129:130] + y[130:131]
                y_peak = jnp.where(total > 0.0, y[131:132] + y[132:133] + y[133:134], FILL)
                spread.append((y, total, y_peak))
                peak = jnp.maximum(peak, y_peak)
            scale = jnp.exp2(exponent_of(first) - peak)
            acc = first[:HD] * scale
            total = first[LSUM : LSUM + 1] * scale
            for y, y_total, y_peak in spread:
                scale = jnp.exp2(y_peak - peak)
                acc = acc + y[:HD] * scale
                total = total + y_total * scale
            finish(h, take, (acc / total).astype(bf16))


def merge(for_other, info, nears, mids, wides, fars):
    place_of = HALF_OTHER if for_other else HALF
    near_block_shape = (HEADS_HERE, ROWS, BLOCK)
    if for_other:
        near_specs = [pl.BlockSpec(near_block_shape, lambda i, info: (0, 0, i))]
    else:
        near_specs = [
            pl.BlockSpec(near_block_shape, lambda i, info: (0, 0, 2)),
            pl.BlockSpec(near_block_shape, lambda i, info: (0, 0, i)),
        ]
    return pl.pallas_call(
        functools.partial(merge_kernel, for_other),
        grid_spec=pltpu.PrefetchScalarGridSpec(
            num_scalar_prefetch=1,
            grid=(2,),
            in_specs=[
                *near_specs,
                *[pl.BlockSpec((HEADS_HERE, ROWS, 256), lambda i, info: (0, 0, 2 * info[place_of] + i))] * 2,
                *[pl.BlockSpec((HEADS_HERE, ROWS, 128), lambda i, info: (0, 0, info[place_of]))] * 2,
                *[whole((HEADS_HERE, ROWS, FAR))] * 2,
            ],
            out_specs=whole((256, LATE)) if for_other else pl.BlockSpec((256, BLOCK), lambda i, info: (0, i)),
            scratch_shapes=[
                pltpu.VMEM((HEADS_HERE, ROWS, 128 if for_other else BLOCK), f32),
            ],
        ),
        out_shape=shaped(256, LATE if for_other else 2 * BLOCK),
        compiler_params=params(),
        cost_estimate=cost(2 * 2 * BLOCK * 256, 6 * 2**20),
        name="merge",
    )(info, *nears, *mids, *wides, *fars)


def project_kernel(info_ref, own_ref, early_ref, late_ref, w_own, w_part, w_rest, out_ref):
    tile = own_ref.shape[1]
    step = pl.program_id(0)
    half = info_ref[HALF]
    parts = [own_ref[...]]
    col = lane_positions(0, tile)
    for h in (info_ref[CORE], 1 - info_ref[CORE]):
        rows = pl.ds(aligned(h * HD, HD), HD)
        mid_off, wide_off, far_off = (info_ref[OFFS_OTHER + level * HEADS_HERE + h] for level in range(3))
        in_mid = wide_off % RATES[0] == mid_off
        far_done = jnp.logical_or(far_off % RATES[0] == mid_off, far_off % RATES[1] == wide_off)
        nowhere = -(1 << 20)
        start = step * tile
        take = one_hot(
            (
                (tile // RATES[0], RATES[0], None, mid_off),
                (128, RATES[1], jnp.where(in_mid, nowhere, wide_off - start)),
                (128, RATES[2], jnp.where(far_done, nowhere, far_off - half * 2 * BLOCK - start)),
            ),
            tile,
        )
        near_rows = late_ref[rows, pl.ds(aligned(step * (tile // RATES[0]), tile // RATES[0]), tile // RATES[0])]
        late = dot(jnp.concatenate([near_rows, late_ref[rows, 512:]], axis=1), take)
        reached = (col % RATES[0] == mid_off) | (col % RATES[1] == wide_off) | (col % RATES[2] == far_off)
        parts.append(jnp.where(reached, late, early_ref[rows].astype(f32)).astype(bf16))
    w = jnp.concatenate([w_own[...], w_part[...], w_rest[...]], axis=0)
    out_ref[...] = dot(jnp.concatenate(parts, axis=0).T, w).astype(bf16)


def project(info, own, early, late, w_own, w_part, w_rest):
    rows, width = own.shape[1], w_own.shape[1]
    tile = 512
    return pl.pallas_call(
        project_kernel,
        grid=(rows // tile,),
        in_specs=[
            SMEM,
            pl.BlockSpec((256, tile), lambda i: (0, i)),
            pl.BlockSpec((256, tile), lambda i: (0, i)),
            whole((256, LATE)),
            whole((256, width)),
            whole((HD, width)),
            whole((HD, width)),
        ],
        out_specs=pl.BlockSpec((tile, width), lambda i: (i, 0)),
        out_shape=shaped(rows, width),
        compiler_params=params(),
        cost_estimate=pl.CostEstimate(flops=2 * rows * 512 * width, bytes_accessed=12 * 2**20, transcendentals=0),
        name="project",
    )(info, own, early, late, w_own, w_part, w_rest)


def place(s):
    return s >> 4, s >> 3 & 1, s >> 1 & 3, s & 1


def index(z, xh, y, core):
    return ((z * 2 + xh) * 4 + y) * 2 + core


def send(x, to):
    pairs = []
    for s in range(64):
        target = to(*place(s))
        if target is not None:
            pairs.append((s, index(*target)))
    return lax.ppermute(x, "seq", pairs)


def other_core(x):
    return send(x, lambda z, xh, y, c: (z, xh, y, 1 - c))


def y_step(x, by):
    return send(x, lambda z, xh, y, c: (z, xh, (y + by) % 4, c))


def later_z(x, by):
    return send(x, lambda z, xh, y, c: (z + by, xh, y, c) if z + by < 4 else None)


def ints(*values):
    return jnp.stack([jnp.asarray(v, jnp.int32) for v in values])


def swap_heads(x):
    return lax.ppermute(x, "head", [(0, 1), (1, 0)])


def scalars(offsets):
    head = lax.axis_index("head")
    z, xh, y, core = place(lax.axis_index("seq"))
    other = 1 - head
    flat = offsets.astype(jnp.int32)

    def offs(group):
        return lax.dynamic_slice_in_dim(flat, group * HEADS_HERE, HEADS_HERE, 1).reshape(-1)

    ys = [y, (y + 3) % 4, (y + 1) % 4, (y + 2) % 4]
    everything, nothing = 1 << 20, -(1 << 20)
    wide_pos = [
        (y * 2 + core) * WIDE,
        jnp.where(xh == 0, everything, nothing),
        *[(p * 2 + c) * WIDE for c in (core, 1 - core) for p in ys],
    ]
    far_pos = [
        ((z * 2 + xh) * 8 + y * 2 + core) * FAR,
        jnp.where((z == 0) & (xh == 1), nothing, ((z * 2 + 1 - xh) * 8 + y * 2 + core) * FAR),
    ]
    for cores, back in ((core, 0), (1 - core, 0), (core, 1), (core, 2), (core, 3), (1 - core, 1), (1 - core, 2), (1 - core, 3)):
        for p in ys:
            here = (((z - back) * 2 + xh) * 8 + p * 2 + cores) * FAR
            far_pos.append(jnp.where(z >= back, here, 2 * everything))
    order = [2 * other, 2 * other + 1, jnp.where(head == 1, 3, -1), 2 * head, jnp.where(head == 1, -1, 1)]
    rest = order + [head, other, core, y % 2] + wide_pos + far_pos
    return jnp.concatenate([offs(head), offs(other), ints(*rest)])


def per_device(queries, keys, values, offsets, out_weight):
    info = scalars(offsets)
    kv_mid, few, kv_mid_again = select_kv(info, keys, values)
    below = y_step(few, 1)
    above = y_step(few, -1)
    across = y_step(few, 2)
    kv_mid_core = send(kv_mid, lambda z, xh, y, c: (z, xh, y, 1) if c == 0 else None)
    q_mid, q_few, weight_rows = select_q(info, queries, out_weight)
    q_few_in = send(q_few, lambda z, xh, y, c: (z, 1 - xh, y, c))

    weight_part = swap_heads(weight_rows)
    near_1, early_other = near(0, 3, info, queries, keys, values, [kv_mid_core, q_few_in])
    packed, far_here, kv_mid_later = pack([few, below, above, across], kv_mid_again, [near_1, weight_part])
    packed_core = other_core(packed)
    kv_mid_below = send(kv_mid_later, lambda z, xh, y, c: (z, xh, y + 1, c) if y % 2 == 0 else None)
    far_z = [later_z(far_here, d) for d in (1, 2, 3)]
    early = swap_heads(early_other)
    mid_a = mid(True, CORE, info, q_mid, [kv_mid, kv_mid_core], [packed])
    wide_places = [(n, b * FEW, WIDE) for n in (0, 1) for b in range(4)]
    wide, wide_out = level("wide", WIDE, 0, WIDE_POS, wide_places, info, [q_few, q_few_in], [packed, packed_core], [mid_a])
    wide_back = send(wide_out, lambda z, xh, y, c: (z, 1, y, c) if xh == 0 else None)
    kv_mid_below_core = other_core(kv_mid_below)
    far_z_core = other_core(jnp.concatenate(far_z, axis=0))
    far_places = [(n, b * FEW + WIDE, FAR) for n in (0, 1) for b in range(4)]
    far_places += [(n, 0, 4 * FAR) for n in (2, 3, 4)] + [(5, 0, 12 * FAR)]
    far_sources = [packed, packed_core, *far_z, far_z_core]
    far, far_out, weight_part = level("far", FAR, WIDE, FAR_POS, far_places, info, [q_few, q_few_in], far_sources, [wide], [weight_part])
    weight_rest = other_core(weight_part)
    far_back = send(far_out, lambda z, xh, y, c: (z, 1 - xh, y, c))
    mid_b = mid(False, Y_ODD, info, q_mid, [kv_mid_below, kv_mid_below_core], [far, early])

    parts = ((mid_a, mid_b), (wide, wide_back), (far, far_back))
    late_rows = merge(True, info, [near_1], *parts)
    late = swap_heads(late_rows)
    (near_2,) = near(3, 2, info, queries, keys, values, [late_rows])
    attended_own = merge(False, info, [near_1, near_2], *parts)
    return project(info, attended_own, early, late, out_weight, weight_part, weight_rest)


def solution(mesh):
    return jax.shard_map(
        per_device,
        mesh=mesh,
        in_specs=(P("seq", "head"), P("seq", "head"), P("seq", "head"), P(), P("head", None)),
        out_specs=P(("seq", "head"), None),
        check_vma=False,
    )
```

```python
import functools
import math

import jax
import jax.numpy as jnp
from jax import lax
from jax.experimental import pallas as pl
from jax.experimental.pallas import tpu as pltpu
from jax.sharding import PartitionSpec as P

HD = 128
HEADS_HERE = 2
RATES = (4, 16, 64)
BLOCK = 1024
TILE = 256
ROWS = 144
LSUM = 128
MROW = 129
LOG2_SCALE = math.log2(math.e) / math.sqrt(HD)
FILL = -1e30
SMALL, LARGE = 2.0**-60, 2.0**100
VMEM_BYTES = 12 * 2**20
MID, WIDE, FAR = 1024, 256, 64
FEW = WIDE + FAR
LATE = MID // 2 + WIDE // 2 + 2 * FAR
OFFS, OFFS_OTHER, ORDER, HALF, HALF_OTHER, CORE, Y_ODD, WIDE_POS, FAR_POS = 0, 6, 12, 17, 18, 19, 20, 21, 31

f32, bf16 = jnp.float32, jnp.bfloat16


def dot(a, b):
    return jnp.dot(a, b, preferred_element_type=f32)


def aligned(x, n):
    return x if isinstance(x, int) else pl.multiple_of(x, n)


def transposed_queries(q):
    q = q.astype(f32) * LOG2_SCALE
    high = q.astype(bf16)
    low = (q - high.astype(f32)).astype(bf16)
    return jnp.concatenate([high, low], axis=1).T


def scores(k, qt):
    return dot(jnp.concatenate([k, k], axis=1), qt)


def with_ones(v):
    return jnp.concatenate([v.T, jnp.ones((ROWS - HD, v.shape[0]), v.dtype)], axis=0)


def pieces(x):
    first = x.astype(bf16).astype(f32)
    second = (x - first).astype(bf16).astype(f32)
    return first, second, x - first - second


def stat_rows(total, exponent, count):
    row = lax.broadcasted_iota(jnp.int32, (ROWS - HD, count), 0)
    parts = (total,) + (pieces(exponent) if exponent is not None else ())
    out = jnp.zeros((ROWS - HD, count), f32)
    for n, part in enumerate(parts):
        out = jnp.where(row == n, part, out)
    return out


def within_range(total, counted=None):
    ok = (total >= SMALL) & (total <= LARGE)
    if counted is not None:
        ok = ok | ~counted
    return jnp.min(jnp.where(ok, 1.0, 0.0)) > 0.5


def rescaled(store, get_queries, count, blocks, block):
    def step(j, carry):
        peak, acc = carry
        k, vt, allowed = block(j)
        s = jnp.where(allowed, scores(k, get_queries()), FILL)
        new = jnp.maximum(peak, jnp.max(s, axis=0, keepdims=True))
        p = jnp.where(allowed, jnp.exp2(s - new), 0.0)
        return new, acc * jnp.exp2(peak - new) + dot(vt, p.astype(bf16))

    peak, acc = lax.fori_loop(
        0, blocks, step, (jnp.full((1, count), FILL, f32), jnp.zeros((ROWS, count), f32))
    )
    store(acc, acc[LSUM : LSUM + 1], peak)


def position_mask(key_first, query_pos, rows):
    key_pos = key_first + lax.broadcasted_iota(jnp.int32, (rows, query_pos.shape[1]), 0)
    return key_pos <= query_pos


def lane_positions(first, count):
    return first + lax.broadcasted_iota(jnp.int32, (1, count), 1)


def pick(x_ref, cols, scr, off_ref, outs):
    scr[...] = x_ref[:, cols].astype(f32)
    step = pl.program_id(0)
    for level, (out_ref, row, out_cols) in enumerate(outs):
        count = scr.shape[0] // RATES[level]
        picked = scr[pl.ds(off_ref[OFFS + level * HEADS_HERE + scr_head(cols)], count, stride=RATES[level]), :]
        first = pl.multiple_of(row + step * count, 16)
        out_ref[pl.ds(first, count), out_cols] = picked.astype(bf16)


def scr_head(cols):
    return cols.start // HD


def select_kv_kernel(info_ref, k_ref, v_ref, mid_ref, few_ref, again_ref, scr):
    for h in range(HEADS_HERE):
        cols = slice(h * HD, (h + 1) * HD)
        for n, x_ref in enumerate((k_ref, v_ref)):
            out_cols = slice((2 * n + h) * HD, (2 * n + h + 1) * HD)
            pick(x_ref, cols, scr.at[n, h], info_ref, ((mid_ref, 0, out_cols), (few_ref, 0, out_cols), (few_ref, WIDE, out_cols)))

    @pl.when(pl.program_id(0) == pl.num_programs(0) - 1)
    def _():
        again_ref[...] = mid_ref[...]


def select_q_kernel(info_ref, q_ref, w_ref, qm_ref, few_ref, part_ref, scr, sem):
    copy = pltpu.make_async_copy(w_ref.at[pl.ds(aligned(info_ref[CORE] * HD, HD), HD)], part_ref, sem)
    pl.when(pl.program_id(0) == 0)(copy.start)
    pl.when(pl.program_id(0) == pl.num_programs(0) - 1)(copy.wait)
    for h in range(HEADS_HERE):
        cols = slice(h * HD, (h + 1) * HD)
        pick(q_ref, cols, scr.at[h], info_ref, ((qm_ref, 0, cols), (few_ref, 0, cols), (few_ref, WIDE, cols)))


def vmem(count):
    return [pl.BlockSpec(memory_space=pltpu.VMEM)] * count


SMEM = pl.BlockSpec(memory_space=pltpu.SMEM)
ANY = pl.BlockSpec(memory_space=pl.ANY)


def whole(shape):
    return pl.BlockSpec(shape, lambda *_: (0,) * len(shape), pipeline_mode=pl.Buffered(1))


def params():
    return pltpu.CompilerParams(vmem_limit_bytes=VMEM_BYTES)


def cost(pairs, bytes_accessed):
    return pl.CostEstimate(
        flops=int(pairs * 1024 * 1.5), bytes_accessed=int(bytes_accessed), transcendentals=int(pairs)
    )


def shaped(*shape, dtype=bf16):
    return jax.ShapeDtypeStruct(shape, dtype)


def select_kv(info, k, v):
    chunk = pl.BlockSpec((BLOCK, 256), lambda i: (i, 0))
    return pl.pallas_call(
        select_kv_kernel,
        grid=(k.shape[0] // BLOCK,),
        in_specs=[SMEM, chunk, chunk],
        out_specs=[whole((MID, 512)), whole((FEW, 512)), whole((MID, 512))],
        out_shape=[shaped(MID, 512), shaped(FEW, 512), shaped(MID, 512)],
        scratch_shapes=[pltpu.VMEM((2, HEADS_HERE, BLOCK, HD), f32)],
        compiler_params=params(),
        name="select_kv",
    )(info, k, v)


def select_q(info, q, w):
    return pl.pallas_call(
        select_q_kernel,
        grid=(q.shape[0] // BLOCK,),
        in_specs=[SMEM, pl.BlockSpec((BLOCK, 256), lambda i: (i, 0)), ANY],
        out_specs=[whole((MID, 256)), whole((FEW, 256)), whole((HD, w.shape[1]))],
        out_shape=[shaped(MID, 256), shaped(FEW, 256), shaped(HD, w.shape[1])],
        scratch_shapes=[pltpu.VMEM((HEADS_HERE, BLOCK, HD), f32), pltpu.SemaphoreType.DMA],
        compiler_params=params(),
        name="select_q",
    )(info, q, w)


def pack_kernel(count, *refs):
    *_, all_ref, far_ref = refs
    for n, x_ref in enumerate(refs[:count]):
        all_ref[n * FEW : (n + 1) * FEW] = x_ref[...]
        far_ref[n * FAR : (n + 1) * FAR] = x_ref[WIDE:]


def pack(few, after):
    count = len(few)
    return pl.pallas_call(
        functools.partial(pack_kernel, count),
        in_specs=vmem(count) + [ANY] * len(after),
        out_specs=vmem(2),
        out_shape=[shaped(count * FEW, 512), shaped(count * FAR, 512)],
        compiler_params=params(),
        cost_estimate=pl.CostEstimate(flops=0, bytes_accessed=4 * 2**20, transcendentals=0),
        name="pack",
    )(*few, *after)


def hand_on_kernel(*refs):
    pass


def hand_on(x, after):
    return pl.pallas_call(
        hand_on_kernel,
        in_specs=[ANY, ANY],
        out_specs=ANY,
        out_shape=shaped(*x.shape),
        input_output_aliases={0: 0},
        compiler_params=pltpu.CompilerParams(vmem_limit_bytes=2**20),
        cost_estimate=pl.CostEstimate(flops=0, bytes_accessed=0, transcendentals=0),
        name="hand_on",
    )(x, after)


def diagonal(out_ref, h, k, vt, qt_ref):
    row = lax.broadcasted_iota(jnp.int32, (TILE, TILE), 0)
    col = lax.broadcasted_iota(jnp.int32, (TILE, TILE), 1)
    rows = []
    for g in range(BLOCK // TILE):
        first = g * TILE
        p = jnp.exp2(scores(k[first : first + TILE], qt_ref[h, :, first:]))
        parts = [jnp.where(row <= col, p[:, :TILE], 0.0), p[:, TILE:]]
        if g:
            parts = [jnp.zeros((TILE, first), f32)] + parts
        rows.append(jnp.concatenate([x for x in parts if x.shape[1]], axis=1).astype(bf16))
    out_ref[h] += dot(vt, jnp.concatenate(rows, axis=0))


def store_partial(out_ref, h, acc, total, exponent):
    count = acc.shape[1]
    out_ref[h, :HD] = acc[:HD]
    out_ref[h, HD:] = stat_rows(total, exponent, count)


def near_kernel(first, skipped, info_ref, q_ref, k_ref, v_ref, *refs):
    refs = refs[skipped:]
    block = info_ref[ORDER + first + pl.program_id(0)]

    @pl.when(block >= 0)
    def _():
        near_block(first, block, q_ref, k_ref, v_ref, *refs)


def near_block(first, block, q_ref, k_ref, v_ref, *refs):
    out_ref, *early_ref, qt = refs

    def values_at(start, rows, h):
        return with_ones(v_ref[pl.ds(start, rows), h * HD : (h + 1) * HD])

    for h in range(HEADS_HERE):
        qt[h] = transposed_queries(q_ref[:, h * HD : (h + 1) * HD])
    out_ref[...] = jnp.zeros(out_ref.shape, f32)

    def full(j, carry):
        start = aligned(j * BLOCK, BLOCK)
        for h in range(HEADS_HERE):
            s = scores(k_ref[pl.ds(start, BLOCK), h * HD : (h + 1) * HD], qt[h])
            out_ref[h] += dot(values_at(start, BLOCK, h), jnp.exp2(s).astype(bf16))
        return carry

    lax.fori_loop(0, block, full, 0)
    start = aligned(block * BLOCK, BLOCK)
    for h in range(HEADS_HERE):
        cols = slice(h * HD, (h + 1) * HD)
        diagonal(out_ref, h, k_ref[pl.ds(start, BLOCK), cols], values_at(start, BLOCK, h), qt)
    total = jnp.concatenate([out_ref[h, LSUM : LSUM + 1] for h in range(HEADS_HERE)], axis=0)
    ok = within_range(total)
    for h in range(HEADS_HERE):
        out_ref[h, HD:] = stat_rows(total[h : h + 1], None, BLOCK)

    @pl.when(jnp.logical_not(ok))
    def _():
        for h in range(HEADS_HERE):
            cols = slice(h * HD, (h + 1) * HD)
            query_pos = lane_positions(block * BLOCK, BLOCK)

            def key_block(j):
                first = aligned(j * TILE, TILE)
                return (
                    k_ref[pl.ds(first, TILE), cols],
                    values_at(first, TILE, h),
                    position_mask(first, query_pos, TILE),
                )

            rescaled(
                functools.partial(store_partial, out_ref, h),
                lambda: qt[h],
                BLOCK,
                (block + 1) * (BLOCK // TILE),
                key_block,
            )

    if early_ref:

        @pl.when(pl.program_id(0) < 2)
        def _():
            for h in range(HEADS_HERE):
                scale = 1.0 / out_ref[h, LSUM : LSUM + 1]
                early_ref[0][h * HD : (h + 1) * HD] = (out_ref[h, :HD] * scale).astype(bf16)


def near(first, steps, info, q, k, v, after):
    tok = q.shape[0]
    early = first == 0
    return pl.pallas_call(
        functools.partial(near_kernel, first, len(after)),
        grid_spec=pltpu.PrefetchScalarGridSpec(
            num_scalar_prefetch=1,
            grid=(steps,),
            in_specs=[
                pl.BlockSpec((BLOCK, 256), lambda i, info: (jnp.maximum(info[ORDER + first + i], 0), 0)),
                whole((tok, 256)),
                whole((tok, 256)),
            ]
            + [ANY] * len(after),
            out_specs=[pl.BlockSpec((HEADS_HERE, ROWS, BLOCK), lambda i, info: (0, 0, i))]
            + [pl.BlockSpec((256, BLOCK), lambda i, info: (0, jnp.minimum(i, 1)))] * early,
            scratch_shapes=[pltpu.VMEM((HEADS_HERE, 256, BLOCK), bf16)],
        ),
        out_shape=[shaped(HEADS_HERE, ROWS, steps * BLOCK, dtype=f32)] + [shaped(256, tok // 2)] * early,
        compiler_params=params(),
        cost_estimate=cost(steps * BLOCK * 2300 * 2, 10 * 2**20),
        name="near",
    )(info, q, k, v, *after)


def mid_kernel(causal, flag_at, info_ref, q_ref, *refs):
    kv_refs, (out_ref, qt, vt) = refs[:2], refs[-3:]
    others = info_ref[flag_at] == 1
    for h in range(HEADS_HERE):
        qt[h] = transposed_queries(q_ref[:, h * HD : (h + 1) * HD])
    out_ref[...] = jnp.zeros(out_ref.shape, f32)

    def keys(n, h):
        return kv_refs[n].at[:, h * HD : (h + 1) * HD]

    def values(n):
        for h in range(HEADS_HERE):
            vt[n, h] = with_ones(kv_refs[n][:, (2 + h) * HD : (3 + h) * HD])

    if causal:
        values(0)
        for h in range(HEADS_HERE):
            diagonal(out_ref, h, keys(0, h)[...], vt[0, h], qt)

    @pl.when(others)
    def _():
        for n in range(1 if causal else 0, len(kv_refs)):
            values(n)
            for h in range(HEADS_HERE):
                p = jnp.exp2(scores(keys(n, h)[...], qt[h])).astype(bf16)
                out_ref[h] += dot(vt[n, h], p)

    total = jnp.concatenate([out_ref[h, LSUM : LSUM + 1] for h in range(HEADS_HERE)], axis=0)
    ok = within_range(total)
    for h in range(HEADS_HERE):
        out_ref[h, HD:] = stat_rows(total[h : h + 1], None, BLOCK)

    @pl.when(jnp.logical_and(jnp.logical_not(ok), True if causal else others))
    def _():
        for h in range(HEADS_HERE):
            query_pos = lane_positions(0, BLOCK)
            peak = jnp.full((1, BLOCK), FILL, f32)
            acc = jnp.zeros((ROWS, BLOCK), f32)
            for n in range(len(kv_refs)):
                own = causal and n == 0
                key_first = 0 if own else jnp.where(others, -BLOCK, BLOCK)

                def step(j, carry):
                    peak, acc = carry
                    first = aligned(j * TILE, TILE)
                    allowed = position_mask(key_first + first, query_pos, TILE)
                    s = jnp.where(allowed, scores(keys(n, h)[pl.ds(first, TILE), :], qt[h]), FILL)
                    new = jnp.maximum(peak, jnp.max(s, axis=0, keepdims=True))
                    p = jnp.where(allowed, jnp.exp2(s - new), 0.0)
                    vt_tile = with_ones(kv_refs[n][pl.ds(first, TILE), (2 + h) * HD : (3 + h) * HD])
                    return new, acc * jnp.exp2(peak - new) + dot(vt_tile, p.astype(bf16))

                peak, acc = lax.fori_loop(0, BLOCK // TILE, step, (peak, acc))
            store_partial(out_ref, h, acc, acc[LSUM : LSUM + 1], peak)


def mid(causal, flag_at, info, q, kvs, after):
    return pl.pallas_call(
        functools.partial(mid_kernel, causal, flag_at),
        grid=(1,),
        in_specs=[SMEM, whole((MID, 256))] + [whole((MID, 512))] * len(kvs) + [ANY] * len(after),
        out_specs=whole((HEADS_HERE, ROWS, BLOCK)),
        out_shape=shaped(HEADS_HERE, ROWS, BLOCK, dtype=f32),
        scratch_shapes=[
            pltpu.VMEM((HEADS_HERE, 256, BLOCK), bf16),
            pltpu.VMEM((len(kvs), HEADS_HERE, ROWS, BLOCK), bf16),
        ],
        compiler_params=params(),
        cost_estimate=cost(2 * BLOCK * BLOCK * 1.8, 5 * 2**20),
        name="mid",
    )(info, q, *kvs, *after)


def pool_level(rows, pos_at, info_ref, q_refs, kv, qt, vt, out_refs):
    q_count = len(q_refs)
    block_rows = q_refs[0].shape[0]
    count = q_count * block_rows
    total_keys = kv.shape[0]
    chunk = min(total_keys, 1024)
    query_pos = jnp.concatenate([lane_positions(info_ref[pos_at + n], block_rows) for n in range(q_count)], axis=1)
    counted = query_pos >= 0
    key_iota = lax.broadcasted_iota(jnp.int32, (rows, 1), 0)
    key_pos = jnp.concatenate(
        [info_ref[pos_at + q_count + n] + key_iota for n in range(total_keys // rows)], axis=0
    )
    for h in range(HEADS_HERE):
        q = jnp.concatenate([q_ref[:, h * HD : (h + 1) * HD] for q_ref in q_refs], axis=0)
        qt[h] = transposed_queries(q)
        vt[h] = with_ones(kv[:, (2 + h) * HD : (3 + h) * HD])

    def store(h, acc, total, peak):
        for n in range(q_count):
            cols = slice(n * block_rows, (n + 1) * block_rows)
            peak_here = None if peak is None else peak[:, cols]
            if n == 0:
                store_partial(out_refs[n], h, acc[:, cols], total[:, cols], peak_here)
            else:
                out_refs[n][h] = split_rows(acc[:HD, cols], total[:, cols], peak_here)

    def keys(h, first, size):
        return kv[first : first + size, h * HD : (h + 1) * HD]

    totals = []
    for h in range(HEADS_HERE):
        acc = jnp.zeros((ROWS, count), f32)
        for first in range(0, total_keys, chunk):
            s = scores(keys(h, first, chunk), qt[h])
            allowed = key_pos[first : first + chunk] <= query_pos
            p = jnp.where(allowed, jnp.exp2(s), 0.0).astype(bf16)
            acc = acc + dot(vt[h, :, first : first + chunk], p)
        total = acc[LSUM : LSUM + 1]
        totals.append(jnp.where(counted, total, 1.0))
        store(h, acc, total, None)

    @pl.when(jnp.logical_not(within_range(jnp.concatenate(totals, axis=0))))
    def _():
        for h in range(HEADS_HERE):
            peak = jnp.full((1, count), FILL, f32)
            acc = jnp.zeros((ROWS, count), f32)
            for first in range(0, total_keys, TILE):
                allowed = key_pos[first : first + TILE] <= query_pos
                s = jnp.where(allowed, scores(keys(h, first, TILE), qt[h]), FILL)
                new = jnp.maximum(peak, jnp.max(s, axis=0, keepdims=True))
                p = jnp.where(allowed, jnp.exp2(s - new), 0.0).astype(bf16)
                acc = acc * jnp.exp2(peak - new) + dot(vt[h, :, first : first + TILE], p)
                peak = new
            store(h, acc, acc[LSUM : LSUM + 1], peak)


def level_kernel(rows, q_row, pos_at, places, q_count, source_count, through, info_ref, *refs):
    *refs, kv, qt, vt, sems = refs
    refs = refs[: len(refs) - through]
    q_refs = [q.at[q_row : q_row + rows] for q in refs[:q_count]]
    sources, out_refs = refs[q_count : q_count + source_count], refs[-q_count:]
    copies = []
    place = 0
    for n, (source, row, count) in enumerate(places):
        dst = kv.at[place : place + count]
        copies.append(pltpu.make_async_copy(sources[source].at[row : row + count], dst, sems.at[n]))
        place += count
    for copy in copies:
        copy.start()
    for copy in copies:
        copy.wait()
    pool_level(rows, pos_at, info_ref, q_refs, kv, qt, vt, out_refs)


def level(name, rows, q_row, pos_at, places, info, qs, sources, after, through=()):
    keys = sum(count for _, _, count in places)
    count = len(qs) * rows
    return pl.pallas_call(
        functools.partial(level_kernel, rows, q_row, pos_at, tuple(places), len(qs), len(sources), len(through)),
        in_specs=[SMEM] + vmem(len(qs)) + [ANY] * (len(sources) + len(after) + len(through)),
        out_specs=vmem(len(qs)) + [ANY] * len(through),
        out_shape=[shaped(HEADS_HERE, ROWS, rows, dtype=bf16 if n else f32) for n in range(len(qs))]
        + [shaped(*x.shape) for x in through],
        input_output_aliases={1 + len(qs) + len(sources) + len(after) + n: len(qs) + n for n in range(len(through))},
        scratch_shapes=[
            pltpu.VMEM((keys, 512), bf16),
            pltpu.VMEM((HEADS_HERE, 256, count), bf16),
            pltpu.VMEM((HEADS_HERE, ROWS, keys), bf16),
            pltpu.SemaphoreType.DMA((len(places),)),
        ],
        compiler_params=params(),
        cost_estimate=cost(2 * count * keys, 4 * 2**20),
        name=name,
    )(info, *qs, *sources, *after, *through)


def exponent_of(x):
    m = x[MROW : MROW + 1] + x[MROW + 1 : MROW + 2] + x[MROW + 2 : MROW + 3]
    return jnp.where(x[LSUM : LSUM + 1] > 0.0, m, FILL)


def combined(parts):
    peaks = [exponent_of(x) for x in parts]
    peak = functools.reduce(jnp.maximum, peaks)
    out = sum(x[: LSUM + 1] * jnp.exp2(m - peak) for x, m in zip(parts, peaks))
    return out, peak


def split_rows(sums, total, peak):
    rows = pieces(total) + (pieces(peak) if peak is not None else ())
    row = lax.broadcasted_iota(jnp.int32, (ROWS - HD, total.shape[1]), 0)
    stats = jnp.zeros((ROWS - HD, total.shape[1]), f32)
    for n, r in enumerate(rows):
        stats = jnp.where(row == n, r, stats)
    return jnp.concatenate([sums, stats], axis=0).astype(bf16)


def wider(x, count):
    return x if x.shape[1] == count else jnp.concatenate([x, jnp.zeros((x.shape[0], count - x.shape[1]), x.dtype)], axis=1)


def one_hot(targets, count):
    parts = []
    for rows, rate, first, *offset in targets:
        width = count if first is not None else TILE
        at = lax.broadcasted_iota(jnp.int32, (1, width), 1) - (offset[0] if first is None else first)
        row_of = jnp.where(at & (rate - 1) == 0, at >> (rate.bit_length() - 1), -1)
        here = rows if first is not None else TILE // rate
        row = lax.broadcasted_iota(jnp.int32, (here, width), 0)
        part = jnp.where(row == row_of, 1.0, 0.0).astype(bf16)
        if first is None:
            groups = []
            for g in range(count // TILE):
                above, below = g * here, rows - (g + 1) * here
                column = [jnp.zeros((above, TILE), bf16)] * (above > 0) + [part] + [jnp.zeros((below, TILE), bf16)] * (below > 0)
                groups.append(jnp.concatenate(column, axis=0))
            part = jnp.concatenate(groups, axis=1)
        parts.append(part)
    return jnp.concatenate(parts, axis=0)


def whole_form(x):
    x = x.astype(f32)
    total = x[LSUM : LSUM + 1] + x[LSUM + 1 : LSUM + 2] + x[LSUM + 2 : LSUM + 3]
    return jnp.concatenate([x[:HD], total, x[LSUM + 3 : LSUM + 6], x[LSUM + 6 :], x[LSUM + 6 : LSUM + 8]], axis=0)


def largest_exponent(parts, places):
    seen = []
    for x, place in zip(parts, places):
        for h in range(HEADS_HERE):
            row = jnp.abs(x[h, place : place + 1].astype(f32))
            width = min(row.shape[1], 128)
            for first in range(0, row.shape[1], width):
                seen.append(wider(row[:, first : first + width], 128))
    return jnp.max(functools.reduce(jnp.maximum, seen))


def merge_kernel(for_other, info_ref, near_ref, *refs):
    near_2, *refs = (None, *refs) if for_other else refs
    mid_a, mid_b, wide_a, wide_b, far_a, far_b, out_ref, first_ref = refs
    step = pl.program_id(0)
    half = info_ref[HALF_OTHER if for_other else HALF]
    start = (2 * half + step) * BLOCK
    if for_other:
        first_ref = near_ref
    else:
        in_first = jnp.logical_and(half == 1, step == 1)

        @pl.when(in_first)
        def _():
            first_ref[...] = near_ref[...]

        @pl.when(jnp.logical_not(in_first))
        def _():
            first_ref[...] = near_2[...]

    local, sent = [first_ref, mid_a, mid_b, wide_a, far_a], [wide_b, far_b]
    largest = largest_exponent(local + sent, [MROW] * len(local) + [LSUM + 3] * len(sent))

    def take_of(h):
        offs = [info_ref[OFFS + level * HEADS_HERE + h] for level in range(3)]
        return one_hot(
            (
                (256, RATES[0], None, offs[0]),
                (128, RATES[1], offs[1] + half * 2 * BLOCK - start),
                (128, RATES[2], offs[2] - start),
            ),
            BLOCK,
        )

    def finish(h, take, rows):
        where = slice(h * HD, (h + 1) * HD)
        if not for_other:
            out_ref[where] = rows
            return
        picked = lax.dot_general(rows, take, (((1,), (1,)), ((), ())), preferred_element_type=f32).astype(bf16)
        out_ref[where, pl.ds(aligned(step * 256, 256), 256)] = picked[:, :256]
        out_ref[where, 512:] = jnp.where(step == 0, picked[:, 256:], out_ref[where, 512:] + picked[:, 256:])

    @pl.when(largest == 0.0)
    def _():
        for h in range(HEADS_HERE):
            take = take_of(h)
            far = far_a[h] + whole_form(far_b[h])
            groups = [mid_a[h] + mid_b[h], wide_a[h] + whole_form(wide_b[h]), wider(far, 128)]
            x = jnp.concatenate([split_rows(g[:HD], g[LSUM : LSUM + 1], None) for g in groups], axis=1)
            y = dot(x, take)
            total = first_ref[h, LSUM : LSUM + 1] + y[HD : HD + 1] + y[HD + 1 : HD + 2] + y[HD + 2 : HD + 3]
            finish(h, take, ((first_ref[h, :HD] + y[:HD]) * (1.0 / total)).astype(bf16))

    @pl.when(largest != 0.0)
    def _():
        for h in range(HEADS_HERE):
            take = take_of(h)
            first = first_ref[h]
            spread = []
            peak = exponent_of(first)
            row = 0
            for level in ((mid_a, mid_b), (wide_a, wide_b), (far_a, far_b)):
                x, x_peak = combined([whole_form(x[h]) if x.dtype == bf16 else x[h] for x in level])
                count = max(x.shape[1], 128)
                split = wider(split_rows(x[:HD], x[LSUM : LSUM + 1], x_peak), count)
                y = dot(split, take[row : row + count])
                row += count
                total = y[128:129] + y[129:130] + y[130:131]
                y_peak = jnp.where(total > 0.0, y[131:132] + y[132:133] + y[133:134], FILL)
                spread.append((y, total, y_peak))
                peak = jnp.maximum(peak, y_peak)
            scale = jnp.exp2(exponent_of(first) - peak)
            acc = first[:HD] * scale
            total = first[LSUM : LSUM + 1] * scale
            for y, y_total, y_peak in spread:
                scale = jnp.exp2(y_peak - peak)
                acc = acc + y[:HD] * scale
                total = total + y_total * scale
            finish(h, take, (acc / total).astype(bf16))


def merge(for_other, info, nears, mids, wides, fars):
    place_of = HALF_OTHER if for_other else HALF
    near_block_shape = (HEADS_HERE, ROWS, BLOCK)
    if for_other:
        near_specs = [pl.BlockSpec(near_block_shape, lambda i, info: (0, 0, i))]
    else:
        near_specs = [
            pl.BlockSpec(near_block_shape, lambda i, info: (0, 0, 2)),
            pl.BlockSpec(near_block_shape, lambda i, info: (0, 0, i)),
        ]
    return pl.pallas_call(
        functools.partial(merge_kernel, for_other),
        grid_spec=pltpu.PrefetchScalarGridSpec(
            num_scalar_prefetch=1,
            grid=(2,),
            in_specs=[
                *near_specs,
                *[pl.BlockSpec((HEADS_HERE, ROWS, 256), lambda i, info: (0, 0, 2 * info[place_of] + i))] * 2,
                *[pl.BlockSpec((HEADS_HERE, ROWS, 128), lambda i, info: (0, 0, info[place_of]))] * 2,
                *[whole((HEADS_HERE, ROWS, FAR))] * 2,
            ],
            out_specs=whole((256, LATE)) if for_other else pl.BlockSpec((256, BLOCK), lambda i, info: (0, i)),
            scratch_shapes=[
                pltpu.VMEM((HEADS_HERE, ROWS, 128 if for_other else BLOCK), f32),
            ],
        ),
        out_shape=shaped(256, LATE if for_other else 2 * BLOCK),
        compiler_params=params(),
        cost_estimate=cost(2 * 2 * BLOCK * 256, 6 * 2**20),
        name="merge",
    )(info, *nears, *mids, *wides, *fars)


def project_kernel(info_ref, own_ref, early_ref, late_ref, w_own, w_part, w_rest, out_ref):
    tile = own_ref.shape[1]
    step = pl.program_id(0)
    half = info_ref[HALF]
    parts = [own_ref[...]]
    col = lane_positions(0, tile)
    for h in (info_ref[CORE], 1 - info_ref[CORE]):
        rows = pl.ds(aligned(h * HD, HD), HD)
        mid_off, wide_off, far_off = (info_ref[OFFS_OTHER + level * HEADS_HERE + h] for level in range(3))
        in_mid = wide_off % RATES[0] == mid_off
        far_done = jnp.logical_or(far_off % RATES[0] == mid_off, far_off % RATES[1] == wide_off)
        nowhere = -(1 << 20)
        start = step * tile
        take = one_hot(
            (
                (tile // RATES[0], RATES[0], None, mid_off),
                (128, RATES[1], jnp.where(in_mid, nowhere, wide_off - start)),
                (128, RATES[2], jnp.where(far_done, nowhere, far_off - half * 2 * BLOCK - start)),
            ),
            tile,
        )
        near_rows = late_ref[rows, pl.ds(aligned(step * (tile // RATES[0]), tile // RATES[0]), tile // RATES[0])]
        late = dot(jnp.concatenate([near_rows, late_ref[rows, 512:]], axis=1), take)
        reached = (col % RATES[0] == mid_off) | (col % RATES[1] == wide_off) | (col % RATES[2] == far_off)
        parts.append(jnp.where(reached, late, early_ref[rows].astype(f32)).astype(bf16))
    w = jnp.concatenate([w_own[...], w_part[...], w_rest[...]], axis=0)
    out_ref[...] = dot(jnp.concatenate(parts, axis=0).T, w).astype(bf16)


def project(info, own, early, late, w_own, w_part, w_rest):
    rows, width = own.shape[1], w_own.shape[1]
    tile = 512
    return pl.pallas_call(
        project_kernel,
        grid=(rows // tile,),
        in_specs=[
            SMEM,
            pl.BlockSpec((256, tile), lambda i: (0, i)),
            pl.BlockSpec((256, tile), lambda i: (0, i)),
            whole((256, LATE)),
            whole((256, width)),
            whole((HD, width)),
            whole((HD, width)),
        ],
        out_specs=pl.BlockSpec((tile, width), lambda i: (i, 0)),
        out_shape=shaped(rows, width),
        compiler_params=params(),
        cost_estimate=pl.CostEstimate(flops=2 * rows * 512 * width, bytes_accessed=12 * 2**20, transcendentals=0),
        name="project",
    )(info, own, early, late, w_own, w_part, w_rest)


def place(s):
    return s >> 4, s >> 3 & 1, s >> 1 & 3, s & 1


def index(z, xh, y, core):
    return ((z * 2 + xh) * 4 + y) * 2 + core


def send(x, to):
    pairs = []
    for s in range(64):
        target = to(*place(s))
        if target is not None:
            pairs.append((s, index(*target)))
    return lax.ppermute(x, "seq", pairs)


def other_core(x):
    return send(x, lambda z, xh, y, c: (z, xh, y, 1 - c))


def y_step(x, by):
    return send(x, lambda z, xh, y, c: (z, xh, (y + by) % 4, c))


def later_z(x, by):
    return send(x, lambda z, xh, y, c: (z + by, xh, y, c) if z + by < 4 else None)


def ints(*values):
    return jnp.stack([jnp.asarray(v, jnp.int32) for v in values])


def swap_heads(x):
    return lax.ppermute(x, "head", [(0, 1), (1, 0)])


def scalars(offsets):
    head = lax.axis_index("head")
    z, xh, y, core = place(lax.axis_index("seq"))
    other = 1 - head
    flat = offsets.astype(jnp.int32)

    def offs(group):
        return lax.dynamic_slice_in_dim(flat, group * HEADS_HERE, HEADS_HERE, 1).reshape(-1)

    ys = [y, (y + 3) % 4, (y + 1) % 4, (y + 2) % 4]
    everything, nothing = 1 << 20, -(1 << 20)
    wide_pos = [
        (y * 2 + core) * WIDE,
        jnp.where(xh == 0, everything, nothing),
        *[(p * 2 + c) * WIDE for c in (core, 1 - core) for p in ys],
    ]
    far_pos = [
        ((z * 2 + xh) * 8 + y * 2 + core) * FAR,
        jnp.where((z == 0) & (xh == 1), nothing, ((z * 2 + 1 - xh) * 8 + y * 2 + core) * FAR),
    ]
    for cores, back in ((core, 0), (1 - core, 0), (core, 1), (core, 2), (core, 3), (1 - core, 1), (1 - core, 2), (1 - core, 3)):
        for p in ys:
            here = (((z - back) * 2 + xh) * 8 + p * 2 + cores) * FAR
            far_pos.append(jnp.where(z >= back, here, 2 * everything))
    order = [2 * other, 2 * other + 1, jnp.where(head == 1, 3, -1), 2 * head, jnp.where(head == 1, -1, 1)]
    rest = order + [head, other, core, y % 2] + wide_pos + far_pos
    return jnp.concatenate([offs(head), offs(other), ints(*rest)])


def per_device(queries, keys, values, offsets, out_weight):
    info = scalars(offsets)
    kv_mid, few, kv_mid_again = select_kv(info, keys, values)
    below = y_step(few, 1)
    above = y_step(few, -1)
    across = y_step(few, 2)
    kv_mid_core = send(kv_mid, lambda z, xh, y, c: (z, xh, y, 1) if c == 0 else None)
    q_mid, q_few, weight_rows = select_q(info, queries, out_weight)
    q_few_in = send(q_few, lambda z, xh, y, c: (z, 1 - xh, y, c))

    kv_mid_below = send(hand_on(kv_mid_again, q_few_in), lambda z, xh, y, c: (z, xh, y + 1, c) if y % 2 == 0 else None)
    weight_part = swap_heads(weight_rows)
    near_1, early_other = near(0, 3, info, queries, keys, values, [kv_mid_core, q_few_in])
    packed, far_here = pack([few, below, above, across], [near_1, weight_part])
    packed_core = other_core(packed)
    far_z = [later_z(far_here, d) for d in (1, 2, 3)]
    early = swap_heads(early_other)
    mid_a = mid(True, CORE, info, q_mid, [kv_mid, kv_mid_core], [packed])
    wide_places = [(n, b * FEW, WIDE) for n in (0, 1) for b in range(4)]
    wide, wide_out = level("wide", WIDE, 0, WIDE_POS, wide_places, info, [q_few, q_few_in], [packed, packed_core], [mid_a])
    wide_back = send(wide_out, lambda z, xh, y, c: (z, 1, y, c) if xh == 0 else None)
    kv_mid_below_core = other_core(kv_mid_below)
    far_z_core = other_core(jnp.concatenate(far_z, axis=0))
    far_places = [(n, b * FEW + WIDE, FAR) for n in (0, 1) for b in range(4)]
    far_places += [(n, 0, 4 * FAR) for n in (2, 3, 4)] + [(5, 0, 12 * FAR)]
    far_sources = [packed, packed_core, *far_z, far_z_core]
    far, far_out, weight_part = level("far", FAR, WIDE, FAR_POS, far_places, info, [q_few, q_few_in], far_sources, [wide], [weight_part])
    weight_rest = other_core(weight_part)
    far_back = send(far_out, lambda z, xh, y, c: (z, 1 - xh, y, c))
    mid_b = mid(False, Y_ODD, info, q_mid, [kv_mid_below, kv_mid_below_core], [far, early])

    parts = ((mid_a, mid_b), (wide, wide_back), (far, far_back))
    late_rows = merge(True, info, [near_1], *parts)
    late = swap_heads(late_rows)
    (near_2,) = near(3, 2, info, queries, keys, values, [late_rows])
    attended_own = merge(False, info, [near_1, near_2], *parts)
    return project(info, attended_own, early, late, out_weight, weight_part, weight_rest)


def solution(mesh):
    return jax.shard_map(
        per_device,
        mesh=mesh,
        in_specs=(P("seq", "head"), P("seq", "head"), P("seq", "head"), P(), P("head", None)),
        out_specs=P(("seq", "head"), None),
        check_vma=False,
    )
```
